128 devices in a mesh: rows: 32 (over z, x, y_hi), chan: 4 (over y_lo, core).
Axes of the slice: x: 4, y: 4 (y_hi: 2, y_lo: 2; y = y_hi * 2 + y_lo), z: 4, core: 2. Of those that a mesh axis runs over, the one named last changes fastest.
Arguments:
- pair: bfloat16 [512, 128, 512], P('rows'), may hold values from -16 to 16
- norm_gain: float32 [2, 128], replicated, may hold values from 0.25 to 1.75
- proj_weight: bfloat16 [2, 4, 128, 128], replicated, may hold values from -0.5 to 0.5
- gate_weight: bfloat16 [2, 128, 128], replicated, may hold values from -0.5 to 0.5
- hidden_gain: float32 [2, 128], replicated, may hold values from 0.25 to 1.75
- out_weight: bfloat16 [2, 128, 128], replicated, may hold values from -0.5 to 0.5
Outputs:
- window_pair: bfloat16 [512, 128, 288], P('rows', 'chan')
The draws below stay inside these ranges and needn't reach their ends.
All inputs are finite; a program needn't handle non-finite values.
Results may differ from the reference program's by a relative error of at most 0.013.
Values may be sent and summed in bfloat16 or wider, within the bound.
A program may use at most 128 MiB of HBM per device.

```python
import math
import jax
import jax.numpy as jnp
from jax import lax

C = 128
H = 128
N_TOK = 512
WIN = 288


def draw_pair(key, part):
    key = jax.random.fold_in(key, 7)
    scale_key, base_key = jax.random.split(key, 2)
    channel_scale = jnp.exp(jax.random.uniform(scale_key, (C,), jnp.float32, math.log(0.4), math.log(4.0)))
    values = jax.random.normal(base_key, (N_TOK, C, N_TOK), jnp.float32)
    return jnp.clip(values * channel_scale[None, :, None], -16.0, 16.0).astype(jnp.bfloat16)


def scatter_about(rng, dims, scale, bound, held_as=jnp.bfloat16):
    entries = scale * jax.random.normal(rng, dims, jnp.float32)
    return jnp.clip(entries, min=-bound, max=bound).astype(held_as)


def setup_inputs(seed: int = 0) -> dict:
    seeds = jax.random.split(jax.random.key(seed), 7)
    return {
        "pair": draw_pair(jax.random.fold_in(seeds[6], 71), 0),
        "norm_gain": jnp.clip(1.0 + 0.15 * jax.random.normal(seeds[1], (2, C), jnp.float32), 0.25, 1.75),
        "proj_weight": scatter_about(seeds[2], (2, 4, C, H), C ** -0.5, 0.5),
        "gate_weight": scatter_about(seeds[3], (2, C, C), C ** -0.5, 0.5),
        "hidden_gain": jnp.clip(1.0 + 0.15 * jax.random.normal(seeds[4], (2, H), jnp.float32), 0.25, 1.75),
        "out_weight": scatter_about(seeds[5], (2, H, C), H ** -0.5, 0.5),
    }


def layer_norm(values, scale_gain):
    average = lax.optimization_barrier(jnp.mean(values, axis=1, keepdims=True))
    centred = values - average
    spread = lax.optimization_barrier(jnp.mean(centred * centred, axis=1, keepdims=True))
    return centred * jax.lax.rsqrt(spread + 1e-05) * scale_gain[None, :, None]

def channel_mix(inputs, weight):
    return jnp.einsum('ick,cd->idk', inputs.astype(jnp.float32), weight.astype(jnp.float32))

def gated_projection(inputs, weight_proj, weight_gate):
    return (jax.nn.sigmoid(channel_mix(inputs, weight_gate)) * channel_mix(inputs, weight_proj)).astype(jnp.bfloat16)

def reference(pair, norm_gain, proj_weight, gate_weight, hidden_gain, out_weight):
    pair_float = pair.astype(jnp.float32)
    normed = layer_norm(pair_float, norm_gain[0]).astype(jnp.bfloat16)
    left_rows = gated_projection(normed, proj_weight[0, 0], proj_weight[0, 1])
    right_rows = gated_projection(normed, proj_weight[0, 2], proj_weight[0, 3])
    gate_full = jax.nn.sigmoid(channel_mix(normed, gate_weight[0]))
    outsum = jnp.einsum('ihk,jhk->ihj', left_rows.astype(jnp.float32), right_rows.astype(jnp.float32))
    outnorm = layer_norm(outsum, hidden_gain[0]).astype(jnp.bfloat16)
    middle = (pair_float + gate_full * channel_mix(outnorm, out_weight[0])).astype(jnp.bfloat16)
    middle_float = middle.astype(jnp.float32)
    normed_mid = layer_norm(middle_float, norm_gain[1]).astype(jnp.bfloat16)
    left_in = gated_projection(normed_mid[:, :, :WIN], proj_weight[1, 0], proj_weight[1, 1])
    right_in = gated_projection(normed_mid, proj_weight[1, 2], proj_weight[1, 3])
    gate_in = jax.nn.sigmoid(channel_mix(normed_mid[:WIN], gate_weight[1]))
    insum = jnp.einsum('khi,khj->ihj', left_in.astype(jnp.float32), right_in.astype(jnp.float32))
    innorm = layer_norm(insum, hidden_gain[1]).astype(jnp.bfloat16)
    result = (middle_float[:WIN] + gate_in * channel_mix(innorm, out_weight[1])).astype(jnp.bfloat16)
    return jnp.transpose(result, (2, 1, 0))
```

```python
import functools

import jax
import jax.numpy as jnp
from jax import lax
from jax.experimental import pallas as pl
from jax.experimental.pallas import tpu as pltpu
from jax.sharding import PartitionSpec as P

MESH = pl.DeviceIdType.MESH
F32 = jnp.float32
BF16 = jnp.bfloat16
C = 128
H = 128
TOK = 512
WIN = 288
ROWS = 32
CHAN = 4
DEV = ROWS * CHAN
R = TOK // ROWS
K = TOK // CHAN
BLOCKS = 3
WPAD = BLOCKS * K
SPREAD = 37


def sigmoid(v):
    return 0.5 * jnp.tanh(0.5 * v) + 0.5


def norm_rows(x, gain):
    average = jnp.mean(x, axis=0, keepdims=True)
    centred = x - average
    spread = jnp.mean(centred * centred, axis=0, keepdims=True)
    return (centred * lax.rsqrt(spread + 1e-05) * gain).astype(BF16)


def norm_hidden(src, z):
    def add(h, total):
        return total + src[h].astype(F32)

    zero = jnp.zeros((R, K), F32)
    average = lax.fori_loop(0, H, add, zero, unroll=8) * (1.0 / H)

    def add_square(h, total):
        d = src[h].astype(F32) - average
        return total + d * d

    spread = lax.fori_loop(0, H, add_square, zero, unroll=8) * (1.0 / H)
    scale = lax.rsqrt(spread + 1e-05)

    def put(h, carry):
        z[pl.ds(pl.multiple_of(h * R, R), R), :] = (src[h].astype(F32) - average) * scale
        return carry

    lax.fori_loop(0, H, put, 0, unroll=8)


def dot(a, b, dims=((1,), (0,))):
    return lax.dot_general(a, b, (dims, ((), ())), preferred_element_type=F32)


def kernel(
    pair_ref, ng_ref, pw_ref, gw_ref, hg_ref, ow_ref, out_ref,
    x_buf, n_buf, wt, gt, ot, gains, z0, z1,
    send_a, recv_a, out_b, recv_b, gate0, mid,
    send_c, left_c, right_c, send_m, recv_m, out_d, recv_d, gate1, resid, out_e, recv_e,
    load_sem, a_ssem, a_rsem, b_ssem, b_rsem, cl_ssem, cr_ssem, cl_rsem, cr_rsem,
    m_ssem, m_rsem, d_ssem, d_rsem, e_ssem, e_rsem,
):
    r = lax.axis_index("rows")
    c = lax.axis_index("chan")
    hid = c * ROWS + r
    block = lax.rem(2 * c, 3)

    barrier = pltpu.get_barrier_semaphore()

    def greet(s, carry):
        q = lax.rem(r * CHAN + c + s, DEV)
        pl.semaphore_signal(
            barrier, inc=1, device_id=(q // CHAN, lax.rem(q, CHAN)), device_id_type=MESH
        )
        return carry

    lax.fori_loop(1, DEV, greet, 0)

    load = pltpu.make_async_copy(
        pair_ref.at[:, :, pl.ds(pl.multiple_of(c * K, K), K)], x_buf, load_sem
    )
    load.start()

    share = H // CHAN

    def turn(t, carry):
        u, m = t // 4, lax.rem(t, 4)
        w = jnp.transpose(pw_ref[u, m].astype(F32)).astype(BF16)
        for q in range(CHAN):
            wt[u, q, pl.ds(pl.multiple_of(m * share, share), share), :] = w[
                q * share : (q + 1) * share
            ]
        return carry

    lax.fori_loop(0, 8, turn, 0)
    for u in range(2):
        gt[u] = jnp.transpose(gw_ref[u].astype(F32)).astype(BF16)
        ot[u] = jnp.transpose(ow_ref[u].astype(F32)).astype(BF16)
        gains[u] = jnp.transpose(jnp.broadcast_to(ng_ref[u : u + 1, :], (C, C)))
        gains[2 + u] = jnp.transpose(jnp.broadcast_to(hg_ref[u : u + 1, :], (H, H)))

    load.wait()

    def norm_in(i, carry):
        n_buf[i] = norm_rows(x_buf[i].astype(F32), gains[0])
        return carry

    lax.fori_loop(0, R, norm_in, 0, unroll=2)

    def project(u, q, dst):
        def one(i, carry):
            y = dot(wt[u, q], n_buf[i])
            z0[pl.ds(i, share, stride=R), :] = sigmoid(y[share : 2 * share]) * y[:share]
            z1[pl.ds(i, share, stride=R), :] = (
                sigmoid(y[3 * share :]) * y[2 * share : 3 * share]
            )
            return carry

        lax.fori_loop(0, R, one, 0, unroll=4)

        def pack(h, carry):
            rows = pl.ds(pl.multiple_of(h * R, R), R)
            dst[q * share + h, 0] = z0[rows, :].astype(BF16)
            dst[q * share + h, 1] = z1[rows, :].astype(BF16)
            return carry

        lax.fori_loop(0, share, pack, 0, unroll=8)

    my_rows = pl.ds(pl.multiple_of(r * R, R), R)
    my_cols = pl.ds(pl.multiple_of(c * K, K), K)

    def chunk_a(s, carry):
        q = lax.rem(s + r, CHAN)
        project(0, q, send_a)

        @pl.when(s == 0)
        def _():
            pl.semaphore_wait(barrier, DEV - 1)

        def send(t, carry):
            r2 = lax.rem(r + t * SPREAD, ROWS)
            h2 = q * ROWS + r2
            src = send_a.at[h2]
            dst = recv_a.at[:, my_rows, my_cols]

            @pl.when(h2 == hid)
            def _():
                pltpu.make_async_copy(src, dst, a_rsem).start()

            @pl.when(h2 != hid)
            def _():
                pltpu.make_async_remote_copy(
                    src, dst, a_ssem, a_rsem, device_id=(r2, q), device_id_type=MESH
                ).start()

            return carry

        lax.fori_loop(0, ROWS, send, 0)
        return carry

    lax.fori_loop(0, CHAN, chunk_a, 0)

    def gate_out(i, carry):
        gate0[i] = sigmoid(dot(gt[0], n_buf[i]))
        return carry

    lax.fori_loop(0, R, gate_out, 0, unroll=2)

    pltpu.make_async_copy(recv_a, recv_a, a_rsem).wait()

    per = K // R

    def chunk_b(s, carry):
        b = lax.rem(s + r // 8, TOK // K)
        rows = pl.ds(pl.multiple_of(b * K, K), K)
        out_b[rows, :] = dot(recv_a[0, rows, :], recv_a[1], ((1,), (1,))).astype(BF16)

        def send(t, carry):
            v = lax.rem(t * SPREAD + r * CHAN + c, per * CHAN)
            r2 = b * per + v // CHAN
            c2 = lax.rem(v, CHAN)
            src = out_b.at[
                pl.ds(pl.multiple_of(r2 * R, R), R), pl.ds(pl.multiple_of(c2 * K, K), K)
            ]
            dst = recv_b.at[hid]
            own = jnp.logical_and(r2 == r, c2 == c)

            @pl.when(own)
            def _():
                pltpu.make_async_copy(src, dst, b_rsem).start()

            @pl.when(jnp.logical_not(own))
            def _():
                pltpu.make_async_remote_copy(
                    src, dst, b_ssem, b_rsem, device_id=(r2, c2), device_id_type=MESH
                ).start()

            return carry

        lax.fori_loop(0, per * CHAN, send, 0)
        return carry

    lax.fori_loop(0, TOK // K, chunk_b, 0)

    pltpu.make_async_copy(recv_b, recv_b, b_rsem).wait()
    norm_hidden(recv_b, z0)

    def update_out(i, carry):
        h = (z0[pl.ds(i, H, stride=R), :] * gains[2]).astype(BF16)
        m = (x_buf[i].astype(F32) + gate0[i] * dot(ot[0], h)).astype(BF16)
        mid[i] = m
        n_buf[i] = norm_rows(m.astype(F32), gains[1])
        return carry

    lax.fori_loop(0, R, update_out, 0, unroll=2)

    def chunk_c(s, carry):
        q = lax.rem(s + r, CHAN)
        project(1, q, send_c)

        def send(t, carry):
            r2 = lax.rem(r + t * SPREAD, ROWS)
            h2 = q * ROWS + r2
            right_src, right_dst = send_c.at[h2, 1], right_c.at[my_rows, my_cols]

            @pl.when(h2 == hid)
            def _():
                pltpu.make_async_copy(right_src, right_dst, cr_rsem).start()

            @pl.when(h2 != hid)
            def _():
                pltpu.make_async_remote_copy(
                    right_src, right_dst, cr_ssem, cr_rsem, device_id=(r2, q), device_id_type=MESH
                ).start()

            @pl.when(c < BLOCKS)
            def _():
                left_src, left_dst = send_c.at[h2, 0], left_c.at[my_rows, my_cols]

                @pl.when(h2 == hid)
                def _():
                    pltpu.make_async_copy(left_src, left_dst, cl_rsem).start()

                @pl.when(h2 != hid)
                def _():
                    pltpu.make_async_remote_copy(
                        left_src, left_dst, cl_ssem, cl_rsem,
                        device_id=(r2, q), device_id_type=MESH,
                    ).start()

            return carry

        lax.fori_loop(0, ROWS, send, 0)
        return carry

    lax.fori_loop(0, CHAN, chunk_c, 0)

    sends_m = r * R < WIN
    row_block = r // per
    m_chan = lax.rem(2 * row_block, 3)
    m_rows = pl.ds(pl.multiple_of(lax.rem(r, per) * R, R), R)

    def m_copy(g):
        r2 = c * per + g
        src = send_m.at[pl.ds(pl.multiple_of(g * R, R), R)]
        dst = recv_m.at[:, m_rows, :]
        own = jnp.logical_and(r2 == r, m_chan == c)
        local = pltpu.make_async_copy(src, dst, m_rsem)
        remote = pltpu.make_async_remote_copy(
            src, dst, m_ssem.at[g], m_rsem, device_id=(r2, m_chan), device_id_type=MESH
        )
        return own, local, remote

    @pl.when(sends_m)
    def _():
        def turn_mid(i, carry):
            z0[pl.ds(i, K, stride=R), :] = jnp.transpose(mid[i].astype(F32))
            return carry

        lax.fori_loop(0, R, turn_mid, 0, unroll=2)

        def pack(j, carry):
            send_m[j] = z0[pl.ds(pl.multiple_of(j * R, R), R), :].astype(BF16)
            return carry

        lax.fori_loop(0, K, pack, 0, unroll=8)

        def send(g, carry):
            own, local, remote = m_copy(g)

            @pl.when(own)
            def _():
                local.start()

            @pl.when(jnp.logical_not(own))
            def _():
                remote.start()

            return carry

        lax.fori_loop(0, per, send, 0)

    pltpu.make_async_copy(left_c, left_c, cl_rsem).wait()
    pltpu.make_async_copy(right_c, right_c, cr_rsem).wait()

    def chunk_d(s, carry):
        b = lax.rem(s + r // 8, TOK // K)
        cols = pl.ds(pl.multiple_of(b * K, K), K)
        out_d[cols, :] = dot(right_c[:, cols], left_c[...], ((0,), (0,))).astype(BF16)

        def send(t, carry):
            v = lax.rem(t * 5 + r * CHAN + c, per * BLOCKS)
            r2 = b * per + v // BLOCKS
            b2 = lax.rem(v, BLOCKS)
            c2 = lax.rem(2 * b2, 3)
            src = out_d.at[
                pl.ds(pl.multiple_of(r2 * R, R), R), pl.ds(pl.multiple_of(b2 * K, K), K)
            ]
            dst = recv_d.at[hid]
            own = jnp.logical_and(r2 == r, c2 == c)

            @pl.when(own)
            def _():
                pltpu.make_async_copy(src, dst, d_rsem).start()

            @pl.when(jnp.logical_not(own))
            def _():
                pltpu.make_async_remote_copy(
                    src, dst, d_ssem, d_rsem, device_id=(r2, c2), device_id_type=MESH
                ).start()

            return carry

        lax.fori_loop(0, per * BLOCKS, send, 0)
        return carry

    lax.fori_loop(0, TOK // K, chunk_d, 0)

    def e_copy(c2):
        src = out_e.at[:, pl.ds(c2 * share, share), :]
        dst = recv_e.at[block]
        local = pltpu.make_async_copy(src, dst, e_rsem)
        remote = pltpu.make_async_remote_copy(
            src, dst, e_ssem.at[c2], e_rsem, device_id=(r, c2), device_id_type=MESH
        )
        return local, remote

    @pl.when(c < BLOCKS)
    def _():
        @pl.when(block < BLOCKS - 1)
        def _():
            pltpu.make_async_copy(recv_m, recv_m, m_rsem).wait()

        @pl.when(block == BLOCKS - 1)
        def _():
            part = recv_m.at[:, pl.ds(0, WIN - (BLOCKS - 1) * K), :]
            pltpu.make_async_copy(part, part, m_rsem).wait()

        def gate_in(j, carry):
            m = jnp.transpose(recv_m[j].astype(F32))
            resid[j] = m.astype(BF16)
            gate1[j] = sigmoid(dot(gt[1], norm_rows(m, gains[1])))
            return carry

        lax.fori_loop(0, R, gate_in, 0, unroll=2)

        pltpu.make_async_copy(recv_d, recv_d, d_rsem).wait()
        norm_hidden(recv_d, z1)

        def update_in(j, carry):
            h = (z1[pl.ds(j, H, stride=R), :] * gains[3]).astype(BF16)
            out_e[j] = (resid[j].astype(F32) + gate1[j] * dot(ot[1], h)).astype(BF16)
            return carry

        lax.fori_loop(0, R, update_in, 0, unroll=2)

        for c2 in range(CHAN):
            local, remote = e_copy(c2)

            @pl.when(c == c2)
            def _():
                local.start()

            @pl.when(c != c2)
            def _():
                remote.start()

    pltpu.make_async_copy(recv_e, recv_e, e_rsem).wait()
    for b in range(BLOCKS):
        width = min(WIN - b * K, K)
        out_ref[:, :, b * K : b * K + width] = recv_e[b, :, :, :width]

    def drain(ref, sem):
        pltpu.make_async_copy(ref, ref, sem).wait()

    drain(send_a.at[pl.ds(0, DEV - 1)], a_ssem)
    drain(recv_b.at[pl.ds(0, DEV - 1)], b_ssem)
    drain(recv_b.at[pl.ds(0, DEV - 1)], cr_ssem)

    @pl.when(c < BLOCKS)
    def _():
        drain(recv_b.at[pl.ds(0, DEV - 1)], cl_ssem)
        drain(recv_b.at[pl.ds(0, ROWS * BLOCKS - 1)], d_ssem)
        for c2 in range(CHAN):

            @pl.when(c != c2)
            def _():
                e_copy(c2)[1].wait_send()

    @pl.when(c == BLOCKS)
    def _():
        drain(recv_b.at[pl.ds(0, ROWS * BLOCKS)], d_ssem)

    @pl.when(sends_m)
    def _():
        def done(g, carry):
            own, _local, remote = m_copy(g)

            @pl.when(jnp.logical_not(own))
            def _():
                remote.wait_send()

            return carry

        lax.fori_loop(0, per, done, 0)


def shards(pair, norm_gain, proj_weight, gate_weight, hidden_gain, out_weight):
    vmem = pl.BlockSpec(memory_space=pltpu.VMEM)
    sem = pltpu.SemaphoreType.DMA
    tiles = lambda n: pltpu.VMEM((n, R, K), BF16)
    return pl.pallas_call(
        kernel,
        out_shape=jax.ShapeDtypeStruct((R, C // CHAN, WIN), BF16),
        in_specs=[pl.BlockSpec(memory_space=pl.ANY)] + [vmem] * 5,
        out_specs=vmem,
        scratch_shapes=[
            pltpu.VMEM((R, C, K), BF16),
            pltpu.VMEM((R, C, K), BF16),
            pltpu.VMEM((2, CHAN, 4 * H // CHAN, C), BF16),
            pltpu.VMEM((2, C, C), BF16),
            pltpu.VMEM((2, C, H), BF16),
            pltpu.VMEM((4, C, K), F32),
            pltpu.VMEM((H * R, K), F32),
            pltpu.VMEM((H * R, K), F32),
            pltpu.VMEM((H, 2, R, K), BF16),
            pltpu.VMEM((2, TOK, TOK), BF16),
            pltpu.VMEM((TOK, TOK), BF16),
            tiles(H),
            pltpu.VMEM((R, C, K), F32),
            pltpu.VMEM((R, C, K), BF16),
            pltpu.VMEM((H, 2, R, K), BF16),
            pltpu.VMEM((TOK, WPAD), BF16),
            pltpu.VMEM((TOK, TOK), BF16),
            pltpu.VMEM((K, R, C), BF16),
            pltpu.VMEM((R, K, C), BF16),
            pltpu.VMEM((TOK, WPAD), BF16),
            tiles(H),
            pltpu.VMEM((R, C, K), F32),
            pltpu.VMEM((R, C, K), BF16),
            pltpu.VMEM((R, C, K), BF16),
            pltpu.VMEM((BLOCKS, R, C // CHAN, K), BF16),
            sem, sem, sem, sem, sem, sem, sem, sem, sem,
            sem((K // R,)), sem, sem, sem, sem((CHAN,)), sem,
        ],
        compiler_params=pltpu.CompilerParams(
            collective_id=0, has_side_effects=True, vmem_limit_bytes=48 * 1024 * 1024
        ),
    )(pair, norm_gain, proj_weight, gate_weight, hidden_gain, out_weight)


def solution(mesh):
    in_specs = (P("rows", None, None), P(), P(), P(), P(), P())
    out_specs = P("rows", "chan", None)
    return jax.shard_map(shards, mesh=mesh, in_specs=in_specs, out_specs=out_specs, check_vma=False)
```

```python
import functools

import jax
import jax.numpy as jnp
from jax import lax
from jax.experimental import pallas as pl
from jax.experimental.pallas import tpu as pltpu
from jax.sharding import PartitionSpec as P

MESH = pl.DeviceIdType.MESH
F32 = jnp.float32
BF16 = jnp.bfloat16
C = 128
H = 128
TOK = 512
WIN = 288
ROWS = 32
CHAN = 4
DEV = ROWS * CHAN
R = TOK // ROWS
K = TOK // CHAN
BLOCKS = 3
WPAD = BLOCKS * K
SPREAD = 37


def swap(n):
    return 2 * lax.rem(n, 2) + n // 2


def column_block(r, c):
    return swap(lax.rem(c + 2 * lax.rem(r // 8, 2), CHAN))


def column_chan(r, b):
    return lax.rem(swap(b) + 2 * lax.rem(r // 8, 2), CHAN)


def sigmoid(v):
    return 0.5 * jnp.tanh(0.5 * v) + 0.5


def norm_rows(x, gain):
    average = jnp.mean(x, axis=0, keepdims=True)
    centred = x - average
    spread = jnp.mean(centred * centred, axis=0, keepdims=True)
    return (centred * lax.rsqrt(spread + 1e-05) * gain).astype(BF16)


def norm_hidden(src, z):
    def add(h, total):
        return total + src[h].astype(F32)

    zero = jnp.zeros((R, K), F32)
    average = lax.fori_loop(0, H, add, zero, unroll=8) * (1.0 / H)

    def add_square(h, total):
        d = src[h].astype(F32) - average
        return total + d * d

    spread = lax.fori_loop(0, H, add_square, zero, unroll=8) * (1.0 / H)
    scale = lax.rsqrt(spread + 1e-05)

    def put(h, carry):
        z[pl.ds(pl.multiple_of(h * R, R), R), :] = (src[h].astype(F32) - average) * scale
        return carry

    lax.fori_loop(0, H, put, 0, unroll=8)


def dot(a, b, dims=((1,), (0,))):
    return lax.dot_general(a, b, (dims, ((), ())), preferred_element_type=F32)


def kernel(
    pair_hbm, ng_hbm, pw_hbm, gw_hbm, hg_hbm, ow_hbm, out_ref,
    ng_ref, pw_ref, gw_ref, hg_ref, ow_ref, x_buf, n_buf, wt, gt, ot, gains, z0, z1,
    send_a, recv_a, out_b, recv_b, gate0, mid,
    send_c, left_c, right_c, send_m, recv_m, out_d, recv_d, gate1, resid, out_e, out_t, recv_e, recv_t,
    load_sem, a_ssem, a_rsem, b_ssem, b_rsem, cl_ssem, cr_ssem, cl_rsem, cr_rsem,
    m_ssem, m_rsem, d_ssem, d_rsem, e_ssem, e_rsem, t_rsem,
):
    r = lax.axis_index("rows")
    c = lax.axis_index("chan")
    hid = c * ROWS + r
    mine = column_block(r, c)
    block = swap(c)

    loads = [
        pltpu.make_async_copy(src, dst, load_sem.at[n])
        for n, (src, dst) in enumerate(
            [
                (pw_hbm, pw_ref),
                (ng_hbm, ng_ref),
                (pair_hbm.at[:, :, pl.ds(pl.multiple_of(mine * K, K), K)], x_buf),
                (gw_hbm, gw_ref),
                (ow_hbm, ow_ref),
                (hg_hbm, hg_ref),
            ]
        )
    ]
    for load in loads:
        load.start()

    barrier = pltpu.get_barrier_semaphore()

    def greet(s, carry):
        q = lax.rem(r * CHAN + c + s, DEV)
        pl.semaphore_signal(
            barrier, inc=1, device_id=(q // CHAN, lax.rem(q, CHAN)), device_id_type=MESH
        )
        return carry

    lax.fori_loop(1, DEV, greet, 0)

    share = H // CHAN

    def turn(u):
        def one(m, carry):
            w = jnp.transpose(pw_ref[u, m].astype(F32)).astype(BF16)
            for q in range(CHAN):
                wt[u, q, pl.ds(pl.multiple_of(m * share, share), share), :] = w[
                    q * share : (q + 1) * share
                ]
            return carry

        lax.fori_loop(0, 4, one, 0)

    def column(row):
        return jnp.transpose(jnp.broadcast_to(row, (C, C)))

    loads[0].wait()
    turn(0)
    loads[1].wait()
    gains[0] = column(ng_ref[0:1, :])
    loads[2].wait()

    def norm_in(i, carry):
        n_buf[i] = norm_rows(x_buf[i].astype(F32), gains[0])
        return carry

    lax.fori_loop(0, R, norm_in, 0, unroll=2)

    def project(u, q, dst):
        def one(i, carry):
            y = dot(wt[u, q], n_buf[i])
            z0[pl.ds(i, share, stride=R), :] = sigmoid(y[share : 2 * share]) * y[:share]
            z1[pl.ds(i, share, stride=R), :] = (
                sigmoid(y[3 * share :]) * y[2 * share : 3 * share]
            )
            return carry

        lax.fori_loop(0, R, one, 0, unroll=4)

        def pack(h, carry):
            rows = pl.ds(pl.multiple_of(h * R, R), R)
            dst[q * share + h, 0] = z0[rows, :].astype(BF16)
            dst[q * share + h, 1] = z1[rows, :].astype(BF16)
            return carry

        lax.fori_loop(0, share, pack, 0, unroll=8)

    my_rows = pl.ds(pl.multiple_of(r * R, R), R)
    my_cols = pl.ds(pl.multiple_of(mine * K, K), K)

    def chunk_a(s, carry):
        q = 2 * lax.rem(s + r, 2) + s // 2
        project(0, q, send_a)

        @pl.when(s == 0)
        def _():
            pl.semaphore_wait(barrier, DEV - 1)

        def send(t, carry):
            r2 = lax.rem(r + t * SPREAD, ROWS)
            h2 = q * ROWS + r2
            src = send_a.at[h2]
            dst = recv_a.at[:, my_rows, my_cols]

            @pl.when(h2 == hid)
            def _():
                pltpu.make_async_copy(src, dst, a_rsem).start()

            @pl.when(h2 != hid)
            def _():
                pltpu.make_async_remote_copy(
                    src, dst, a_ssem, a_rsem, device_id=(r2, q), device_id_type=MESH
                ).start()

            return carry

        lax.fori_loop(0, ROWS, send, 0)
        return carry

    lax.fori_loop(0, CHAN, chunk_a, 0)

    for load in loads[3:]:
        load.wait()
    turn(1)
    for u in range(2):
        gt[u] = jnp.transpose(gw_ref[u].astype(F32)).astype(BF16)
        ot[u] = jnp.transpose(ow_ref[u].astype(F32)).astype(BF16)
        gains[2 + u] = column(hg_ref[u : u + 1, :])
    gains[1] = column(ng_ref[1:2, :])

    def gate_out(i, carry):
        gate0[i] = sigmoid(dot(gt[0], n_buf[i]))
        return carry

    lax.fori_loop(0, R, gate_out, 0, unroll=2)

    pltpu.make_async_copy(recv_a, recv_a, a_rsem).wait()

    per = K // R

    def send_b(r2, b2):
        c2 = column_chan(r2, b2)
        src = out_b.at[
            pl.ds(pl.multiple_of(r2 * R, R), R), pl.ds(pl.multiple_of(b2 * K, K), K)
        ]
        dst = recv_b.at[hid]
        own = jnp.logical_and(r2 == r, c2 == c)

        @pl.when(own)
        def _():
            pltpu.make_async_copy(src, dst, b_rsem).start()

        @pl.when(jnp.logical_not(own))
        def _():
            pltpu.make_async_remote_copy(
                src, dst, b_ssem, b_rsem, device_id=(r2, c2), device_id_type=MESH
            ).start()

    def chunk_b(s, carry):
        b = lax.rem(s + r // 8, TOK // K)
        rows = pl.ds(pl.multiple_of(b * K, K), K)
        out_b[rows, :] = dot(recv_a[0, rows, :], recv_a[1], ((1,), (1,))).astype(BF16)

        def send(t, carry):
            v = lax.rem(t * 5 + r * CHAN + c, per * 2)
            send_b(b * per + v // 2, lax.rem(v, 2))
            return carry

        lax.fori_loop(0, per * 2, send, 0)
        return carry

    lax.fori_loop(0, TOK // K, chunk_b, 0)

    def late_b(t, carry):
        v = lax.rem(t * SPREAD + r * CHAN + c, ROWS * 2)
        send_b(v // 2, 2 + lax.rem(v, 2))
        return carry

    lax.fori_loop(0, ROWS * 2, late_b, 0)

    pltpu.make_async_copy(recv_b, recv_b, b_rsem).wait()
    norm_hidden(recv_b, z0)

    def update_out(i, carry):
        h = (z0[pl.ds(i, H, stride=R), :] * gains[2]).astype(BF16)
        m = (x_buf[i].astype(F32) + gate0[i] * dot(ot[0], h)).astype(BF16)
        mid[i] = m
        n_buf[i] = norm_rows(m.astype(F32), gains[1])
        return carry

    lax.fori_loop(0, R, update_out, 0, unroll=2)

    def chunk_c(s, carry):
        q = 2 * lax.rem(s + r, 2) + s // 2
        project(1, q, send_c)

        def send(t, carry):
            r2 = lax.rem(r + t * SPREAD, ROWS)
            h2 = q * ROWS + r2
            right_src, right_dst = send_c.at[h2, 1], right_c.at[my_rows, my_cols]

            @pl.when(h2 == hid)
            def _():
                pltpu.make_async_copy(right_src, right_dst, cr_rsem).start()

            @pl.when(h2 != hid)
            def _():
                pltpu.make_async_remote_copy(
                    right_src, right_dst, cr_ssem, cr_rsem, device_id=(r2, q), device_id_type=MESH
                ).start()

            @pl.when(mine < BLOCKS)
            def _():
                left_src, left_dst = send_c.at[h2, 0], left_c.at[my_rows, my_cols]

                @pl.when(h2 == hid)
                def _():
                    pltpu.make_async_copy(left_src, left_dst, cl_rsem).start()

                @pl.when(h2 != hid)
                def _():
                    pltpu.make_async_remote_copy(
                        left_src, left_dst, cl_ssem, cl_rsem,
                        device_id=(r2, q), device_id_type=MESH,
                    ).start()

            return carry

        lax.fori_loop(0, ROWS, send, 0)
        return carry

    lax.fori_loop(0, CHAN, chunk_c, 0)

    sends_m = r * R < WIN
    row_block = r // per
    m_chan = swap(row_block)
    m_rows = pl.ds(pl.multiple_of(lax.rem(r, per) * R, R), R)

    def m_copy(g):
        r2 = mine * per + g
        src = send_m.at[pl.ds(pl.multiple_of(g * R, R), R)]
        dst = recv_m.at[:, m_rows, :]
        own = jnp.logical_and(r2 == r, m_chan == c)
        local = lambda: pltpu.make_async_copy(src, dst, m_rsem)
        remote = lambda: pltpu.make_async_remote_copy(
            src, dst, m_ssem.at[g], m_rsem, device_id=(r2, m_chan), device_id_type=MESH
        )
        return own, local, remote

    @pl.when(sends_m)
    def _():
        def turn_mid(i, carry):
            z0[pl.ds(i, K, stride=R), :] = jnp.transpose(mid[i].astype(F32))
            return carry

        lax.fori_loop(0, R, turn_mid, 0, unroll=2)

        def pack(j, carry):
            send_m[j] = z0[pl.ds(pl.multiple_of(j * R, R), R), :].astype(BF16)
            return carry

        lax.fori_loop(0, K, pack, 0, unroll=8)

        def send(g, carry):
            own, local, remote = m_copy(g)

            @pl.when(own)
            def _():
                local().start()

            @pl.when(jnp.logical_not(own))
            def _():
                remote().start()

            return carry

        lax.fori_loop(0, per, send, 0)

    pltpu.make_async_copy(left_c, left_c, cl_rsem).wait()
    pltpu.make_async_copy(right_c, right_c, cr_rsem).wait()

    tail = WIN - (BLOCKS - 1) * K
    group = K // tail

    def chunk_d(s, carry):
        b = lax.rem(s + r // 8, TOK // K)
        cols = pl.ds(pl.multiple_of(b * K, K), K)
        out_d[cols, :] = dot(right_c[:, cols], left_c[...], ((0,), (0,))).astype(BF16)

        def send(t, carry):
            v = lax.rem(t * 5 + r * CHAN + c, per * BLOCKS)
            r2 = b * per + v // BLOCKS
            b2 = lax.rem(v, BLOCKS)
            c2 = swap(b2)
            src = out_d.at[
                pl.ds(pl.multiple_of(r2 * R, R), R), pl.ds(pl.multiple_of(b2 * K, K), K)
            ]
            dst = recv_d.at[hid]
            own = jnp.logical_and(r2 == r, c2 == c)

            @pl.when(own)
            def _():
                pltpu.make_async_copy(src, dst, d_rsem).start()

            @pl.when(jnp.logical_not(own))
            def _():
                pltpu.make_async_remote_copy(
                    src, dst, d_ssem, d_rsem, device_id=(r2, c2), device_id_type=MESH
                ).start()

            return carry

        lax.fori_loop(0, per * BLOCKS, send, 0)
        return carry

    lax.fori_loop(0, TOK // K, chunk_d, 0)

    @pl.when(block < BLOCKS)
    def _():
        @pl.when(block < BLOCKS - 1)
        def _():
            pltpu.make_async_copy(recv_m, recv_m, m_rsem).wait()

        @pl.when(block == BLOCKS - 1)
        def _():
            part = recv_m.at[:, pl.ds(0, tail), :]
            pltpu.make_async_copy(part, part, m_rsem).wait()

        def gate_in(j, carry):
            m = jnp.transpose(recv_m[j].astype(F32))
            resid[j] = m.astype(BF16)
            gate1[j] = sigmoid(dot(gt[1], norm_rows(m, gains[1])))
            return carry

        lax.fori_loop(0, R, gate_in, 0, unroll=2)

        pltpu.make_async_copy(recv_d, recv_d, d_rsem).wait()
        norm_hidden(recv_d, z1)

        def update_in(g, carry):
            first = pl.multiple_of(g * group, group)
            parts = []
            for t in range(group):
                h = (z1[pl.ds(first + t, H, stride=R), :] * gains[3]).astype(BF16)
                parts.append(
                    (resid[first + t].astype(F32) + gate1[first + t] * dot(ot[1], h)).astype(BF16)
                )

            def send(src, dst, sem):
                def one(s, carry):
                    c2 = lax.rem(c + 1 + s, CHAN)
                    rows = pl.ds(pl.multiple_of(c2 * share, share), share)

                    @pl.when(c2 == c)
                    def _():
                        pltpu.make_async_copy(src(rows), dst, sem).start()

                    @pl.when(c2 != c)
                    def _():
                        pltpu.make_async_remote_copy(
                            src(rows), dst, e_ssem, sem, device_id=(r, c2), device_id_type=MESH
                        ).start()

                    return carry

                lax.fori_loop(0, CHAN, one, 0)

            @pl.when(block < BLOCKS - 1)
            def _():
                for t in range(group):
                    out_e[first + t] = parts[t]
                some = pl.ds(first, group)
                send(lambda rows: out_e.at[some, rows, :], recv_e.at[block, some], e_rsem)

            @pl.when(block == BLOCKS - 1)
            def _():
                out_t[g] = jnp.concatenate([part[:, :tail] for part in parts], axis=1)
                send(lambda rows: out_t.at[g, rows, :], recv_t.at[g], t_rsem)

            return carry

        lax.fori_loop(0, R // group, update_in, 0)

    pltpu.make_async_copy(recv_t, recv_t, t_rsem).wait()
    for g in range(R // group):
        for t in range(group):
            out_ref[g * group + t, :, WIN - tail :] = recv_t[g, :, t * tail : (t + 1) * tail]
    pltpu.make_async_copy(recv_e, recv_e, e_rsem).wait()
    for b in range(BLOCKS - 1):
        out_ref[:, :, b * K : (b + 1) * K] = recv_e[b]

    def drain(ref, sem):
        pltpu.make_async_copy(ref, ref, sem).wait()

    drain(send_a.at[pl.ds(0, DEV - 1)], a_ssem)
    drain(recv_b.at[pl.ds(0, DEV - 1)], b_ssem)
    drain(recv_b.at[pl.ds(0, DEV - 1)], cr_ssem)

    @pl.when(mine < BLOCKS)
    def _():
        drain(recv_b.at[pl.ds(0, DEV - 1)], cl_ssem)

    @pl.when(block < BLOCKS)
    def _():
        drain(recv_b.at[pl.ds(0, ROWS * BLOCKS - 1)], d_ssem)

    @pl.when(block == BLOCKS)
    def _():
        drain(recv_b.at[pl.ds(0, ROWS * BLOCKS)], d_ssem)

    tiles = R * share // R

    @pl.when(block < BLOCKS - 1)
    def _():
        drain(recv_b.at[pl.ds(0, (CHAN - 1) * tiles)], e_ssem)

    @pl.when(block == BLOCKS - 1)
    def _():
        drain(recv_b.at[pl.ds(0, (CHAN - 1) * tiles // group)], e_ssem)

    @pl.when(sends_m)
    def _():
        def done(g, carry):
            own, _local, remote = m_copy(g)

            @pl.when(jnp.logical_not(own))
            def _():
                remote().wait_send()

            return carry

        lax.fori_loop(0, per, done, 0)


def shards(pair, norm_gain, proj_weight, gate_weight, hidden_gain, out_weight):
    vmem = pl.BlockSpec(memory_space=pltpu.VMEM)
    sem = pltpu.SemaphoreType.DMA
    tiles = lambda n: pltpu.VMEM((n, R, K), BF16)
    return pl.pallas_call(
        kernel,
        out_shape=jax.ShapeDtypeStruct((R, C // CHAN, WIN), BF16),
        in_specs=[pl.BlockSpec(memory_space=pltpu.HBM)] * 6,
        out_specs=vmem,
        scratch_shapes=[
            pltpu.VMEM((2, C), F32),
            pltpu.VMEM((2, 4, C, H), BF16),
            pltpu.VMEM((2, C, C), BF16),
            pltpu.VMEM((2, H), F32),
            pltpu.VMEM((2, H, C), BF16),
            pltpu.VMEM((R, C, K), BF16),
            pltpu.VMEM((R, C, K), BF16),
            pltpu.VMEM((2, CHAN, 4 * H // CHAN, C), BF16),
            pltpu.VMEM((2, C, C), BF16),
            pltpu.VMEM((2, C, H), BF16),
            pltpu.VMEM((4, C, K), F32),
            pltpu.VMEM((H * R, K), F32),
            pltpu.VMEM((H * R, K), F32),
            pltpu.VMEM((H, 2, R, K), BF16),
            pltpu.VMEM((2, TOK, TOK), BF16),
            pltpu.VMEM((TOK, TOK), BF16),
            tiles(H),
            pltpu.VMEM((R, C, K), F32),
            pltpu.VMEM((R, C, K), BF16),
            pltpu.VMEM((H, 2, R, K), BF16),
            pltpu.VMEM((TOK, WPAD), BF16),
            pltpu.VMEM((TOK, TOK), BF16),
            pltpu.VMEM((K, R, C), BF16),
            pltpu.VMEM((R, K, C), BF16),
            pltpu.VMEM((TOK, WPAD), BF16),
            tiles(H),
            pltpu.VMEM((R, C, K), F32),
            pltpu.VMEM((R, C, K), BF16),
            pltpu.VMEM((R, C, K), BF16),
            pltpu.VMEM((R // 4, C, K), BF16),
            pltpu.VMEM((BLOCKS - 1, R, C // CHAN, K), BF16),
            pltpu.VMEM((R // 4, C // CHAN, K), BF16),
            sem((6,)), sem, sem, sem, sem, sem, sem, sem, sem,
            sem((K // R,)), sem, sem, sem, sem, sem, sem,
        ],
        compiler_params=pltpu.CompilerParams(
            collective_id=0, has_side_effects=True, vmem_limit_bytes=48 * 1024 * 1024
        ),
    )(pair, norm_gain, proj_weight, gate_weight, hidden_gain, out_weight)


def solution(mesh):
    in_specs = (P("rows", None, None), P(), P(), P(), P(), P())
    out_specs = P("rows", "chan", None)
    return jax.shard_map(shards, mesh=mesh, in_specs=in_specs, out_specs=out_specs, check_vma=False)
```

```python
import functools

import jax
import jax.numpy as jnp
from jax import lax
from jax.experimental import pallas as pl
from jax.experimental.pallas import tpu as pltpu
from jax.sharding import PartitionSpec as P

MESH = pl.DeviceIdType.MESH
F32 = jnp.float32
BF16 = jnp.bfloat16
C = 128
H = 128
TOK = 512
WIN = 288
ROWS = 32
CHAN = 4
DEV = ROWS * CHAN
R = TOK // ROWS
K = TOK // CHAN
BLOCKS = 3
WPAD = BLOCKS * K
SPREAD = 37
VMEM_BYTES = 63 * 1024 * 1024


def swap(n):
    return 2 * lax.rem(n, 2) + n // 2


def turned(r):
    return lax.rem(r // 2 + r // 8, 2)


def column_block(r, c):
    return swap(lax.rem(c + 2 * turned(r), CHAN))


def column_chan(r, b):
    return lax.rem(swap(b) + 2 * turned(r), CHAN)


def sigmoid(v):
    return 0.5 * jnp.tanh(0.5 * v) + 0.5


def norm_rows(x, gain):
    average = jnp.mean(x, axis=0, keepdims=True)
    centred = x - average
    spread = jnp.mean(centred * centred, axis=0, keepdims=True)
    return (centred * lax.rsqrt(spread + 1e-05) * gain).astype(BF16)


def norm_hidden(src, z):
    def add(h, total):
        return total + src[h].astype(F32)

    zero = jnp.zeros((R, K), F32)
    average = lax.fori_loop(0, H, add, zero, unroll=8) * (1.0 / H)

    def add_square(h, total):
        d = src[h].astype(F32) - average
        return total + d * d

    spread = lax.fori_loop(0, H, add_square, zero, unroll=8) * (1.0 / H)
    scale = lax.rsqrt(spread + 1e-05)

    def put(h, carry):
        z[pl.ds(pl.multiple_of(h * R, R), R), :] = (src[h].astype(F32) - average) * scale
        return carry

    lax.fori_loop(0, H, put, 0, unroll=8)


def dot(a, b, dims=((1,), (0,))):
    return lax.dot_general(a, b, (dims, ((), ())), preferred_element_type=F32)


def kernel(
    pair_hbm, ng_hbm, pw_hbm, gw_hbm, hg_hbm, ow_hbm, out_ref,
    ng_ref, pw_ref, gw_ref, hg_ref, ow_ref, x_buf, n_buf, wt, gt, ot, gains, z0, z1,
    send_a, recv_a, out_b, recv_b, gate0, mid,
    send_c, left_c, right_c, send_m, recv_m, out_d, recv_d, gate1, resid, out_e, out_t, recv_e, recv_t,
    load_sem, a_ssem, a_rsem, b_ssem, b_rsem, cl_ssem, cr_ssem, cl_rsem, cr_rsem,
    m_ssem, m_rsem, d_ssem, d_rsem, e_ssem, e_rsem, t_rsem,
):
    r = lax.axis_index("rows")
    c = lax.axis_index("chan")
    hid = c * ROWS + r
    mine = column_block(r, c)
    block = mine

    loads = [
        pltpu.make_async_copy(src, dst, load_sem.at[n])
        for n, (src, dst) in enumerate(
            [
                (pw_hbm, pw_ref),
                (ng_hbm, ng_ref),
                (pair_hbm.at[:, :, pl.ds(pl.multiple_of(mine * K, K), K)], x_buf),
                (gw_hbm, gw_ref),
                (ow_hbm, ow_ref),
                (hg_hbm, hg_ref),
            ]
        )
    ]
    for load in loads:
        load.start()

    barrier = pltpu.get_barrier_semaphore()

    def greet(s, carry):
        q = lax.rem(r * CHAN + c + s, DEV)
        pl.semaphore_signal(
            barrier, inc=1, device_id=(q // CHAN, lax.rem(q, CHAN)), device_id_type=MESH
        )
        return carry

    lax.fori_loop(1, DEV, greet, 0)

    share = H // CHAN

    def turn(u):
        def one(m, carry):
            w = jnp.transpose(pw_ref[u, m].astype(F32)).astype(BF16)
            for q in range(CHAN):
                wt[u, q, pl.ds(pl.multiple_of(m * share, share), share), :] = w[
                    q * share : (q + 1) * share
                ]
            return carry

        lax.fori_loop(0, 4, one, 0)

    def column(row):
        return jnp.transpose(jnp.broadcast_to(row, (C, C)))

    loads[0].wait()
    turn(0)
    loads[1].wait()
    gains[0] = column(ng_ref[0:1, :])
    loads[2].wait()

    def norm_in(i, carry):
        n_buf[i] = norm_rows(x_buf[i].astype(F32), gains[0])
        return carry

    lax.fori_loop(0, R, norm_in, 0, unroll=2)

    def project(u, q, dst):
        def one(i, carry):
            y = dot(wt[u, q], n_buf[i])
            z0[pl.ds(i, share, stride=R), :] = sigmoid(y[share : 2 * share]) * y[:share]
            z1[pl.ds(i, share, stride=R), :] = (
                sigmoid(y[3 * share :]) * y[2 * share : 3 * share]
            )
            return carry

        lax.fori_loop(0, R, one, 0, unroll=4)

        def pack(h, carry):
            rows = pl.ds(pl.multiple_of(h * R, R), R)
            dst[q * share + h, 0] = z0[rows, :].astype(BF16)
            dst[q * share + h, 1] = z1[rows, :].astype(BF16)
            return carry

        lax.fori_loop(0, share, pack, 0, unroll=8)

    my_rows = pl.ds(pl.multiple_of(r * R, R), R)
    my_cols = pl.ds(pl.multiple_of(mine * K, K), K)

    def chunk_a(s, carry):
        q = 2 * lax.rem(s + r, 2) + s // 2
        project(0, q, send_a)

        @pl.when(s == 0)
        def _():
            pl.semaphore_wait(barrier, DEV - 1)

        def send(t, carry):
            r2 = lax.rem(r + t * SPREAD, ROWS)
            h2 = q * ROWS + r2
            src = send_a.at[h2]
            dst = recv_a.at[:, my_rows, my_cols]

            @pl.when(h2 == hid)
            def _():
                pltpu.make_async_copy(src, dst, a_rsem).start()

            @pl.when(h2 != hid)
            def _():
                pltpu.make_async_remote_copy(
                    src, dst, a_ssem, a_rsem, device_id=(r2, q), device_id_type=MESH
                ).start()

            return carry

        lax.fori_loop(0, ROWS, send, 0)
        return carry

    lax.fori_loop(0, CHAN, chunk_a, 0)

    for load in loads[3:]:
        load.wait()
    turn(1)
    for u in range(2):
        gt[u] = jnp.transpose(gw_ref[u].astype(F32)).astype(BF16)
        ot[u] = jnp.transpose(ow_ref[u].astype(F32)).astype(BF16)
        gains[2 + u] = column(hg_ref[u : u + 1, :])
    gains[1] = column(ng_ref[1:2, :])

    def gate_out(i, carry):
        gate0[i] = sigmoid(dot(gt[0], n_buf[i]))
        return carry

    lax.fori_loop(0, R, gate_out, 0, unroll=2)

    pltpu.make_async_copy(recv_a, recv_a, a_rsem).wait()

    per = K // R

    def send_b(r2, b2):
        c2 = column_chan(r2, b2)
        src = out_b.at[
            pl.ds(pl.multiple_of(r2 * R, R), R), pl.ds(pl.multiple_of(b2 * K, K), K)
        ]
        dst = recv_b.at[hid]
        own = jnp.logical_and(r2 == r, c2 == c)

        @pl.when(own)
        def _():
            pltpu.make_async_copy(src, dst, b_rsem).start()

        @pl.when(jnp.logical_not(own))
        def _():
            pltpu.make_async_remote_copy(
                src, dst, b_ssem, b_rsem, device_id=(r2, c2), device_id_type=MESH
            ).start()

    def chunk_b(s, carry):
        b = lax.rem(s + r // 8, TOK // K)
        rows = pl.ds(pl.multiple_of(b * K, K), K)
        out_b[rows, :] = dot(recv_a[0, rows, :], recv_a[1], ((1,), (1,))).astype(BF16)

        def send(t, carry):
            v = lax.rem(t * 5 + r * CHAN + c, per * 2)
            send_b(b * per + v // 2, lax.rem(v, 2))
            return carry

        lax.fori_loop(0, per * 2, send, 0)
        return carry

    lax.fori_loop(0, TOK // K, chunk_b, 0)

    def late_b(t, carry):
        v = lax.rem(t * SPREAD + r * CHAN + c, ROWS * 2)
        send_b(v // 2, 2 + lax.rem(v, 2))
        return carry

    lax.fori_loop(0, ROWS * 2, late_b, 0)

    pltpu.make_async_copy(recv_b, recv_b, b_rsem).wait()
    norm_hidden(recv_b, z0)

    def update_out(i, carry):
        h = (z0[pl.ds(i, H, stride=R), :] * gains[2]).astype(BF16)
        m = (x_buf[i].astype(F32) + gate0[i] * dot(ot[0], h)).astype(BF16)
        mid[i] = m
        n_buf[i] = norm_rows(m.astype(F32), gains[1])
        return carry

    lax.fori_loop(0, R, update_out, 0, unroll=2)

    def chunk_c(s, carry):
        q = 2 * lax.rem(s + r, 2) + s // 2
        project(1, q, send_c)

        def send(t, carry):
            r2 = lax.rem(r + t * SPREAD, ROWS)
            h2 = q * ROWS + r2
            right_src, right_dst = send_c.at[h2, 1], right_c.at[my_rows, my_cols]

            @pl.when(h2 == hid)
            def _():
                pltpu.make_async_copy(right_src, right_dst, cr_rsem).start()

            @pl.when(h2 != hid)
            def _():
                pltpu.make_async_remote_copy(
                    right_src, right_dst, cr_ssem, cr_rsem, device_id=(r2, q), device_id_type=MESH
                ).start()

            @pl.when(mine < BLOCKS)
            def _():
                left_src, left_dst = send_c.at[h2, 0], left_c.at[my_rows, my_cols]

                @pl.when(h2 == hid)
                def _():
                    pltpu.make_async_copy(left_src, left_dst, cl_rsem).start()

                @pl.when(h2 != hid)
                def _():
                    pltpu.make_async_remote_copy(
                        left_src, left_dst, cl_ssem, cl_rsem,
                        device_id=(r2, q), device_id_type=MESH,
                    ).start()

            return carry

        lax.fori_loop(0, ROWS, send, 0)
        return carry

    lax.fori_loop(0, CHAN, chunk_c, 0)

    sends_m = r * R < WIN
    row_block = r // per
    m_rows = pl.ds(pl.multiple_of(lax.rem(r, per) * R, R), R)

    def m_copy(n):
        g = lax.rem(n + r, per)
        r2 = mine * per + g
        m_chan = column_chan(r2, row_block)
        src = send_m.at[pl.ds(pl.multiple_of(g * R, R), R)]
        dst = recv_m.at[:, m_rows, :]
        own = jnp.logical_and(r2 == r, m_chan == c)
        local = lambda: pltpu.make_async_copy(src, dst, m_rsem)
        remote = lambda: pltpu.make_async_remote_copy(
            src, dst, m_ssem.at[g], m_rsem, device_id=(r2, m_chan), device_id_type=MESH
        )
        return own, local, remote

    @pl.when(sends_m)
    def _():
        def turn_mid(i, carry):
            z0[pl.ds(i, K, stride=R), :] = jnp.transpose(mid[i].astype(F32))
            return carry

        lax.fori_loop(0, R, turn_mid, 0, unroll=2)

        def pack(j, carry):
            send_m[j] = z0[pl.ds(pl.multiple_of(j * R, R), R), :].astype(BF16)
            return carry

        lax.fori_loop(0, K, pack, 0, unroll=8)

        def send(g, carry):
            own, local, remote = m_copy(g)

            @pl.when(own)
            def _():
                local().start()

            @pl.when(jnp.logical_not(own))
            def _():
                remote().start()

            return carry

        lax.fori_loop(0, per, send, 0)

    pltpu.make_async_copy(left_c, left_c, cl_rsem).wait()
    pltpu.make_async_copy(right_c, right_c, cr_rsem).wait()

    tail = WIN - (BLOCKS - 1) * K
    group = K // tail

    def chunk_d(s, carry):
        b = lax.rem(s + r // 8, TOK // K)
        cols = pl.ds(pl.multiple_of(b * K, K), K)
        out_d[cols, :] = dot(right_c[:, cols], left_c[...], ((0,), (0,))).astype(BF16)

        def send(t, carry):
            v = lax.rem(t * 5 + r * CHAN + c, per * BLOCKS)
            r2 = b * per + v // BLOCKS
            b2 = lax.rem(v, BLOCKS)
            c2 = column_chan(r2, b2)
            src = out_d.at[
                pl.ds(pl.multiple_of(r2 * R, R), R), pl.ds(pl.multiple_of(b2 * K, K), K)
            ]
            dst = recv_d.at[hid]
            own = jnp.logical_and(r2 == r, c2 == c)

            @pl.when(own)
            def _():
                pltpu.make_async_copy(src, dst, d_rsem).start()

            @pl.when(jnp.logical_not(own))
            def _():
                pltpu.make_async_remote_copy(
                    src, dst, d_ssem, d_rsem, device_id=(r2, c2), device_id_type=MESH
                ).start()

            return carry

        lax.fori_loop(0, per * BLOCKS, send, 0)
        return carry

    lax.fori_loop(0, TOK // K, chunk_d, 0)

    @pl.when(block < BLOCKS)
    def _():
        @pl.when(block < BLOCKS - 1)
        def _():
            pltpu.make_async_copy(recv_m, recv_m, m_rsem).wait()

        @pl.when(block == BLOCKS - 1)
        def _():
            part = recv_m.at[:, pl.ds(0, tail), :]
            pltpu.make_async_copy(part, part, m_rsem).wait()

        def gate_in(j, carry):
            m = jnp.transpose(recv_m[j].astype(F32))
            resid[j] = m.astype(BF16)
            gate1[j] = sigmoid(dot(gt[1], norm_rows(m, gains[1])))
            return carry

        lax.fori_loop(0, R, gate_in, 0, unroll=2)

        pltpu.make_async_copy(recv_d, recv_d, d_rsem).wait()
        norm_hidden(recv_d, z1)

        def update_in(g, carry):
            first = pl.multiple_of(g * group, group)
            parts = []
            for t in range(group):
                h = (z1[pl.ds(first + t, H, stride=R), :] * gains[3]).astype(BF16)
                parts.append(
                    (resid[first + t].astype(F32) + gate1[first + t] * dot(ot[1], h)).astype(BF16)
                )

            def send(src, dst, sem):
                def one(s, carry):
                    c2 = lax.rem(c + 1 + s, CHAN)
                    rows = pl.ds(pl.multiple_of(c2 * share, share), share)

                    @pl.when(c2 == c)
                    def _():
                        pltpu.make_async_copy(src(rows), dst, sem).start()

                    @pl.when(c2 != c)
                    def _():
                        pltpu.make_async_remote_copy(
                            src(rows), dst, e_ssem, sem, device_id=(r, c2), device_id_type=MESH
                        ).start()

                    return carry

                lax.fori_loop(0, CHAN, one, 0)

            @pl.when(block < BLOCKS - 1)
            def _():
                for t in range(group):
                    out_e[first + t] = parts[t]
                some = pl.ds(first, group)
                send(lambda rows: out_e.at[some, rows, :], recv_e.at[block, some], e_rsem)

            @pl.when(block == BLOCKS - 1)
            def _():
                out_t[g] = jnp.concatenate([part[:, :tail] for part in parts], axis=1)
                send(lambda rows: out_t.at[g, rows, :], recv_t.at[g], t_rsem)

            return carry

        lax.fori_loop(0, R // group, update_in, 0)

    pltpu.make_async_copy(recv_t, recv_t, t_rsem).wait()
    for g in range(R // group):
        for t in range(group):
            out_ref[g * group + t, :, WIN - tail :] = recv_t[g, :, t * tail : (t + 1) * tail]
    pltpu.make_async_copy(recv_e, recv_e, e_rsem).wait()
    for b in range(BLOCKS - 1):
        out_ref[:, :, b * K : (b + 1) * K] = recv_e[b]

    def drain(ref, sem):
        pltpu.make_async_copy(ref, ref, sem).wait()

    drain(send_a.at[pl.ds(0, DEV - 1)], a_ssem)
    drain(recv_b.at[pl.ds(0, DEV - 1)], b_ssem)
    drain(recv_b.at[pl.ds(0, DEV - 1)], cr_ssem)

    @pl.when(mine < BLOCKS)
    def _():
        drain(recv_b.at[pl.ds(0, DEV - 1)], cl_ssem)

    @pl.when(block < BLOCKS)
    def _():
        drain(recv_b.at[pl.ds(0, ROWS * BLOCKS - 1)], d_ssem)

    @pl.when(block == BLOCKS)
    def _():
        drain(recv_b.at[pl.ds(0, ROWS * BLOCKS)], d_ssem)

    tiles = R * share // R

    @pl.when(block < BLOCKS - 1)
    def _():
        drain(recv_b.at[pl.ds(0, (CHAN - 1) * tiles)], e_ssem)

    @pl.when(block == BLOCKS - 1)
    def _():
        drain(recv_b.at[pl.ds(0, (CHAN - 1) * tiles // group)], e_ssem)

    @pl.when(sends_m)
    def _():
        def done(g, carry):
            own, _local, remote = m_copy(g)

            @pl.when(jnp.logical_not(own))
            def _():
                remote().wait_send()

            return carry

        lax.fori_loop(0, per, done, 0)


def shards(pair, norm_gain, proj_weight, gate_weight, hidden_gain, out_weight):
    vmem = pl.BlockSpec(memory_space=pltpu.VMEM)
    sem = pltpu.SemaphoreType.DMA
    tiles = lambda n: pltpu.VMEM((n, R, K), BF16)
    return pl.pallas_call(
        kernel,
        out_shape=jax.ShapeDtypeStruct((R, C // CHAN, WIN), BF16),
        in_specs=[pl.BlockSpec(memory_space=pltpu.HBM)] * 6,
        out_specs=vmem,
        scratch_shapes=[
            pltpu.VMEM((2, C), F32),
            pltpu.VMEM((2, 4, C, H), BF16),
            pltpu.VMEM((2, C, C), BF16),
            pltpu.VMEM((2, H), F32),
            pltpu.VMEM((2, H, C), BF16),
            pltpu.VMEM((R, C, K), BF16),
            pltpu.VMEM((R, C, K), BF16),
            pltpu.VMEM((2, CHAN, 4 * H // CHAN, C), BF16),
            pltpu.VMEM((2, C, C), BF16),
            pltpu.VMEM((2, C, H), BF16),
            pltpu.VMEM((4, C, K), F32),
            pltpu.VMEM((H * R, K), F32),
            pltpu.VMEM((H * R, K), F32),
            pltpu.VMEM((H, 2, R, K), BF16),
            pltpu.VMEM((2, TOK, TOK), BF16),
            pltpu.VMEM((TOK, TOK), BF16),
            tiles(H),
            pltpu.VMEM((R, C, K), F32),
            pltpu.VMEM((R, C, K), BF16),
            pltpu.VMEM((H, 2, R, K), BF16),
            pltpu.VMEM((TOK, WPAD), BF16),
            pltpu.VMEM((TOK, TOK), BF16),
            pltpu.VMEM((K, R, C), BF16),
            pltpu.VMEM((R, K, C), BF16),
            pltpu.VMEM((TOK, WPAD), BF16),
            tiles(H),
            pltpu.VMEM((R, C, K), F32),
            pltpu.VMEM((R, C, K), BF16),
            pltpu.VMEM((R, C, K), BF16),
            pltpu.VMEM((R // 4, C, K), BF16),
            pltpu.VMEM((BLOCKS - 1, R, C // CHAN, K), BF16),
            pltpu.VMEM((R // 4, C // CHAN, K), BF16),
            sem((6,)), sem, sem, sem, sem, sem, sem, sem, sem,
            sem((K // R,)), sem, sem, sem, sem, sem, sem,
        ],
        compiler_params=pltpu.CompilerParams(
            collective_id=0, has_side_effects=True, vmem_limit_bytes=VMEM_BYTES
        ),
    )(pair, norm_gain, proj_weight, gate_weight, hidden_gain, out_weight)


def solution(mesh):
    in_specs = (P("rows", None, None), P(), P(), P(), P(), P())
    out_specs = P("rows", "chan", None)
    return jax.shard_map(shards, mesh=mesh, in_specs=in_specs, out_specs=out_specs, check_vma=False)
```

```python
import functools

import jax
import jax.numpy as jnp
from jax import lax
from jax.experimental import pallas as pl
from jax.experimental.pallas import tpu as pltpu
from jax.sharding import PartitionSpec as P

MESH = pl.DeviceIdType.MESH
F32 = jnp.float32
BF16 = jnp.bfloat16
C = 128
H = 128
TOK = 512
WIN = 288
ROWS = 32
CHAN = 4
DEV = ROWS * CHAN
R = TOK // ROWS
K = TOK // CHAN
BLOCKS = 3
SPREAD = 37
VMEM_BYTES = 63 * 1024 * 1024


def swap(n):
    return 2 * lax.rem(n, 2) + n // 2


def turned(r):
    return lax.rem(r // 2 + r // 8, 2)


def column_block(r, c):
    return swap(lax.rem(c + 2 * turned(r), CHAN))


def column_chan(r, b):
    return lax.rem(swap(b) + 2 * turned(r), CHAN)


def sigmoid(v):
    return 0.5 * jnp.tanh(0.5 * v) + 0.5


def norm_rows(x, gain):
    average = jnp.mean(x, axis=0, keepdims=True)
    centred = x - average
    spread = jnp.mean(centred * centred, axis=0, keepdims=True)
    return (centred * lax.rsqrt(spread + 1e-05) * gain).astype(BF16)


def norm_hidden(src, z):
    lanes = 4

    def some(n):
        return src[pl.ds(pl.multiple_of(n * lanes, lanes), lanes)].astype(F32)

    def add(n, total):
        return total + some(n)

    zero = jnp.zeros((lanes, R, K), F32)
    steps = H // lanes
    average = jnp.sum(lax.fori_loop(0, steps, add, zero, unroll=8), axis=0) * (1.0 / H)

    def add_square(n, total):
        d = some(n) - average
        return total + d * d

    spread = jnp.sum(lax.fori_loop(0, steps, add_square, zero, unroll=8), axis=0) * (1.0 / H)
    scale = lax.rsqrt(spread + 1e-05)

    def put(h, carry):
        z[pl.ds(pl.multiple_of(h * R, R), R), :] = (src[h].astype(F32) - average) * scale
        return carry

    lax.fori_loop(0, H, put, 0, unroll=8)


def dot(a, b, dims=((1,), (0,))):
    return lax.dot_general(a, b, (dims, ((), ())), preferred_element_type=F32)


def kernel(
    pair_hbm, ng_hbm, pw_hbm, gw_hbm, hg_hbm, ow_hbm, out_ref,
    ng_ref, pw_ref, gw_ref, hg_ref, ow_ref, x_buf, n_buf, wt, gt, ot, gains, z0, z1,
    send_a, recv_a, out_b, recv_b, gate0, mid,
    send_c, left_c, right_c, send_m, recv_m, out_d, recv_d, gate1, resid, out_e, out_t, recv_e, recv_t,
    load_sem, a_ssem, a_rsem, b_ssem, b_rsem, cl_ssem, cr_ssem, cl_rsem, cr_rsem,
    m_ssem, m_rsem, d_ssem, d_rsem, e_ssem, e_rsem, t_rsem,
):
    r = lax.axis_index("rows")
    c = lax.axis_index("chan")
    hid = c * ROWS + r
    mine = column_block(r, c)
    block = mine

    loads = [
        pltpu.make_async_copy(src, dst, load_sem.at[n])
        for n, (src, dst) in enumerate(
            [
                (pw_hbm, pw_ref),
                (ng_hbm, ng_ref),
                (pair_hbm.at[:, :, pl.ds(pl.multiple_of(mine * K, K), K)], x_buf),
                (gw_hbm, gw_ref),
                (ow_hbm, ow_ref),
                (hg_hbm, hg_ref),
            ]
        )
    ]
    for load in loads:
        load.start()

    barrier = pltpu.get_barrier_semaphore()

    def greet(s, carry):
        q = lax.rem(r * CHAN + c + s, DEV)
        pl.semaphore_signal(
            barrier, inc=1, device_id=(q // CHAN, lax.rem(q, CHAN)), device_id_type=MESH
        )
        return carry

    lax.fori_loop(1, DEV, greet, 0)

    share = H // CHAN

    def turn(u):
        def one(m, carry):
            w = jnp.transpose(pw_ref[u, m].astype(F32)).astype(BF16)
            for q in range(CHAN):
                wt[u, q, pl.ds(pl.multiple_of(m * share, share), share), :] = w[
                    q * share : (q + 1) * share
                ]
            return carry

        lax.fori_loop(0, 4, one, 0)

    def column(row):
        return jnp.transpose(jnp.broadcast_to(row, (C, C)))

    loads[0].wait()
    turn(0)
    loads[1].wait()
    gains[0] = column(ng_ref[0:1, :])
    loads[2].wait()

    def norm_in(i, carry):
        n_buf[i] = norm_rows(x_buf[i].astype(F32), gains[0])
        return carry

    lax.fori_loop(0, R, norm_in, 0, unroll=8)

    def project(u, q, dst):
        def one(i, carry):
            y = dot(wt[u, q], n_buf[i])
            z0[pl.ds(i, share, stride=R), :] = sigmoid(y[share : 2 * share]) * y[:share]
            z1[pl.ds(i, share, stride=R), :] = (
                sigmoid(y[3 * share :]) * y[2 * share : 3 * share]
            )
            return carry

        lax.fori_loop(0, R, one, 0, unroll=8)

        def pack(h, carry):
            rows = pl.ds(pl.multiple_of(h * R, R), R)
            dst[q * share + h, 0] = z0[rows, :].astype(BF16)
            dst[q * share + h, 1] = z1[rows, :].astype(BF16)
            return carry

        lax.fori_loop(0, share, pack, 0, unroll=8)

    my_rows = pl.ds(pl.multiple_of(r * R, R), R)

    def chunk_a(s, carry):
        q = lax.rem(s + r, CHAN)
        project(0, q, send_a)

        @pl.when(s == 0)
        def _():
            pl.semaphore_wait(barrier, DEV - 1)

        def send(t, carry):
            r2 = lax.rem(r + t * SPREAD, ROWS)
            h2 = q * ROWS + r2
            src = send_a.at[h2]
            dst = recv_a.at[:, mine, my_rows]

            @pl.when(h2 == hid)
            def _():
                pltpu.make_async_copy(src, dst, a_rsem).start()

            @pl.when(h2 != hid)
            def _():
                pltpu.make_async_remote_copy(
                    src, dst, a_ssem, a_rsem, device_id=(r2, q), device_id_type=MESH
                ).start()

            return carry

        lax.fori_loop(0, ROWS, send, 0)
        return carry

    lax.fori_loop(0, CHAN, chunk_a, 0)

    for load in loads[3:]:
        load.wait()
    turn(1)
    for u in range(2):
        gt[u] = jnp.transpose(gw_ref[u].astype(F32)).astype(BF16)
        ot[u] = jnp.transpose(ow_ref[u].astype(F32)).astype(BF16)
        gains[2 + u] = column(hg_ref[u : u + 1, :])
    gains[1] = column(ng_ref[1:2, :])

    def gate_out(i, carry):
        gate0[i] = sigmoid(dot(gt[0], n_buf[i]))
        return carry

    lax.fori_loop(0, R, gate_out, 0, unroll=8)

    pltpu.make_async_copy(recv_a, recv_a, a_rsem).wait()

    per = K // R

    def send_b(r2, b2):
        c2 = column_chan(r2, b2)
        src = out_b.at[b2, pl.ds(pl.multiple_of(r2 * R, R), R)]
        dst = recv_b.at[hid]
        own = jnp.logical_and(r2 == r, c2 == c)

        @pl.when(own)
        def _():
            pltpu.make_async_copy(src, dst, b_rsem).start()

        @pl.when(jnp.logical_not(own))
        def _():
            pltpu.make_async_remote_copy(
                src, dst, b_ssem, b_rsem, device_id=(r2, c2), device_id_type=MESH
            ).start()

    def chunk_b(s, carry):
        b = lax.rem(s + r // 8, TOK // K)
        rows = pl.ds(pl.multiple_of(b * K, K), K)
        left = jnp.concatenate([recv_a[0, n, rows, :] for n in range(TOK // K)], axis=1)
        right = jnp.concatenate([recv_a[1, n] for n in range(TOK // K)], axis=1)
        total = dot(left, right, ((1,), (1,))).astype(BF16)
        for n in range(TOK // K):
            out_b[n, rows, :] = total[:, n * K : (n + 1) * K]

        def send(t, carry):
            v = lax.rem(t * 5 + r * CHAN + c, per * 2)
            send_b(b * per + v // 2, lax.rem(v, 2))
            return carry

        lax.fori_loop(0, per * 2, send, 0)
        return carry

    lax.fori_loop(0, TOK // K, chunk_b, 0)

    def late_b(t, carry):
        v = lax.rem(t * SPREAD + r * CHAN + c, ROWS * 2)
        send_b(v // 2, 2 + lax.rem(v, 2))
        return carry

    lax.fori_loop(0, ROWS * 2, late_b, 0)

    pltpu.make_async_copy(recv_b, recv_b, b_rsem).wait()
    norm_hidden(recv_b, z0)

    def update_out(i, carry):
        h = (z0[pl.ds(i, H, stride=R), :] * gains[2]).astype(BF16)
        m = (x_buf[i].astype(F32) + gate0[i] * dot(ot[0], h)).astype(BF16)
        mid[i] = m
        n_buf[i] = norm_rows(m.astype(F32), gains[1])
        return carry

    lax.fori_loop(0, R, update_out, 0, unroll=8)

    def chunk_c(s, carry):
        q = lax.rem(s + r, CHAN)
        project(1, q, send_c)

        def send(t, carry):
            r2 = lax.rem(r + t * SPREAD, ROWS)
            h2 = q * ROWS + r2
            right_src, right_dst = send_c.at[h2, 1], right_c.at[mine, my_rows]

            @pl.when(h2 == hid)
            def _():
                pltpu.make_async_copy(right_src, right_dst, cr_rsem).start()

            @pl.when(h2 != hid)
            def _():
                pltpu.make_async_remote_copy(
                    right_src, right_dst, cr_ssem, cr_rsem, device_id=(r2, q), device_id_type=MESH
                ).start()

            @pl.when(mine < BLOCKS)
            def _():
                left_src, left_dst = send_c.at[h2, 0], left_c.at[mine, my_rows]

                @pl.when(h2 == hid)
                def _():
                    pltpu.make_async_copy(left_src, left_dst, cl_rsem).start()

                @pl.when(h2 != hid)
                def _():
                    pltpu.make_async_remote_copy(
                        left_src, left_dst, cl_ssem, cl_rsem,
                        device_id=(r2, q), device_id_type=MESH,
                    ).start()

            return carry

        lax.fori_loop(0, ROWS, send, 0)
        return carry

    lax.fori_loop(0, CHAN, chunk_c, 0)

    sends_m = r * R < WIN
    row_block = r // per
    m_rows = pl.ds(pl.multiple_of(lax.rem(r, per) * R, R), R)

    def m_copy(n):
        g = lax.rem(n + r, per)
        r2 = mine * per + g
        m_chan = column_chan(r2, row_block)
        src = send_m.at[pl.ds(pl.multiple_of(g * R, R), R)]
        dst = recv_m.at[:, m_rows, :]
        own = jnp.logical_and(r2 == r, m_chan == c)
        local = lambda: pltpu.make_async_copy(src, dst, m_rsem)
        remote = lambda: pltpu.make_async_remote_copy(
            src, dst, m_ssem.at[g], m_rsem, device_id=(r2, m_chan), device_id_type=MESH
        )
        return own, local, remote

    @pl.when(sends_m)
    def _():
        def turn_mid(i, carry):
            z0[pl.ds(i, K, stride=R), :] = jnp.transpose(mid[i].astype(F32))
            return carry

        lax.fori_loop(0, R, turn_mid, 0, unroll=8)

        def pack(j, carry):
            send_m[j] = z0[pl.ds(pl.multiple_of(j * R, R), R), :].astype(BF16)
            return carry

        lax.fori_loop(0, K, pack, 0, unroll=8)

        def send(g, carry):
            own, local, remote = m_copy(g)

            @pl.when(own)
            def _():
                local().start()

            @pl.when(jnp.logical_not(own))
            def _():
                remote().start()

            return carry

        lax.fori_loop(0, per, send, 0)

    pltpu.make_async_copy(left_c, left_c, cl_rsem).wait()
    pltpu.make_async_copy(right_c, right_c, cr_rsem).wait()

    tail = WIN - (BLOCKS - 1) * K
    group = K // tail

    def chunk_d(s, carry):
        b = lax.rem(s + r // 8, TOK // K)
        cols = pl.ds(pl.multiple_of(b * K, K), K)
        left = jnp.concatenate([left_c[n] for n in range(BLOCKS)], axis=1)
        total = dot(right_c[b], left, ((0,), (0,))).astype(BF16)
        for n in range(BLOCKS):
            out_d[n, cols, :] = total[:, n * K : (n + 1) * K]

        def send(t, carry):
            v = lax.rem(t * 5 + r * CHAN + c, per * BLOCKS)
            r2 = b * per + v // BLOCKS
            b2 = lax.rem(v, BLOCKS)
            c2 = column_chan(r2, b2)
            src = out_d.at[b2, pl.ds(pl.multiple_of(r2 * R, R), R)]
            dst = recv_d.at[hid]
            own = jnp.logical_and(r2 == r, c2 == c)

            @pl.when(own)
            def _():
                pltpu.make_async_copy(src, dst, d_rsem).start()

            @pl.when(jnp.logical_not(own))
            def _():
                pltpu.make_async_remote_copy(
                    src, dst, d_ssem, d_rsem, device_id=(r2, c2), device_id_type=MESH
                ).start()

            return carry

        lax.fori_loop(0, per * BLOCKS, send, 0)
        return carry

    lax.fori_loop(0, TOK // K, chunk_d, 0)

    @pl.when(block < BLOCKS)
    def _():
        @pl.when(block < BLOCKS - 1)
        def _():
            pltpu.make_async_copy(recv_m, recv_m, m_rsem).wait()

        @pl.when(block == BLOCKS - 1)
        def _():
            part = recv_m.at[:, pl.ds(0, tail), :]
            pltpu.make_async_copy(part, part, m_rsem).wait()

        def gate_in(j, carry):
            m = jnp.transpose(recv_m[j].astype(F32))
            resid[j] = m.astype(BF16)
            gate1[j] = sigmoid(dot(gt[1], norm_rows(m, gains[1])))
            return carry

        lax.fori_loop(0, R, gate_in, 0, unroll=8)

        pltpu.make_async_copy(recv_d, recv_d, d_rsem).wait()
        norm_hidden(recv_d, z1)

        def update_in(g, carry):
            first = pl.multiple_of(g * group, group)
            parts = []
            for t in range(group):
                h = (z1[pl.ds(first + t, H, stride=R), :] * gains[3]).astype(BF16)
                parts.append(
                    (resid[first + t].astype(F32) + gate1[first + t] * dot(ot[1], h)).astype(BF16)
                )

            def send(src, dst, sem):
                def one(s, carry):
                    c2 = lax.rem(c + 1 + s, CHAN)
                    rows = pl.ds(pl.multiple_of(c2 * share, share), share)

                    @pl.when(c2 == c)
                    def _():
                        pltpu.make_async_copy(src(rows), dst, sem).start()

                    @pl.when(c2 != c)
                    def _():
                        pltpu.make_async_remote_copy(
                            src(rows), dst, e_ssem, sem, device_id=(r, c2), device_id_type=MESH
                        ).start()

                    return carry

                lax.fori_loop(0, CHAN, one, 0)

            @pl.when(block < BLOCKS - 1)
            def _():
                for t in range(group):
                    out_e[first + t] = parts[t]
                some = pl.ds(first, group)
                send(lambda rows: out_e.at[some, rows, :], recv_e.at[block, some], e_rsem)

            @pl.when(block == BLOCKS - 1)
            def _():
                out_t[g] = jnp.concatenate([part[:, :tail] for part in parts], axis=1)
                send(lambda rows: out_t.at[g, rows, :], recv_t.at[g], t_rsem)

            return carry

        lax.fori_loop(0, R // group, update_in, 0)

    pltpu.make_async_copy(recv_t, recv_t, t_rsem).wait()
    for g in range(R // group):
        for t in range(group):
            out_ref[g * group + t, :, WIN - tail :] = recv_t[g, :, t * tail : (t + 1) * tail]
    pltpu.make_async_copy(recv_e, recv_e, e_rsem).wait()
    for b in range(BLOCKS - 1):
        out_ref[:, :, b * K : (b + 1) * K] = recv_e[b]

    def drain(ref, sem):
        pltpu.make_async_copy(ref, ref, sem).wait()

    drain(send_a.at[pl.ds(0, DEV - 1)], a_ssem)
    drain(recv_b.at[pl.ds(0, DEV - 1)], b_ssem)
    drain(recv_b.at[pl.ds(0, DEV - 1)], cr_ssem)

    @pl.when(mine < BLOCKS)
    def _():
        drain(recv_b.at[pl.ds(0, DEV - 1)], cl_ssem)

    @pl.when(block < BLOCKS)
    def _():
        drain(recv_b.at[pl.ds(0, ROWS * BLOCKS - 1)], d_ssem)

    @pl.when(block == BLOCKS)
    def _():
        drain(recv_b.at[pl.ds(0, ROWS * BLOCKS)], d_ssem)

    tiles = R * share // R

    @pl.when(block < BLOCKS - 1)
    def _():
        drain(recv_b.at[pl.ds(0, (CHAN - 1) * tiles)], e_ssem)

    @pl.when(block == BLOCKS - 1)
    def _():
        drain(recv_b.at[pl.ds(0, (CHAN - 1) * tiles // group)], e_ssem)

    @pl.when(sends_m)
    def _():
        def done(g, carry):
            own, _local, remote = m_copy(g)

            @pl.when(jnp.logical_not(own))
            def _():
                remote().wait_send()

            return carry

        lax.fori_loop(0, per, done, 0)


def shards(pair, norm_gain, proj_weight, gate_weight, hidden_gain, out_weight):
    vmem = pl.BlockSpec(memory_space=pltpu.VMEM)
    sem = pltpu.SemaphoreType.DMA
    tiles = lambda n: pltpu.VMEM((n, R, K), BF16)
    return pl.pallas_call(
        kernel,
        out_shape=jax.ShapeDtypeStruct((R, C // CHAN, WIN), BF16),
        in_specs=[pl.BlockSpec(memory_space=pltpu.HBM)] * 6,
        out_specs=vmem,
        scratch_shapes=[
            pltpu.VMEM((2, C), F32),
            pltpu.VMEM((2, 4, C, H), BF16),
            pltpu.VMEM((2, C, C), BF16),
            pltpu.VMEM((2, H), F32),
            pltpu.VMEM((2, H, C), BF16),
            pltpu.VMEM((R, C, K), BF16),
            pltpu.VMEM((R, C, K), BF16),
            pltpu.VMEM((2, CHAN, 4 * H // CHAN, C), BF16),
            pltpu.VMEM((2, C, C), BF16),
            pltpu.VMEM((2, C, H), BF16),
            pltpu.VMEM((4, C, K), F32),
            pltpu.VMEM((H * R, K), F32),
            pltpu.VMEM((H * R, K), F32),
            pltpu.VMEM((H, 2, R, K), BF16),
            pltpu.VMEM((2, CHAN, TOK, K), BF16),
            pltpu.VMEM((CHAN, TOK, K), BF16),
            tiles(H),
            pltpu.VMEM((R, C, K), F32),
            pltpu.VMEM((R, C, K), BF16),
            pltpu.VMEM((H, 2, R, K), BF16),
            pltpu.VMEM((BLOCKS, TOK, K), BF16),
            pltpu.VMEM((CHAN, TOK, K), BF16),
            pltpu.VMEM((K, R, C), BF16),
            pltpu.VMEM((R, K, C), BF16),
            pltpu.VMEM((BLOCKS, TOK, K), BF16),
            tiles(H),
            pltpu.VMEM((R, C, K), F32),
            pltpu.VMEM((R, C, K), BF16),
            pltpu.VMEM((R, C, K), BF16),
            pltpu.VMEM((R // 4, C, K), BF16),
            pltpu.VMEM((BLOCKS - 1, R, C // CHAN, K), BF16),
            pltpu.VMEM((R // 4, C // CHAN, K), BF16),
            sem((6,)), sem, sem, sem, sem, sem, sem, sem, sem,
            sem((K // R,)), sem, sem, sem, sem, sem, sem,
        ],
        compiler_params=pltpu.CompilerParams(
            collective_id=0, has_side_effects=True, vmem_limit_bytes=VMEM_BYTES
        ),
    )(pair, norm_gain, proj_weight, gate_weight, hidden_gain, out_weight)


def solution(mesh):
    in_specs = (P("rows", None, None), P(), P(), P(), P(), P())
    out_specs = P("rows", "chan", None)
    return jax.shard_map(shards, mesh=mesh, in_specs=in_specs, out_specs=out_specs, check_vma=False)
```

```python
import functools

import jax
import jax.numpy as jnp
from jax import lax
from jax.experimental import pallas as pl
from jax.experimental.pallas import tpu as pltpu
from jax.sharding import PartitionSpec as P

MESH = pl.DeviceIdType.MESH
F32 = jnp.float32
BF16 = jnp.bfloat16
C = 128
H = 128
TOK = 512
WIN = 288
ROWS = 32
CHAN = 4
DEV = ROWS * CHAN
R = TOK // ROWS
K = TOK // CHAN
BLOCKS = 3
SPREAD = 37
VMEM_BYTES = 63 * 1024 * 1024


def swap(n):
    return 2 * lax.rem(n, 2) + n // 2


def turned(r):
    return lax.rem(r // 2 + r // 8, 2)


def column_block(r, c):
    return swap(lax.rem(c + 2 * turned(r), CHAN))


def column_chan(r, b):
    return lax.rem(swap(b) + 2 * turned(r), CHAN)


def far_first(n):
    return jnp.where(n == 0, 2, jnp.where(n == 3, 0, 2 * n - 1))


def row_plane(r, s):
    return lax.rem(r // 8 + far_first(s), 4)


def row_in_plane(r, plane, t):
    x = lax.rem(r // 2 + far_first(t // 2), 4)
    return plane * 8 + x * 2 + lax.rem(r + 1 + t, 2)


def sigmoid(v):
    return 0.5 * jnp.tanh(0.5 * v) + 0.5


def norm_rows(x, gain):
    average = jnp.mean(x, axis=0, keepdims=True)
    centred = x - average
    spread = jnp.mean(centred * centred, axis=0, keepdims=True)
    return (centred * lax.rsqrt(spread + 1e-05) * gain).astype(BF16)


def take_hidden(src, sem, z, stat, r):
    planes, lanes = 4, 4
    near = H // CHAN // planes
    steps = CHAN * near // lanes

    def plane_of(s):
        return lax.rem(r // 8 + planes - far_first(s), planes)

    def some(plane, n):
        first = n * lanes // near * (H // CHAN) + plane * near + lax.rem(n * lanes, near)
        return pl.multiple_of(first, lanes)

    def load(first):
        return src[pl.ds(first, lanes)].astype(F32)

    zero = jnp.zeros((lanes, R, K), F32)
    pivot = None
    sums = (zero, zero)
    for s in range(planes):
        plane = plane_of(s)
        landed = src.at[pl.ds(0, CHAN * near)]
        pltpu.make_async_copy(landed, landed, sem.at[plane]).wait()
        if s == 0:
            total = lax.fori_loop(
                0, steps, lambda n, t: t + load(some(plane, n)), zero, unroll=True
            )
            pivot = jnp.sum(total, axis=0) * (1.0 / (CHAN * near))

        def add(n, carry):
            first = some(plane, n)
            x = load(first)
            rows = pl.ds(pl.multiple_of(first * R, lanes * R), lanes * R)
            z[rows, :] = x.reshape(lanes * R, K)
            d = x - pivot
            return carry[0] + d, carry[1] + d * d

        sums = lax.fori_loop(0, steps, add, sums, unroll=True)
    shift = jnp.sum(sums[0], axis=0) * (1.0 / H)
    spread = jnp.sum(sums[1], axis=0) * (1.0 / H) - shift * shift
    stat[0] = pivot + shift
    stat[1] = lax.rsqrt(spread + 1e-05)


def normed_hidden(z, stat, gain, i):
    row = pl.ds(i, 1)
    return ((z[pl.ds(i, H, stride=R), :] - stat[0, row, :]) * stat[1, row, :] * gain).astype(BF16)


def dot(a, b, dims=((1,), (0,))):
    return lax.dot_general(a, b, (dims, ((), ())), preferred_element_type=F32)


def kernel(
    pair_hbm, ng_hbm, pw_hbm, gw_hbm, hg_hbm, ow_hbm, out_ref,
    ng_ref, pw_ref, gw_ref, hg_ref, ow_ref, x_buf, n_buf, wt, gt, ot, gains, z0, z1,
    send_a, recv_a, out_b, recv_b, gate0, mid,
    send_c, left_c, right_c, send_m, recv_m, out_d, recv_d, stat, gate1, resid, out_e, out_t, recv_e, recv_t,
    load_sem, a_ssem, a_rsem, b_ssem, b_rsem, cl_ssem, cr_ssem, cl_rsem, cr_rsem,
    m_ssem, m_rsem, d_ssem, d_rsem, e_ssem, e_rsem, t_rsem,
):
    r = lax.axis_index("rows")
    c = lax.axis_index("chan")
    hid = c * ROWS + r
    mine = column_block(r, c)
    block = mine

    loads = [
        pltpu.make_async_copy(src, dst, load_sem.at[n])
        for n, (src, dst) in enumerate(
            [
                (pw_hbm, pw_ref),
                (ng_hbm, ng_ref),
                (pair_hbm.at[:, :, pl.ds(pl.multiple_of(mine * K, K), K)], x_buf),
                (gw_hbm, gw_ref),
                (ow_hbm, ow_ref),
                (hg_hbm, hg_ref),
            ]
        )
    ]
    for load in loads:
        load.start()

    barrier = pltpu.get_barrier_semaphore()

    def greet(n, carry):
        r2 = r + n
        r2 = jnp.where(r2 >= ROWS, r2 - ROWS, r2)
        for m in range(CHAN):
            c2 = c + m
            c2 = jnp.where(c2 >= CHAN, c2 - CHAN, c2)
            pl.semaphore_signal(barrier, inc=1, device_id=(r2, c2), device_id_type=MESH)
        return carry

    lax.fori_loop(0, ROWS, greet, 0, unroll=4)

    share = H // CHAN

    def turn(u):
        def one(m, carry):
            w = jnp.transpose(pw_ref[u, m].astype(F32)).astype(BF16)
            for q in range(CHAN):
                wt[u, q, pl.ds(pl.multiple_of(m * share, share), share), :] = w[
                    q * share : (q + 1) * share
                ]
            return carry

        lax.fori_loop(0, 4, one, 0)

    def column(row):
        return jnp.transpose(jnp.broadcast_to(row, (C, C)))

    loads[0].wait()
    turn(0)
    loads[1].wait()
    gains[0] = column(ng_ref[0:1, :])
    loads[2].wait()

    def norm_in(i, carry):
        n_buf[i] = norm_rows(x_buf[i].astype(F32), gains[0])
        return carry

    lax.fori_loop(0, R, norm_in, 0, unroll=8)

    def project(u, q, dst):
        def one(i, carry):
            y = dot(wt[u, q], n_buf[i])
            z0[pl.ds(i, share, stride=R), :] = sigmoid(y[share : 2 * share]) * y[:share]
            z1[pl.ds(i, share, stride=R), :] = (
                sigmoid(y[3 * share :]) * y[2 * share : 3 * share]
            )
            return carry

        lax.fori_loop(0, R, one, 0, unroll=8)

        def pack(h, carry):
            rows = pl.ds(pl.multiple_of(h * R, R), R)
            dst[q * share + h, 0] = z0[rows, :].astype(BF16)
            dst[q * share + h, 1] = z1[rows, :].astype(BF16)
            return carry

        lax.fori_loop(0, share, pack, 0, unroll=8)

    my_rows = pl.ds(pl.multiple_of(r * R, R), R)

    def chunk_a(s, carry):
        q = lax.rem(s + r, CHAN)
        project(0, q, send_a)

        @pl.when(s == 0)
        def _():
            pl.semaphore_wait(barrier, DEV)

        def send(t, carry):
            r2 = row_in_plane(r, row_plane(r, t // 8), lax.rem(t, 8))
            h2 = q * ROWS + r2
            src = send_a.at[h2]
            dst = recv_a.at[:, mine, my_rows]

            @pl.when(h2 == hid)
            def _():
                pltpu.make_async_copy(src, dst, a_rsem).start()

            @pl.when(h2 != hid)
            def _():
                pltpu.make_async_remote_copy(
                    src, dst, a_ssem, a_rsem, device_id=(r2, q), device_id_type=MESH
                ).start()

            return carry

        lax.fori_loop(0, ROWS, send, 0)
        return carry

    lax.fori_loop(0, CHAN, chunk_a, 0)

    for load in loads[3:]:
        load.wait()
    turn(1)
    for u in range(2):
        gt[u] = jnp.transpose(gw_ref[u].astype(F32)).astype(BF16)
        ot[u] = jnp.transpose(ow_ref[u].astype(F32)).astype(BF16)
        gains[2 + u] = column(hg_ref[u : u + 1, :])
    gains[1] = column(ng_ref[1:2, :])

    def gate_out(i, carry):
        gate0[i] = sigmoid(dot(gt[0], n_buf[i]))
        return carry

    lax.fori_loop(0, R, gate_out, 0, unroll=8)

    pltpu.make_async_copy(recv_a, recv_a, a_rsem).wait()

    per = K // R

    def send_b(r2, b2):
        c2 = column_chan(r2, b2)
        src = out_b.at[b2, pl.ds(pl.multiple_of(r2 * R, R), R)]
        dst = recv_b.at[hid]
        own = jnp.logical_and(r2 == r, c2 == c)

        @pl.when(own)
        def _():
            pltpu.make_async_copy(src, dst, b_rsem.at[r // 8]).start()

        @pl.when(jnp.logical_not(own))
        def _():
            pltpu.make_async_remote_copy(
                src, dst, b_ssem, b_rsem.at[r // 8], device_id=(r2, c2), device_id_type=MESH
            ).start()

    def chunk_b(s, carry):
        b = row_plane(r, s)
        rows = pl.ds(pl.multiple_of(b * K, K), K)
        left = jnp.concatenate([recv_a[0, n, rows, :] for n in range(TOK // K)], axis=1)
        right = jnp.concatenate([recv_a[1, n] for n in range(TOK // K)], axis=1)
        total = dot(left, right, ((1,), (1,))).astype(BF16)
        for n in range(TOK // K):
            out_b[n, rows, :] = total[:, n * K : (n + 1) * K]

        def send(t, carry):
            send_b(row_in_plane(r, b, t // 2), lax.rem(t + c, 2))
            return carry

        lax.fori_loop(0, per * 2, send, 0)
        return carry

    lax.fori_loop(0, TOK // K, chunk_b, 0)

    def late_b(t, carry):
        send_b(row_in_plane(r, row_plane(r, t // 16), lax.rem(t, 16) // 2), 2 + lax.rem(t + c, 2))
        return carry

    lax.fori_loop(0, ROWS * 2, late_b, 0)

    take_hidden(recv_b, b_rsem, z0, stat, r)

    def update_out(i, carry):
        h = normed_hidden(z0, stat, gains[2], i)
        m = (x_buf[i].astype(F32) + gate0[i] * dot(ot[0], h)).astype(BF16)
        mid[i] = m
        n_buf[i] = norm_rows(m.astype(F32), gains[1])
        return carry

    lax.fori_loop(0, R, update_out, 0, unroll=8)

    def chunk_c(s, carry):
        q = lax.rem(s + r, CHAN)
        project(1, q, send_c)

        def send(t, carry):
            r2 = row_in_plane(r, row_plane(r, t // 8), lax.rem(t, 8))
            h2 = q * ROWS + r2
            right_src, right_dst = send_c.at[h2, 1], right_c.at[mine, my_rows]

            @pl.when(h2 == hid)
            def _():
                pltpu.make_async_copy(right_src, right_dst, cr_rsem).start()

            @pl.when(h2 != hid)
            def _():
                pltpu.make_async_remote_copy(
                    right_src, right_dst, cr_ssem, cr_rsem, device_id=(r2, q), device_id_type=MESH
                ).start()

            @pl.when(mine < BLOCKS)
            def _():
                left_src, left_dst = send_c.at[h2, 0], left_c.at[mine, my_rows]

                @pl.when(h2 == hid)
                def _():
                    pltpu.make_async_copy(left_src, left_dst, cl_rsem).start()

                @pl.when(h2 != hid)
                def _():
                    pltpu.make_async_remote_copy(
                        left_src, left_dst, cl_ssem, cl_rsem,
                        device_id=(r2, q), device_id_type=MESH,
                    ).start()

            return carry

        lax.fori_loop(0, ROWS, send, 0)
        return carry

    lax.fori_loop(0, CHAN, chunk_c, 0)

    sends_m = r * R < WIN
    row_block = r // per
    m_rows = pl.ds(pl.multiple_of(lax.rem(r, per) * R, R), R)

    def m_copy(n):
        g = lax.rem(n + r, per)
        r2 = mine * per + g
        m_chan = column_chan(r2, row_block)
        src = send_m.at[pl.ds(pl.multiple_of(g * R, R), R)]
        dst = recv_m.at[:, m_rows, :]
        own = jnp.logical_and(r2 == r, m_chan == c)
        local = lambda: pltpu.make_async_copy(src, dst, m_rsem)
        remote = lambda: pltpu.make_async_remote_copy(
            src, dst, m_ssem.at[g], m_rsem, device_id=(r2, m_chan), device_id_type=MESH
        )
        return own, local, remote

    @pl.when(sends_m)
    def _():
        def turn_mid(i, carry):
            z0[pl.ds(i, K, stride=R), :] = jnp.transpose(mid[i].astype(F32))
            return carry

        lax.fori_loop(0, R, turn_mid, 0, unroll=8)

        def pack(j, carry):
            send_m[j] = z0[pl.ds(pl.multiple_of(j * R, R), R), :].astype(BF16)
            return carry

        lax.fori_loop(0, K, pack, 0, unroll=8)

        def send(g, carry):
            own, local, remote = m_copy(g)

            @pl.when(own)
            def _():
                local().start()

            @pl.when(jnp.logical_not(own))
            def _():
                remote().start()

            return carry

        lax.fori_loop(0, per, send, 0)

    pltpu.make_async_copy(left_c, left_c, cl_rsem).wait()
    pltpu.make_async_copy(right_c, right_c, cr_rsem).wait()

    tail = WIN - (BLOCKS - 1) * K
    group = K // tail

    def chunk_d(s, carry):
        b = row_plane(r, s)
        cols = pl.ds(pl.multiple_of(b * K, K), K)
        left = jnp.concatenate([left_c[n] for n in range(BLOCKS)], axis=1)
        total = dot(right_c[b], left, ((0,), (0,))).astype(BF16)
        for n in range(BLOCKS):
            out_d[n, cols, :] = total[:, n * K : (n + 1) * K]

        def send(t, carry):
            r2 = row_in_plane(r, b, t // BLOCKS)
            b2 = lax.rem(t + c, BLOCKS)
            c2 = column_chan(r2, b2)
            src = out_d.at[b2, pl.ds(pl.multiple_of(r2 * R, R), R)]
            dst = recv_d.at[hid]
            own = jnp.logical_and(r2 == r, c2 == c)

            @pl.when(own)
            def _():
                pltpu.make_async_copy(src, dst, d_rsem.at[r // 8]).start()

            @pl.when(jnp.logical_not(own))
            def _():
                pltpu.make_async_remote_copy(
                    src, dst, d_ssem, d_rsem.at[r // 8], device_id=(r2, c2), device_id_type=MESH
                ).start()

            return carry

        lax.fori_loop(0, per * BLOCKS, send, 0)
        return carry

    lax.fori_loop(0, TOK // K, chunk_d, 0)

    @pl.when(block < BLOCKS)
    def _():
        @pl.when(block < BLOCKS - 1)
        def _():
            pltpu.make_async_copy(recv_m, recv_m, m_rsem).wait()

        @pl.when(block == BLOCKS - 1)
        def _():
            part = recv_m.at[:, pl.ds(0, tail), :]
            pltpu.make_async_copy(part, part, m_rsem).wait()

        def gate_in(j, carry):
            m = jnp.transpose(recv_m[j].astype(F32))
            resid[j] = m.astype(BF16)
            gate1[j] = sigmoid(dot(gt[1], norm_rows(m, gains[1])))
            return carry

        lax.fori_loop(0, R, gate_in, 0, unroll=8)

        take_hidden(recv_d, d_rsem, z1, stat, r)

        def update_in(j):
            h = normed_hidden(z1, stat, gains[3], j)
            return (resid[j].astype(F32) + gate1[j] * dot(ot[1], h)).astype(BF16)

        def send(src, dst, sem):
            for s in range(1, CHAN):
                c2 = lax.rem(c + s, CHAN)
                rows = pl.ds(pl.multiple_of(c2 * share, share), share)
                pltpu.make_async_remote_copy(
                    src.at[..., rows, :], dst, e_ssem, sem, device_id=(r, c2), device_id_type=MESH
                ).start()
            rows = pl.ds(pl.multiple_of(c * share, share), share)
            pltpu.make_async_copy(src.at[..., rows, :], dst, sem).start()

        @pl.when(block < BLOCKS - 1)
        def _():
            def whole(g, carry):
                first = pl.multiple_of(g * group, group)
                for t in range(group):
                    out_e[first + t] = update_in(first + t)
                some = pl.ds(first, group)
                send(out_e.at[some], recv_e.at[block, some], e_rsem)
                return carry

            lax.fori_loop(0, R // group, whole, 0)

        @pl.when(block == BLOCKS - 1)
        def _():
            def packed(g, carry):
                first = pl.multiple_of(g * group, group)
                parts = [update_in(first + t)[:, :tail] for t in range(group)]
                out_t[g] = jnp.concatenate(parts, axis=1)
                send(out_t.at[g], recv_t.at[g], t_rsem)
                return carry

            lax.fori_loop(0, R // group, packed, 0)

    pltpu.make_async_copy(recv_t, recv_t, t_rsem).wait()
    for g in range(R // group):
        for t in range(group):
            out_ref[g * group + t, :, WIN - tail :] = recv_t[g, :, t * tail : (t + 1) * tail]
    pltpu.make_async_copy(recv_e, recv_e, e_rsem).wait()
    for b in range(BLOCKS - 1):
        out_ref[:, :, b * K : (b + 1) * K] = recv_e[b]

    def drain(ref, sem):
        pltpu.make_async_copy(ref, ref, sem).wait()

    drain(send_a.at[pl.ds(0, DEV - 1)], a_ssem)
    drain(recv_b.at[pl.ds(0, DEV - 1)], b_ssem)
    drain(recv_b.at[pl.ds(0, DEV - 1)], cr_ssem)

    @pl.when(mine < BLOCKS)
    def _():
        drain(recv_b.at[pl.ds(0, DEV - 1)], cl_ssem)

    @pl.when(block < BLOCKS)
    def _():
        drain(recv_b.at[pl.ds(0, ROWS * BLOCKS - 1)], d_ssem)

    @pl.when(block == BLOCKS)
    def _():
        drain(recv_b.at[pl.ds(0, ROWS * BLOCKS)], d_ssem)

    tiles = R * share // R

    @pl.when(block < BLOCKS - 1)
    def _():
        drain(recv_b.at[pl.ds(0, (CHAN - 1) * tiles)], e_ssem)

    @pl.when(block == BLOCKS - 1)
    def _():
        drain(recv_b.at[pl.ds(0, (CHAN - 1) * tiles // group)], e_ssem)

    @pl.when(sends_m)
    def _():
        def done(g, carry):
            own, _local, remote = m_copy(g)

            @pl.when(jnp.logical_not(own))
            def _():
                remote().wait_send()

            return carry

        lax.fori_loop(0, per, done, 0)


def shards(pair, norm_gain, proj_weight, gate_weight, hidden_gain, out_weight):
    vmem = pl.BlockSpec(memory_space=pltpu.VMEM)
    sem = pltpu.SemaphoreType.DMA
    tiles = lambda n: pltpu.VMEM((n, R, K), BF16)
    return pl.pallas_call(
        kernel,
        out_shape=jax.ShapeDtypeStruct((R, C // CHAN, WIN), BF16),
        in_specs=[pl.BlockSpec(memory_space=pltpu.HBM)] * 6,
        out_specs=vmem,
        scratch_shapes=[
            pltpu.VMEM((2, C), F32),
            pltpu.VMEM((2, 4, C, H), BF16),
            pltpu.VMEM((2, C, C), BF16),
            pltpu.VMEM((2, H), F32),
            pltpu.VMEM((2, H, C), BF16),
            pltpu.VMEM((R, C, K), BF16),
            pltpu.VMEM((R, C, K), BF16),
            pltpu.VMEM((2, CHAN, 4 * H // CHAN, C), BF16),
            pltpu.VMEM((2, C, C), BF16),
            pltpu.VMEM((2, C, H), BF16),
            pltpu.VMEM((4, C, K), F32),
            pltpu.VMEM((H * R, K), F32),
            pltpu.VMEM((H * R, K), F32),
            pltpu.VMEM((H, 2, R, K), BF16),
            pltpu.VMEM((2, CHAN, TOK, K), BF16),
            pltpu.VMEM((CHAN, TOK, K), BF16),
            tiles(H),
            pltpu.VMEM((R, C, K), F32),
            pltpu.VMEM((R, C, K), BF16),
            pltpu.VMEM((H, 2, R, K), BF16),
            pltpu.VMEM((BLOCKS, TOK, K), BF16),
            pltpu.VMEM((CHAN, TOK, K), BF16),
            pltpu.VMEM((K, R, C), BF16),
            pltpu.VMEM((R, K, C), BF16),
            pltpu.VMEM((BLOCKS, TOK, K), BF16),
            tiles(H),
            pltpu.VMEM((2, R, K), F32),
            pltpu.VMEM((R, C, K), F32),
            pltpu.VMEM((R, C, K), BF16),
            pltpu.VMEM((R, C, K), BF16),
            pltpu.VMEM((R // 4, C, K), BF16),
            pltpu.VMEM((BLOCKS - 1, R, C // CHAN, K), BF16),
            pltpu.VMEM((R // 4, C // CHAN, K), BF16),
            sem((6,)), sem, sem, sem, sem((4,)), sem, sem, sem, sem,
            sem((K // R,)), sem, sem, sem((4,)), sem, sem, sem,
        ],
        compiler_params=pltpu.CompilerParams(
            collective_id=0, has_side_effects=True, vmem_limit_bytes=VMEM_BYTES
        ),
    )(pair, norm_gain, proj_weight, gate_weight, hidden_gain, out_weight)


def solution(mesh):
    in_specs = (P("rows", None, None), P(), P(), P(), P(), P())
    out_specs = P("rows", "chan", None)
    return jax.shard_map(shards, mesh=mesh, in_specs=in_specs, out_specs=out_specs, check_vma=False)
```

```python
import functools

import jax
import jax.numpy as jnp
from jax import lax
from jax.experimental import pallas as pl
from jax.experimental.pallas import tpu as pltpu
from jax.sharding import PartitionSpec as P

MESH = pl.DeviceIdType.MESH
F32 = jnp.float32
BF16 = jnp.bfloat16
C = 128
H = 128
TOK = 512
WIN = 288
ROWS = 32
CHAN = 4
DEV = ROWS * CHAN
R = TOK // ROWS
K = TOK // CHAN
BLOCKS = 3
SPREAD = 37
VMEM_BYTES = 63 * 1024 * 1024


def swap(n):
    return 2 * lax.rem(n, 2) + n // 2


def turned(r):
    return lax.rem(r // 2 + r // 8, 2)


def column_block(r, c):
    return swap(lax.rem(c + 2 * turned(r), CHAN))


def column_chan(r, b):
    return lax.rem(swap(b) + 2 * turned(r), CHAN)


def far_first(n):
    return jnp.where(n == 0, 2, jnp.where(n == 3, 0, 2 * n - 1))


def row_plane(r, s):
    return lax.rem(r // 8 + far_first(s), 4)


def row_in_plane(r, plane, t):
    x = lax.rem(r // 2 + far_first(t // 2), 4)
    return plane * 8 + x * 2 + lax.rem(r + 1 + t, 2)


def sigmoid(v):
    return 0.5 * jnp.tanh(0.5 * v) + 0.5


def norm_rows(x, gain):
    average = jnp.mean(x, axis=0, keepdims=True)
    centred = x - average
    spread = jnp.mean(centred * centred, axis=0, keepdims=True)
    return (centred * lax.rsqrt(spread + 1e-05) * gain).astype(BF16)


def take_hidden(src, sem, z, stat, r):
    planes, lanes = 4, 4
    near = H // CHAN // planes
    steps = CHAN * near // lanes

    def plane_of(s):
        return lax.rem(r // 8 + planes - far_first(s), planes)

    def some(plane, n):
        first = n * lanes // near * (H // CHAN) + plane * near + lax.rem(n * lanes, near)
        return pl.multiple_of(first, lanes)

    def load(first):
        return src[pl.ds(first, lanes)].astype(F32)

    zero = jnp.zeros((lanes, R, K), F32)
    pivot = None
    sums = (zero, zero)
    for s in range(planes):
        plane = plane_of(s)
        landed = src.at[pl.ds(0, CHAN * near)]
        pltpu.make_async_copy(landed, landed, sem.at[plane]).wait()
        if s == 0:
            total = lax.fori_loop(
                0, steps, lambda n, t: t + load(some(plane, n)), zero, unroll=True
            )
            pivot = jnp.sum(total, axis=0) * (1.0 / (CHAN * near))

        def add(n, carry):
            first = some(plane, n)
            x = load(first)
            rows = pl.ds(pl.multiple_of(first * R, lanes * R), lanes * R)
            z[rows, :] = x.reshape(lanes * R, K)
            d = x - pivot
            return carry[0] + d, carry[1] + d * d

        sums = lax.fori_loop(0, steps, add, sums, unroll=True)
    shift = jnp.sum(sums[0], axis=0) * (1.0 / H)
    spread = jnp.sum(sums[1], axis=0) * (1.0 / H) - shift * shift
    stat[0] = pivot + shift
    stat[1] = lax.rsqrt(spread + 1e-05)


def normed_hidden(z, stat, gain, i):
    row = pl.ds(i, 1)
    return ((z[pl.ds(i, H, stride=R), :] - stat[0, row, :]) * stat[1, row, :] * gain).astype(BF16)


def dot(a, b, dims=((1,), (0,))):
    return lax.dot_general(a, b, (dims, ((), ())), preferred_element_type=F32)


def kernel(
    pair_hbm, ng_hbm, pw_hbm, gw_hbm, hg_hbm, ow_hbm, out_ref,
    ng_ref, pw_ref, gw_ref, hg_ref, ow_ref, x_buf, n_buf, wt, gt, ot, gains, z0, z1,
    send_a, recv_a, out_b, recv_b, gate0, mid,
    send_c, left_c, right_c, send_m, recv_m, out_d, recv_d, stat, gate1, resid, out_e, out_t, recv_e, recv_t,
    load_sem, ready, a_ssem, a_rsem, b_ssem, b_rsem, cl_ssem, cr_ssem, cl_rsem, cr_rsem,
    m_ssem, m_rsem, d_ssem, d_rsem, e_ssem, e_rsem, t_rsem,
):
    r = lax.axis_index("rows")
    c = lax.axis_index("chan")
    hid = c * ROWS + r
    mine = column_block(r, c)
    block = mine

    loads = [
        pltpu.make_async_copy(src, dst, load_sem.at[n])
        for n, (src, dst) in enumerate(
            [
                (pw_hbm, pw_ref),
                (ng_hbm, ng_ref),
                (pair_hbm.at[:, :, pl.ds(pl.multiple_of(mine * K, K), K)], x_buf),
                (gw_hbm, gw_ref),
                (ow_hbm, ow_ref),
                (hg_hbm, hg_ref),
            ]
        )
    ]
    for load in loads:
        load.start()

    barrier = pltpu.get_barrier_semaphore()

    def greet(n, carry):
        r2 = r + n
        r2 = jnp.where(r2 >= ROWS, r2 - ROWS, r2)
        pl.semaphore_signal(barrier, inc=1, device_id=(r2, c), device_id_type=MESH)
        pl.semaphore_signal(barrier, inc=1, device_id=(r2, opposite), device_id_type=MESH)
        return carry

    opposite = lax.rem(c + 2, CHAN)
    partner = 2 * (c // 2) + lax.rem(c + 1, 2)
    lax.fori_loop(0, ROWS, greet, 0, unroll=4)
    pl.semaphore_signal(barrier, inc=1, device_id=(r, partner), device_id_type=MESH)

    share = H // CHAN

    def turn(u):
        def one(m, carry):
            w = jnp.transpose(pw_ref[u, m].astype(F32)).astype(BF16)
            for q in range(CHAN):
                wt[u, q, pl.ds(pl.multiple_of(m * share, share), share), :] = w[
                    q * share : (q + 1) * share
                ]
            return carry

        lax.fori_loop(0, 4, one, 0)

    def column(row):
        return jnp.transpose(jnp.broadcast_to(row, (C, C)))

    loads[0].wait()
    turn(0)
    loads[1].wait()
    gains[0] = column(ng_ref[0:1, :])
    loads[2].wait()

    def norm_in(i, carry):
        n_buf[i] = norm_rows(x_buf[i].astype(F32), gains[0])
        return carry

    lax.fori_loop(0, R, norm_in, 0, unroll=8)

    def project(u, q, dst):
        def one(i, carry):
            y = dot(wt[u, q], n_buf[i])
            z0[pl.ds(i, share, stride=R), :] = sigmoid(y[share : 2 * share]) * y[:share]
            z1[pl.ds(i, share, stride=R), :] = (
                sigmoid(y[3 * share :]) * y[2 * share : 3 * share]
            )
            return carry

        lax.fori_loop(0, R, one, 0, unroll=8)

        def pack(h, carry):
            rows = pl.ds(pl.multiple_of(h * R, R), R)
            dst[q * share + h, 0] = z0[rows, :].astype(BF16)
            dst[q * share + h, 1] = z1[rows, :].astype(BF16)
            return carry

        lax.fori_loop(0, share, pack, 0, unroll=8)

    my_rows = pl.ds(pl.multiple_of(r * R, R), R)

    def chunk_a(s, carry):
        q = 2 * lax.rem(s + c // 2, 2) + lax.rem(c + s // 2, 2)
        project(0, q, send_a)

        @pl.when(s == 0)
        def _():
            pl.semaphore_wait(barrier, 2 * ROWS + 1)
            pl.semaphore_signal(ready, inc=1, device_id=(r, partner), device_id_type=MESH)

        @pl.when(s == 2)
        def _():
            pl.semaphore_wait(ready, 1)

        def send(t, carry):
            r2 = row_in_plane(r, row_plane(r, t // 8), lax.rem(t, 8))
            h2 = q * ROWS + r2
            src = send_a.at[h2]
            dst = recv_a.at[:, mine, my_rows]

            @pl.when(h2 == hid)
            def _():
                pltpu.make_async_copy(src, dst, a_rsem).start()

            @pl.when(h2 != hid)
            def _():
                pltpu.make_async_remote_copy(
                    src, dst, a_ssem, a_rsem, device_id=(r2, q), device_id_type=MESH
                ).start()

            return carry

        lax.fori_loop(0, ROWS, send, 0)
        return carry

    lax.fori_loop(0, CHAN, chunk_a, 0)

    for load in loads[3:]:
        load.wait()
    turn(1)
    for u in range(2):
        gt[u] = jnp.transpose(gw_ref[u].astype(F32)).astype(BF16)
        ot[u] = jnp.transpose(ow_ref[u].astype(F32)).astype(BF16)
        gains[2 + u] = column(hg_ref[u : u + 1, :])
    gains[1] = column(ng_ref[1:2, :])

    def gate_out(i, carry):
        gate0[i] = sigmoid(dot(gt[0], n_buf[i]))
        return carry

    lax.fori_loop(0, R, gate_out, 0, unroll=8)

    pltpu.make_async_copy(recv_a, recv_a, a_rsem).wait()

    per = K // R

    def send_b(r2, b2):
        c2 = column_chan(r2, b2)
        src = out_b.at[b2, pl.ds(pl.multiple_of(r2 * R, R), R)]
        dst = recv_b.at[hid]
        own = jnp.logical_and(r2 == r, c2 == c)

        @pl.when(own)
        def _():
            pltpu.make_async_copy(src, dst, b_rsem.at[r // 8]).start()

        @pl.when(jnp.logical_not(own))
        def _():
            pltpu.make_async_remote_copy(
                src, dst, b_ssem, b_rsem.at[r // 8], device_id=(r2, c2), device_id_type=MESH
            ).start()

    def chunk_b(s, carry):
        b = row_plane(r, s)
        rows = pl.ds(pl.multiple_of(b * K, K), K)
        left = jnp.concatenate([recv_a[0, n, rows, :] for n in range(TOK // K)], axis=1)
        right = jnp.concatenate([recv_a[1, n] for n in range(TOK // K)], axis=1)
        total = dot(left, right, ((1,), (1,))).astype(BF16)
        for n in range(TOK // K):
            out_b[n, rows, :] = total[:, n * K : (n + 1) * K]

        def send(t, carry):
            send_b(row_in_plane(r, b, t // 2), lax.rem(t + c, 2))
            return carry

        lax.fori_loop(0, per * 2, send, 0)
        return carry

    lax.fori_loop(0, TOK // K, chunk_b, 0)

    def late_b(t, carry):
        send_b(row_in_plane(r, row_plane(r, t // 16), lax.rem(t, 16) // 2), 2 + lax.rem(t + c, 2))
        return carry

    lax.fori_loop(0, ROWS * 2, late_b, 0)

    take_hidden(recv_b, b_rsem, z0, stat, r)

    def update_out(i, carry):
        h = normed_hidden(z0, stat, gains[2], i)
        m = (x_buf[i].astype(F32) + gate0[i] * dot(ot[0], h)).astype(BF16)
        mid[i] = m
        n_buf[i] = norm_rows(m.astype(F32), gains[1])
        return carry

    lax.fori_loop(0, R, update_out, 0, unroll=8)

    def chunk_c(s, carry):
        q = lax.rem(s + r, CHAN)
        project(1, q, send_c)

        def send(t, carry):
            r2 = row_in_plane(r, row_plane(r, t // 8), lax.rem(t, 8))
            h2 = q * ROWS + r2
            right_src, right_dst = send_c.at[h2, 1], right_c.at[mine, my_rows]

            @pl.when(h2 == hid)
            def _():
                pltpu.make_async_copy(right_src, right_dst, cr_rsem).start()

            @pl.when(h2 != hid)
            def _():
                pltpu.make_async_remote_copy(
                    right_src, right_dst, cr_ssem, cr_rsem, device_id=(r2, q), device_id_type=MESH
                ).start()

            @pl.when(mine < BLOCKS)
            def _():
                left_src, left_dst = send_c.at[h2, 0], left_c.at[mine, my_rows]

                @pl.when(h2 == hid)
                def _():
                    pltpu.make_async_copy(left_src, left_dst, cl_rsem).start()

                @pl.when(h2 != hid)
                def _():
                    pltpu.make_async_remote_copy(
                        left_src, left_dst, cl_ssem, cl_rsem,
                        device_id=(r2, q), device_id_type=MESH,
                    ).start()

            return carry

        lax.fori_loop(0, ROWS, send, 0)
        return carry

    lax.fori_loop(0, CHAN, chunk_c, 0)

    sends_m = r * R < WIN
    row_block = r // per
    m_rows = pl.ds(pl.multiple_of(lax.rem(r, per) * R, R), R)

    def m_copy(n):
        g = lax.rem(n + r, per)
        r2 = mine * per + g
        m_chan = column_chan(r2, row_block)
        src = send_m.at[pl.ds(pl.multiple_of(g * R, R), R)]
        dst = recv_m.at[:, m_rows, :]
        own = jnp.logical_and(r2 == r, m_chan == c)
        local = lambda: pltpu.make_async_copy(src, dst, m_rsem)
        remote = lambda: pltpu.make_async_remote_copy(
            src, dst, m_ssem.at[g], m_rsem, device_id=(r2, m_chan), device_id_type=MESH
        )
        return own, local, remote

    @pl.when(sends_m)
    def _():
        def turn_mid(i, carry):
            z0[pl.ds(i, K, stride=R), :] = jnp.transpose(mid[i].astype(F32))
            return carry

        lax.fori_loop(0, R, turn_mid, 0, unroll=8)

        def pack(j, carry):
            send_m[j] = z0[pl.ds(pl.multiple_of(j * R, R), R), :].astype(BF16)
            return carry

        lax.fori_loop(0, K, pack, 0, unroll=8)

        def send(g, carry):
            own, local, remote = m_copy(g)

            @pl.when(own)
            def _():
                local().start()

            @pl.when(jnp.logical_not(own))
            def _():
                remote().start()

            return carry

        lax.fori_loop(0, per, send, 0)

    pltpu.make_async_copy(left_c, left_c, cl_rsem).wait()
    pltpu.make_async_copy(right_c, right_c, cr_rsem).wait()

    tail = WIN - (BLOCKS - 1) * K
    group = K // tail

    def chunk_d(s, carry):
        b = row_plane(r, s)
        cols = pl.ds(pl.multiple_of(b * K, K), K)
        left = jnp.concatenate([left_c[n] for n in range(BLOCKS)], axis=1)
        total = dot(right_c[b], left, ((0,), (0,))).astype(BF16)
        for n in range(BLOCKS):
            out_d[n, cols, :] = total[:, n * K : (n + 1) * K]

        def send(t, carry):
            r2 = row_in_plane(r, b, t // BLOCKS)
            b2 = lax.rem(t + c, BLOCKS)
            c2 = column_chan(r2, b2)
            src = out_d.at[b2, pl.ds(pl.multiple_of(r2 * R, R), R)]
            dst = recv_d.at[hid]
            own = jnp.logical_and(r2 == r, c2 == c)

            @pl.when(own)
            def _():
                pltpu.make_async_copy(src, dst, d_rsem.at[r // 8]).start()

            @pl.when(jnp.logical_not(own))
            def _():
                pltpu.make_async_remote_copy(
                    src, dst, d_ssem, d_rsem.at[r // 8], device_id=(r2, c2), device_id_type=MESH
                ).start()

            return carry

        lax.fori_loop(0, per * BLOCKS, send, 0)
        return carry

    lax.fori_loop(0, TOK // K, chunk_d, 0)

    @pl.when(block < BLOCKS)
    def _():
        @pl.when(block < BLOCKS - 1)
        def _():
            pltpu.make_async_copy(recv_m, recv_m, m_rsem).wait()

        @pl.when(block == BLOCKS - 1)
        def _():
            part = recv_m.at[:, pl.ds(0, tail), :]
            pltpu.make_async_copy(part, part, m_rsem).wait()

        def gate_in(j, carry):
            m = jnp.transpose(recv_m[j].astype(F32))
            resid[j] = m.astype(BF16)
            gate1[j] = sigmoid(dot(gt[1], norm_rows(m, gains[1])))
            return carry

        lax.fori_loop(0, R, gate_in, 0, unroll=8)

        take_hidden(recv_d, d_rsem, z1, stat, r)

        def update_in(j):
            h = normed_hidden(z1, stat, gains[3], j)
            return (resid[j].astype(F32) + gate1[j] * dot(ot[1], h)).astype(BF16)

        def send(src, dst, sem):
            for s in range(1, CHAN):
                c2 = lax.rem(c + s, CHAN)
                rows = pl.ds(pl.multiple_of(c2 * share, share), share)
                pltpu.make_async_remote_copy(
                    src.at[..., rows, :], dst, e_ssem, sem, device_id=(r, c2), device_id_type=MESH
                ).start()
            rows = pl.ds(pl.multiple_of(c * share, share), share)
            pltpu.make_async_copy(src.at[..., rows, :], dst, sem).start()

        @pl.when(block < BLOCKS - 1)
        def _():
            def whole(g, carry):
                first = pl.multiple_of(g * group, group)
                for t in range(group):
                    out_e[first + t] = update_in(first + t)
                some = pl.ds(first, group)
                send(out_e.at[some], recv_e.at[block, some], e_rsem)
                return carry

            lax.fori_loop(0, R // group, whole, 0)

        @pl.when(block == BLOCKS - 1)
        def _():
            def packed(g, carry):
                first = pl.multiple_of(g * group, group)
                parts = [update_in(first + t)[:, :tail] for t in range(group)]
                out_t[g] = jnp.concatenate(parts, axis=1)
                send(out_t.at[g], recv_t.at[g], t_rsem)
                return carry

            lax.fori_loop(0, R // group, packed, 0)

    pltpu.make_async_copy(recv_t, recv_t, t_rsem).wait()
    for g in range(R // group):
        for t in range(group):
            out_ref[g * group + t, :, WIN - tail :] = recv_t[g, :, t * tail : (t + 1) * tail]
    pltpu.make_async_copy(recv_e, recv_e, e_rsem).wait()
    for b in range(BLOCKS - 1):
        out_ref[:, :, b * K : (b + 1) * K] = recv_e[b]

    def drain(ref, sem):
        pltpu.make_async_copy(ref, ref, sem).wait()

    drain(send_a.at[pl.ds(0, DEV - 1)], a_ssem)
    drain(recv_b.at[pl.ds(0, DEV - 1)], b_ssem)
    drain(recv_b.at[pl.ds(0, DEV - 1)], cr_ssem)

    @pl.when(mine < BLOCKS)
    def _():
        drain(recv_b.at[pl.ds(0, DEV - 1)], cl_ssem)

    @pl.when(block < BLOCKS)
    def _():
        drain(recv_b.at[pl.ds(0, ROWS * BLOCKS - 1)], d_ssem)

    @pl.when(block == BLOCKS)
    def _():
        drain(recv_b.at[pl.ds(0, ROWS * BLOCKS)], d_ssem)

    tiles = R * share // R

    @pl.when(block < BLOCKS - 1)
    def _():
        drain(recv_b.at[pl.ds(0, (CHAN - 1) * tiles)], e_ssem)

    @pl.when(block == BLOCKS - 1)
    def _():
        drain(recv_b.at[pl.ds(0, (CHAN - 1) * tiles // group)], e_ssem)

    @pl.when(sends_m)
    def _():
        def done(g, carry):
            own, _local, remote = m_copy(g)

            @pl.when(jnp.logical_not(own))
            def _():
                remote().wait_send()

            return carry

        lax.fori_loop(0, per, done, 0)


def shards(pair, norm_gain, proj_weight, gate_weight, hidden_gain, out_weight):
    vmem = pl.BlockSpec(memory_space=pltpu.VMEM)
    sem = pltpu.SemaphoreType.DMA
    tiles = lambda n: pltpu.VMEM((n, R, K), BF16)
    return pl.pallas_call(
        kernel,
        out_shape=jax.ShapeDtypeStruct((R, C // CHAN, WIN), BF16),
        in_specs=[pl.BlockSpec(memory_space=pltpu.HBM)] * 6,
        out_specs=vmem,
        scratch_shapes=[
            pltpu.VMEM((2, C), F32),
            pltpu.VMEM((2, 4, C, H), BF16),
            pltpu.VMEM((2, C, C), BF16),
            pltpu.VMEM((2, H), F32),
            pltpu.VMEM((2, H, C), BF16),
            pltpu.VMEM((R, C, K), BF16),
            pltpu.VMEM((R, C, K), BF16),
            pltpu.VMEM((2, CHAN, 4 * H // CHAN, C), BF16),
            pltpu.VMEM((2, C, C), BF16),
            pltpu.VMEM((2, C, H), BF16),
            pltpu.VMEM((4, C, K), F32),
            pltpu.VMEM((H * R, K), F32),
            pltpu.VMEM((H * R, K), F32),
            pltpu.VMEM((H, 2, R, K), BF16),
            pltpu.VMEM((2, CHAN, TOK, K), BF16),
            pltpu.VMEM((CHAN, TOK, K), BF16),
            tiles(H),
            pltpu.VMEM((R, C, K), F32),
            pltpu.VMEM((R, C, K), BF16),
            pltpu.VMEM((H, 2, R, K), BF16),
            pltpu.VMEM((BLOCKS, TOK, K), BF16),
            pltpu.VMEM((CHAN, TOK, K), BF16),
            pltpu.VMEM((K, R, C), BF16),
            pltpu.VMEM((R, K, C), BF16),
            pltpu.VMEM((BLOCKS, TOK, K), BF16),
            tiles(H),
            pltpu.VMEM((2, R, K), F32),
            pltpu.VMEM((R, C, K), F32),
            pltpu.VMEM((R, C, K), BF16),
            pltpu.VMEM((R, C, K), BF16),
            pltpu.VMEM((R // 4, C, K), BF16),
            pltpu.VMEM((BLOCKS - 1, R, C // CHAN, K), BF16),
            pltpu.VMEM((R // 4, C // CHAN, K), BF16),
            sem((6,)), pltpu.SemaphoreType.REGULAR, sem, sem, sem, sem((4,)), sem, sem, sem, sem,
            sem((K // R,)), sem, sem, sem((4,)), sem, sem, sem,
        ],
        compiler_params=pltpu.CompilerParams(
            collective_id=0, has_side_effects=True, vmem_limit_bytes=VMEM_BYTES
        ),
    )(pair, norm_gain, proj_weight, gate_weight, hidden_gain, out_weight)


def solution(mesh):
    in_specs = (P("rows", None, None), P(), P(), P(), P(), P())
    out_specs = P("rows", "chan", None)
    return jax.shard_map(shards, mesh=mesh, in_specs=in_specs, out_specs=out_specs, check_vma=False)
```

```python
import functools

import jax
import jax.numpy as jnp
from jax import lax
from jax.experimental import pallas as pl
from jax.experimental.pallas import tpu as pltpu
from jax.sharding import PartitionSpec as P

MESH = pl.DeviceIdType.MESH
F32 = jnp.float32
BF16 = jnp.bfloat16
C = 128
H = 128
TOK = 512
WIN = 288
ROWS = 32
CHAN = 4
DEV = ROWS * CHAN
R = TOK // ROWS
K = TOK // CHAN
BLOCKS = 3
SPREAD = 37
VMEM_BYTES = 63 * 1024 * 1024


def swap(n):
    return 2 * lax.rem(n, 2) + n // 2


def turned(r):
    return lax.rem(r // 2 + r // 8, 2)


def column_block(r, c):
    return swap(lax.rem(c + 2 * turned(r), CHAN))


def column_chan(r, b):
    return lax.rem(swap(b) + 2 * turned(r), CHAN)


def far_first(n):
    return jnp.where(n == 0, 2, jnp.where(n == 3, 0, 2 * n - 1))


def row_plane(r, s):
    return lax.rem(r // 8 + far_first(s), 4)


def row_in_plane(r, plane, t):
    x = lax.rem(r // 2 + far_first(t // 2), 4)
    return plane * 8 + x * 2 + lax.rem(r + 1 + t, 2)


def sigmoid(v):
    return 0.5 * jnp.tanh(0.5 * v) + 0.5


def norm_rows(x, gain):
    average = jnp.mean(x, axis=0, keepdims=True)
    centred = x - average
    spread = jnp.mean(centred * centred, axis=0, keepdims=True)
    return (centred * lax.rsqrt(spread + 1e-05) * gain).astype(BF16)


def take_hidden(src, sem, z, stat, r):
    planes, lanes = 4, 4
    near = H // CHAN // planes
    steps = CHAN * near // lanes

    def plane_of(s):
        return lax.rem(r // 8 + planes - far_first(s), planes)

    def some(plane, n):
        first = n * lanes // near * (H // CHAN) + plane * near + lax.rem(n * lanes, near)
        return pl.multiple_of(first, lanes)

    def load(first):
        return src[pl.ds(first, lanes)].astype(F32)

    zero = jnp.zeros((lanes, R, K), F32)
    pivot = None
    sums = (zero, zero)
    for s in range(planes):
        plane = plane_of(s)
        landed = src.at[pl.ds(0, CHAN * near)]
        pltpu.make_async_copy(landed, landed, sem.at[plane]).wait()
        if s == 0:
            total = lax.fori_loop(
                0, steps, lambda n, t: t + load(some(plane, n)), zero, unroll=True
            )
            pivot = jnp.sum(total, axis=0) * (1.0 / (CHAN * near))

        def add(n, carry):
            first = some(plane, n)
            x = load(first)
            rows = pl.ds(pl.multiple_of(first * R, lanes * R), lanes * R)
            z[rows, :] = x.reshape(lanes * R, K)
            d = x - pivot
            return carry[0] + d, carry[1] + d * d

        sums = lax.fori_loop(0, steps, add, sums, unroll=True)
    shift = jnp.sum(sums[0], axis=0) * (1.0 / H)
    spread = jnp.sum(sums[1], axis=0) * (1.0 / H) - shift * shift
    stat[0] = pivot + shift
    stat[1] = lax.rsqrt(spread + 1e-05)


def normed_hidden(z, stat, gain, i):
    row = pl.ds(i, 1)
    return ((z[pl.ds(i, H, stride=R), :] - stat[0, row, :]) * stat[1, row, :] * gain).astype(BF16)


def dot(a, b, dims=((1,), (0,))):
    return lax.dot_general(a, b, (dims, ((), ())), preferred_element_type=F32)


def kernel(
    pair_hbm, ng_hbm, pw_hbm, gw_hbm, hg_hbm, ow_hbm, out_ref,
    ng_ref, pw_ref, gw_ref, hg_ref, ow_ref, x_buf, n_buf, wt, gt, ot, gains, z0, z1,
    send_a, recv_a, out_b, recv_b, gate0, mid,
    send_c, left_c, right_c, send_m, recv_m, out_d, recv_d, stat, gate1, resid, out_e, out_t, recv_e, recv_t,
    load_sem, ready, a_ssem, a_rsem, b_ssem, b_rsem, cl_ssem, cr_ssem, cl_rsem, cr_rsem,
    m_ssem, m_rsem, d_ssem, d_rsem, e_ssem, e_rsem, t_rsem,
):
    r = lax.axis_index("rows")
    c = lax.axis_index("chan")
    hid = c * ROWS + r
    mine = column_block(r, c)
    block = mine

    loads = [
        pltpu.make_async_copy(src, dst, load_sem.at[n])
        for n, (src, dst) in enumerate(
            [
                (pw_hbm, pw_ref),
                (ng_hbm, ng_ref),
                (pair_hbm.at[:, :, pl.ds(pl.multiple_of(mine * K, K), K)], x_buf),
                (gw_hbm, gw_ref),
                (ow_hbm, ow_ref),
                (hg_hbm, hg_ref),
            ]
        )
    ]
    for load in loads:
        load.start()

    barrier = pltpu.get_barrier_semaphore()

    def greet(n, carry):
        r2 = r + n
        r2 = jnp.where(r2 >= ROWS, r2 - ROWS, r2)
        pl.semaphore_signal(barrier, inc=1, device_id=(r2, c), device_id_type=MESH)
        pl.semaphore_signal(barrier, inc=1, device_id=(r2, opposite), device_id_type=MESH)
        return carry

    opposite = lax.rem(c + 2, CHAN)
    partner = 2 * (c // 2) + lax.rem(c + 1, 2)
    lax.fori_loop(0, ROWS, greet, 0, unroll=4)
    pl.semaphore_signal(barrier, inc=1, device_id=(r, partner), device_id_type=MESH)

    share = H // CHAN

    def turn(u):
        def one(m, carry):
            w = jnp.transpose(pw_ref[u, m].astype(F32)).astype(BF16)
            for q in range(CHAN):
                wt[u, q, pl.ds(pl.multiple_of(m * share, share), share), :] = w[
                    q * share : (q + 1) * share
                ]
            return carry

        lax.fori_loop(0, 4, one, 0)

    def column(row):
        return jnp.transpose(jnp.broadcast_to(row, (C, C)))

    loads[0].wait()
    turn(0)
    loads[1].wait()
    gains[0] = column(ng_ref[0:1, :])
    loads[2].wait()

    def norm_in(i, carry):
        n_buf[i] = norm_rows(x_buf[i].astype(F32), gains[0])
        return carry

    lax.fori_loop(0, R, norm_in, 0, unroll=8)

    def project(u, q, dst):
        def one(i, carry):
            y = dot(wt[u, q], n_buf[i])
            z0[pl.ds(i, share, stride=R), :] = sigmoid(y[share : 2 * share]) * y[:share]
            z1[pl.ds(i, share, stride=R), :] = (
                sigmoid(y[3 * share :]) * y[2 * share : 3 * share]
            )
            return carry

        lax.fori_loop(0, R, one, 0, unroll=8)

        def pack(h, carry):
            rows = pl.ds(pl.multiple_of(h * R, R), R)
            dst[q * share + h, 0] = z0[rows, :].astype(BF16)
            dst[q * share + h, 1] = z1[rows, :].astype(BF16)
            return carry

        lax.fori_loop(0, share, pack, 0, unroll=8)

    my_rows = pl.ds(pl.multiple_of(r * R, R), R)

    def chunk_a(s, carry):
        q = 2 * lax.rem(s + c // 2, 2) + lax.rem(c + s // 2, 2)
        project(0, q, send_a)

        @pl.when(s == 0)
        def _():
            pl.semaphore_wait(barrier, 2 * ROWS + 1)
            pl.semaphore_signal(ready, inc=1, device_id=(r, partner), device_id_type=MESH)

        @pl.when(s == 2)
        def _():
            pl.semaphore_wait(ready, 1)

        def send(t, carry):
            r2 = row_in_plane(r, row_plane(r, t // 8), lax.rem(t, 8))
            h2 = q * ROWS + r2
            src = send_a.at[h2]
            dst = recv_a.at[:, mine, my_rows]

            @pl.when(h2 == hid)
            def _():
                pltpu.make_async_copy(src, dst, a_rsem).start()

            @pl.when(h2 != hid)
            def _():
                pltpu.make_async_remote_copy(
                    src, dst, a_ssem, a_rsem, device_id=(r2, q), device_id_type=MESH
                ).start()

            return carry

        lax.fori_loop(0, ROWS, send, 0)
        return carry

    lax.fori_loop(0, CHAN, chunk_a, 0)

    for load in loads[3:]:
        load.wait()
    turn(1)
    for u in range(2):
        gt[u] = jnp.transpose(gw_ref[u].astype(F32)).astype(BF16)
        ot[u] = jnp.transpose(ow_ref[u].astype(F32)).astype(BF16)
        gains[2 + u] = column(hg_ref[u : u + 1, :])
    gains[1] = column(ng_ref[1:2, :])

    def gate_out(i, carry):
        gate0[i] = sigmoid(dot(gt[0], n_buf[i]))
        return carry

    lax.fori_loop(0, R, gate_out, 0, unroll=8)

    pltpu.make_async_copy(recv_a, recv_a, a_rsem).wait()

    per = K // R

    def send_b(r2, b2):
        c2 = column_chan(r2, b2)
        src = out_b.at[b2, pl.ds(pl.multiple_of(r2 * R, R), R)]
        dst = recv_b.at[hid]
        own = jnp.logical_and(r2 == r, c2 == c)

        @pl.when(own)
        def _():
            pltpu.make_async_copy(src, dst, b_rsem.at[r // 8]).start()

        @pl.when(jnp.logical_not(own))
        def _():
            pltpu.make_async_remote_copy(
                src, dst, b_ssem, b_rsem.at[r // 8], device_id=(r2, c2), device_id_type=MESH
            ).start()

    def chunk_b(s, carry):
        b = row_plane(r, s)
        rows = pl.ds(pl.multiple_of(b * K, K), K)
        left = jnp.concatenate([recv_a[0, n, rows, :] for n in range(TOK // K)], axis=1)
        right = jnp.concatenate([recv_a[1, n] for n in range(TOK // K)], axis=1)
        total = dot(left, right, ((1,), (1,))).astype(BF16)
        for n in range(TOK // K):
            out_b[n, rows, :] = total[:, n * K : (n + 1) * K]

        def send(t, carry):
            send_b(row_in_plane(r, b, t // 2), lax.rem(t + c, 2))
            return carry

        lax.fori_loop(0, per * 2, send, 0)
        return carry

    lax.fori_loop(0, TOK // K, chunk_b, 0)

    def late_b(t, carry):
        send_b(row_in_plane(r, row_plane(r, t // 16), lax.rem(t, 16) // 2), 2 + lax.rem(t + c, 2))
        return carry

    lax.fori_loop(0, ROWS * 2, late_b, 0)

    take_hidden(recv_b, b_rsem, z0, stat, r)

    def update_out(i, carry):
        h = normed_hidden(z0, stat, gains[2], i)
        m = (x_buf[i].astype(F32) + gate0[i] * dot(ot[0], h)).astype(BF16)
        mid[i] = m
        n_buf[i] = norm_rows(m.astype(F32), gains[1])
        return carry

    lax.fori_loop(0, R, update_out, 0, unroll=8)

    def chunk_c(s, carry):
        q = lax.rem(s + c, CHAN)
        project(1, q, send_c)

        def send(t, carry):
            r2 = row_in_plane(r, row_plane(r, t // 8), lax.rem(t, 8))
            h2 = q * ROWS + r2
            right_src, right_dst = send_c.at[h2, 1], right_c.at[mine, my_rows]

            @pl.when(h2 == hid)
            def _():
                pltpu.make_async_copy(right_src, right_dst, cr_rsem).start()

            @pl.when(h2 != hid)
            def _():
                pltpu.make_async_remote_copy(
                    right_src, right_dst, cr_ssem, cr_rsem, device_id=(r2, q), device_id_type=MESH
                ).start()

            @pl.when(mine < BLOCKS)
            def _():
                left_src, left_dst = send_c.at[h2, 0], left_c.at[mine, my_rows]

                @pl.when(h2 == hid)
                def _():
                    pltpu.make_async_copy(left_src, left_dst, cl_rsem).start()

                @pl.when(h2 != hid)
                def _():
                    pltpu.make_async_remote_copy(
                        left_src, left_dst, cl_ssem, cl_rsem,
                        device_id=(r2, q), device_id_type=MESH,
                    ).start()

            return carry

        lax.fori_loop(0, ROWS, send, 0)
        return carry

    lax.fori_loop(0, CHAN, chunk_c, 0)

    sends_m = r * R < WIN
    row_block = r // per
    m_rows = pl.ds(pl.multiple_of(lax.rem(r, per) * R, R), R)

    def m_copy(n):
        g = lax.rem(n + r, per)
        r2 = mine * per + g
        m_chan = column_chan(r2, row_block)
        src = send_m.at[pl.ds(pl.multiple_of(g * R, R), R)]
        dst = recv_m.at[:, m_rows, :]
        own = jnp.logical_and(r2 == r, m_chan == c)
        local = lambda: pltpu.make_async_copy(src, dst, m_rsem)
        remote = lambda: pltpu.make_async_remote_copy(
            src, dst, m_ssem.at[g], m_rsem, device_id=(r2, m_chan), device_id_type=MESH
        )
        return own, local, remote

    @pl.when(sends_m)
    def _():
        def turn_mid(i, carry):
            z0[pl.ds(i, K, stride=R), :] = jnp.transpose(mid[i].astype(F32))
            return carry

        lax.fori_loop(0, R, turn_mid, 0, unroll=8)

        def pack(j, carry):
            send_m[j] = z0[pl.ds(pl.multiple_of(j * R, R), R), :].astype(BF16)
            return carry

        lax.fori_loop(0, K, pack, 0, unroll=8)

        def send(g, carry):
            own, local, remote = m_copy(g)

            @pl.when(own)
            def _():
                local().start()

            @pl.when(jnp.logical_not(own))
            def _():
                remote().start()

            return carry

        lax.fori_loop(0, per, send, 0)

    pltpu.make_async_copy(left_c, left_c, cl_rsem).wait()
    pltpu.make_async_copy(right_c, right_c, cr_rsem).wait()

    tail = WIN - (BLOCKS - 1) * K
    group = K // tail

    def send_d(r2, b2):
        c2 = column_chan(r2, b2)
        src = out_d.at[b2, pl.ds(pl.multiple_of(r2 * R, R), R)]
        dst = recv_d.at[hid]
        own = jnp.logical_and(r2 == r, c2 == c)

        @pl.when(own)
        def _():
            pltpu.make_async_copy(src, dst, d_rsem.at[r // 8]).start()

        @pl.when(jnp.logical_not(own))
        def _():
            pltpu.make_async_remote_copy(
                src, dst, d_ssem, d_rsem.at[r // 8], device_id=(r2, c2), device_id_type=MESH
            ).start()

    def chunk_d(s, carry):
        b = row_plane(r, s)
        cols = pl.ds(pl.multiple_of(b * K, K), K)
        left = jnp.concatenate([left_c[n] for n in range(BLOCKS)], axis=1)
        total = dot(right_c[b], left, ((0,), (0,))).astype(BF16)
        for n in range(BLOCKS):
            out_d[n, cols, :] = total[:, n * K : (n + 1) * K]

        def send(t, carry):
            send_d(row_in_plane(r, b, t // 2), lax.rem(t + c, 2))
            return carry

        lax.fori_loop(0, per * 2, send, 0)
        return carry

    lax.fori_loop(0, TOK // K, chunk_d, 0)

    def late_d(t, carry):
        send_d(row_in_plane(r, row_plane(r, t // 8), lax.rem(t, 8)), BLOCKS - 1)
        return carry

    lax.fori_loop(0, ROWS, late_d, 0)

    @pl.when(block < BLOCKS)
    def _():
        @pl.when(block < BLOCKS - 1)
        def _():
            pltpu.make_async_copy(recv_m, recv_m, m_rsem).wait()

        @pl.when(block == BLOCKS - 1)
        def _():
            part = recv_m.at[:, pl.ds(0, tail), :]
            pltpu.make_async_copy(part, part, m_rsem).wait()

        def gate_in(j, carry):
            m = jnp.transpose(recv_m[j].astype(F32))
            resid[j] = m.astype(BF16)
            gate1[j] = sigmoid(dot(gt[1], norm_rows(m, gains[1])))
            return carry

        lax.fori_loop(0, R, gate_in, 0, unroll=8)

        take_hidden(recv_d, d_rsem, z1, stat, r)

        def update_in(j):
            h = normed_hidden(z1, stat, gains[3], j)
            return (resid[j].astype(F32) + gate1[j] * dot(ot[1], h)).astype(BF16)

        def send(src, dst, sem):
            for s in range(1, CHAN):
                c2 = lax.rem(c + s, CHAN)
                rows = pl.ds(pl.multiple_of(c2 * share, share), share)
                pltpu.make_async_remote_copy(
                    src.at[..., rows, :], dst, e_ssem, sem, device_id=(r, c2), device_id_type=MESH
                ).start()
            rows = pl.ds(pl.multiple_of(c * share, share), share)
            pltpu.make_async_copy(src.at[..., rows, :], dst, sem).start()

        @pl.when(block < BLOCKS - 1)
        def _():
            def whole(g, carry):
                first = pl.multiple_of(g * group, group)
                for t in range(group):
                    out_e[first + t] = update_in(first + t)
                some = pl.ds(first, group)
                send(out_e.at[some], recv_e.at[block, some], e_rsem)
                return carry

            lax.fori_loop(0, R // group, whole, 0)

        @pl.when(block == BLOCKS - 1)
        def _():
            def packed(g, carry):
                first = pl.multiple_of(g * group, group)
                parts = [update_in(first + t)[:, :tail] for t in range(group)]
                out_t[g] = jnp.concatenate(parts, axis=1)
                send(out_t.at[g], recv_t.at[g], t_rsem)
                return carry

            lax.fori_loop(0, R // group, packed, 0)

    pltpu.make_async_copy(recv_e, recv_e, e_rsem).wait()
    for b in range(BLOCKS - 1):
        out_ref[:, :, b * K : (b + 1) * K] = recv_e[b]

    pltpu.make_async_copy(recv_t, recv_t, t_rsem).wait()
    for g in range(R // group):
        for t in range(group):
            out_ref[g * group + t, :, WIN - tail :] = recv_t[g, :, t * tail : (t + 1) * tail]

    def drain(ref, sem):
        pltpu.make_async_copy(ref, ref, sem).wait()

    drain(send_a.at[pl.ds(0, DEV - 1)], a_ssem)
    drain(recv_b.at[pl.ds(0, DEV - 1)], b_ssem)
    drain(recv_b.at[pl.ds(0, DEV - 1)], cr_ssem)

    @pl.when(mine < BLOCKS)
    def _():
        drain(recv_b.at[pl.ds(0, DEV - 1)], cl_ssem)

    @pl.when(block < BLOCKS)
    def _():
        drain(recv_b.at[pl.ds(0, ROWS * BLOCKS - 1)], d_ssem)

    @pl.when(block == BLOCKS)
    def _():
        drain(recv_b.at[pl.ds(0, ROWS * BLOCKS)], d_ssem)

    tiles = R * share // R

    @pl.when(block < BLOCKS - 1)
    def _():
        drain(recv_b.at[pl.ds(0, (CHAN - 1) * tiles)], e_ssem)

    @pl.when(block == BLOCKS - 1)
    def _():
        drain(recv_b.at[pl.ds(0, (CHAN - 1) * tiles // group)], e_ssem)

    @pl.when(sends_m)
    def _():
        def done(g, carry):
            own, _local, remote = m_copy(g)

            @pl.when(jnp.logical_not(own))
            def _():
                remote().wait_send()

            return carry

        lax.fori_loop(0, per, done, 0)


def shards(pair, norm_gain, proj_weight, gate_weight, hidden_gain, out_weight):
    vmem = pl.BlockSpec(memory_space=pltpu.VMEM)
    sem = pltpu.SemaphoreType.DMA
    tiles = lambda n: pltpu.VMEM((n, R, K), BF16)
    return pl.pallas_call(
        kernel,
        out_shape=jax.ShapeDtypeStruct((R, C // CHAN, WIN), BF16),
        in_specs=[pl.BlockSpec(memory_space=pltpu.HBM)] * 6,
        out_specs=vmem,
        scratch_shapes=[
            pltpu.VMEM((2, C), F32),
            pltpu.VMEM((2, 4, C, H), BF16),
            pltpu.VMEM((2, C, C), BF16),
            pltpu.VMEM((2, H), F32),
            pltpu.VMEM((2, H, C), BF16),
            pltpu.VMEM((R, C, K), BF16),
            pltpu.VMEM((R, C, K), BF16),
            pltpu.VMEM((2, CHAN, 4 * H // CHAN, C), BF16),
            pltpu.VMEM((2, C, C), BF16),
            pltpu.VMEM((2, C, H), BF16),
            pltpu.VMEM((4, C, K), F32),
            pltpu.VMEM((H * R, K), F32),
            pltpu.VMEM((H * R, K), F32),
            pltpu.VMEM((H, 2, R, K), BF16),
            pltpu.VMEM((2, CHAN, TOK, K), BF16),
            pltpu.VMEM((CHAN, TOK, K), BF16),
            tiles(H),
            pltpu.VMEM((R, C, K), F32),
            pltpu.VMEM((R, C, K), BF16),
            pltpu.VMEM((H, 2, R, K), BF16),
            pltpu.VMEM((BLOCKS, TOK, K), BF16),
            pltpu.VMEM((CHAN, TOK, K), BF16),
            pltpu.VMEM((K, R, C), BF16),
            pltpu.VMEM((R, K, C), BF16),
            pltpu.VMEM((BLOCKS, TOK, K), BF16),
            tiles(H),
            pltpu.VMEM((2, R, K), F32),
            pltpu.VMEM((R, C, K), F32),
            pltpu.VMEM((R, C, K), BF16),
            pltpu.VMEM((R, C, K), BF16),
            pltpu.VMEM((R // 4, C, K), BF16),
            pltpu.VMEM((BLOCKS - 1, R, C // CHAN, K), BF16),
            pltpu.VMEM((R // 4, C // CHAN, K), BF16),
            sem((6,)), pltpu.SemaphoreType.REGULAR, sem, sem, sem, sem((4,)), sem, sem, sem, sem,
            sem((K // R,)), sem, sem, sem((4,)), sem, sem, sem,
        ],
        compiler_params=pltpu.CompilerParams(
            collective_id=0, has_side_effects=True, vmem_limit_bytes=VMEM_BYTES
        ),
    )(pair, norm_gain, proj_weight, gate_weight, hidden_gain, out_weight)


def solution(mesh):
    in_specs = (P("rows", None, None), P(), P(), P(), P(), P())
    out_specs = P("rows", "chan", None)
    return jax.shard_map(shards, mesh=mesh, in_specs=in_specs, out_specs=out_specs, check_vma=False)
```

```python
import functools

import jax
import jax.numpy as jnp
from jax import lax
from jax.experimental import pallas as pl
from jax.experimental.pallas import tpu as pltpu
from jax.sharding import PartitionSpec as P

MESH = pl.DeviceIdType.MESH
F32 = jnp.float32
BF16 = jnp.bfloat16
C = 128
H = 128
TOK = 512
WIN = 288
ROWS = 32
CHAN = 4
DEV = ROWS * CHAN
R = TOK // ROWS
K = TOK // CHAN
BLOCKS = 3
SPREAD = 37
VMEM_BYTES = 63 * 1024 * 1024


def swap(n):
    return 2 * lax.rem(n, 2) + n // 2


def turned(r):
    return lax.rem(r // 2 + r // 8, 2)


def column_block(r, c):
    return swap(lax.rem(c + 2 * turned(r), CHAN))


def column_chan(r, b):
    return lax.rem(swap(b) + 2 * turned(r), CHAN)


def far_first(n):
    return jnp.where(n == 0, 2, jnp.where(n == 3, 0, 2 * n - 1))


def row_plane(r, s):
    return lax.rem(r // 8 + far_first(s), 4)


def row_in_plane(r, plane, t):
    x = lax.rem(r // 2 + far_first(t // 2), 4)
    return plane * 8 + x * 2 + lax.rem(r + 1 + t, 2)


def sigmoid(v):
    return 0.5 * jnp.tanh(0.5 * v) + 0.5


def norm_rows(x, gain):
    average = jnp.mean(x, axis=0, keepdims=True)
    centred = x - average
    spread = jnp.mean(centred * centred, axis=0, keepdims=True)
    return (centred * lax.rsqrt(spread + 1e-05) * gain).astype(BF16)


def take_hidden(src, sem, z, stat, r):
    planes, lanes = 4, 4
    near = H // CHAN // planes
    steps = CHAN * near // lanes

    def plane_of(s):
        return lax.rem(r // 8 + planes - far_first(s), planes)

    def some(plane, n):
        first = n * lanes // near * (H // CHAN) + plane * near + lax.rem(n * lanes, near)
        return pl.multiple_of(first, lanes)

    def load(first):
        return src[pl.ds(first, lanes)].astype(F32)

    zero = jnp.zeros((lanes, R, K), F32)
    pivot = None
    sums = (zero, zero)
    for s in range(planes):
        plane = plane_of(s)
        landed = src.at[pl.ds(0, CHAN * near)]
        pltpu.make_async_copy(landed, landed, sem.at[plane]).wait()
        if s == 0:
            total = lax.fori_loop(
                0, steps, lambda n, t: t + load(some(plane, n)), zero, unroll=True
            )
            pivot = jnp.sum(total, axis=0) * (1.0 / (CHAN * near))

        def add(n, carry):
            first = some(plane, n)
            x = load(first)
            rows = pl.ds(pl.multiple_of(first * R, lanes * R), lanes * R)
            z[rows, :] = x.reshape(lanes * R, K)
            d = x - pivot
            return carry[0] + d, carry[1] + d * d

        sums = lax.fori_loop(0, steps, add, sums, unroll=True)
    shift = jnp.sum(sums[0], axis=0) * (1.0 / H)
    spread = jnp.sum(sums[1], axis=0) * (1.0 / H) - shift * shift
    stat[0] = pivot + shift
    stat[1] = lax.rsqrt(spread + 1e-05)


def normed_hidden(z, stat, gain, i):
    row = pl.ds(i, 1)
    return ((z[pl.ds(i, H, stride=R), :] - stat[0, row, :]) * stat[1, row, :] * gain).astype(BF16)


def dot(a, b, dims=((1,), (0,))):
    return lax.dot_general(a, b, (dims, ((), ())), preferred_element_type=F32)


def kernel(
    pair_hbm, ng_hbm, pw_hbm, gw_hbm, hg_hbm, ow_hbm, out_ref,
    ng_ref, pw_ref, gw_ref, hg_ref, ow_ref, x_buf, n_buf, wt, gt, ot, gains, z0, z1,
    send_a, recv_a, out_b, recv_b, gate0, mid,
    send_c, left_c, right_c, send_m, recv_m, out_d, recv_d, stat, gate1, resid, out_e, out_t, recv_e, recv_t,
    load_sem, ready, a_ssem, a_rsem, b_ssem, b_rsem, cl_ssem, cr_ssem, cl_rsem, cr_rsem,
    m_ssem, m_rsem, d_ssem, d_rsem, e_ssem, e_rsem, t_rsem,
):
    r = lax.axis_index("rows")
    c = lax.axis_index("chan")
    hid = c * ROWS + r
    mine = column_block(r, c)
    block = mine

    loads = [
        pltpu.make_async_copy(src, dst, load_sem.at[n])
        for n, (src, dst) in enumerate(
            [
                (pw_hbm, pw_ref),
                (ng_hbm, ng_ref),
                (pair_hbm.at[:, :, pl.ds(pl.multiple_of(mine * K, K), K)], x_buf),
                (gw_hbm, gw_ref),
                (ow_hbm, ow_ref),
                (hg_hbm, hg_ref),
            ]
        )
    ]
    for load in loads:
        load.start()

    barrier = pltpu.get_barrier_semaphore()

    def greet(n, carry):
        r2 = r + n
        r2 = jnp.where(r2 >= ROWS, r2 - ROWS, r2)
        pl.semaphore_signal(barrier, inc=1, device_id=(r2, c), device_id_type=MESH)
        pl.semaphore_signal(barrier, inc=1, device_id=(r2, opposite), device_id_type=MESH)
        return carry

    opposite = lax.rem(c + 2, CHAN)
    partner = 2 * (c // 2) + lax.rem(c + 1, 2)
    lax.fori_loop(0, ROWS, greet, 0, unroll=4)
    pl.semaphore_signal(barrier, inc=1, device_id=(r, partner), device_id_type=MESH)

    share = H // CHAN

    def turn(u):
        def one(m, carry):
            w = jnp.transpose(pw_ref[u, m].astype(F32)).astype(BF16)
            for q in range(CHAN):
                wt[u, q, pl.ds(pl.multiple_of(m * share, share), share), :] = w[
                    q * share : (q + 1) * share
                ]
            return carry

        lax.fori_loop(0, 4, one, 0)

    def column(row):
        return jnp.transpose(jnp.broadcast_to(row, (C, C)))

    loads[0].wait()
    turn(0)
    loads[1].wait()
    gains[0] = column(ng_ref[0:1, :])
    loads[2].wait()

    def norm_in(i, carry):
        n_buf[i] = norm_rows(x_buf[i].astype(F32), gains[0])
        return carry

    lax.fori_loop(0, R, norm_in, 0, unroll=8)

    def project(u, q, dst):
        def one(i, carry):
            y = dot(wt[u, q], n_buf[i])
            z0[pl.ds(i, share, stride=R), :] = sigmoid(y[share : 2 * share]) * y[:share]
            z1[pl.ds(i, share, stride=R), :] = (
                sigmoid(y[3 * share :]) * y[2 * share : 3 * share]
            )
            return carry

        lax.fori_loop(0, R, one, 0, unroll=8)

        def pack(h, carry):
            rows = pl.ds(pl.multiple_of(h * R, R), R)
            dst[q * share + h, 0] = z0[rows, :].astype(BF16)
            dst[q * share + h, 1] = z1[rows, :].astype(BF16)
            return carry

        lax.fori_loop(0, share, pack, 0, unroll=8)

    my_rows = pl.ds(pl.multiple_of(r * R, R), R)

    def chunk_a(s, carry):
        q = 2 * lax.rem(s + c // 2 + 1, 2) + lax.rem(c + s // 2, 2)
        project(0, q, send_a)

        @pl.when(s == 0)
        def _():
            pl.semaphore_wait(barrier, 2 * ROWS + 1)
            pl.semaphore_signal(ready, inc=1, device_id=(r, partner), device_id_type=MESH)

        @pl.when(s == 2)
        def _():
            pl.semaphore_wait(ready, 1)

        def send(t, carry):
            r2 = row_in_plane(r, row_plane(r, t // 8), lax.rem(t, 8))
            h2 = q * ROWS + r2
            src = send_a.at[h2]
            dst = recv_a.at[:, mine, my_rows]

            @pl.when(h2 == hid)
            def _():
                pltpu.make_async_copy(src, dst, a_rsem).start()

            @pl.when(h2 != hid)
            def _():
                pltpu.make_async_remote_copy(
                    src, dst, a_ssem, a_rsem, device_id=(r2, q), device_id_type=MESH
                ).start()

            return carry

        lax.fori_loop(0, ROWS, send, 0)
        return carry

    lax.fori_loop(0, CHAN, chunk_a, 0)

    for load in loads[3:]:
        load.wait()
    turn(1)
    for u in range(2):
        gt[u] = jnp.transpose(gw_ref[u].astype(F32)).astype(BF16)
        ot[u] = jnp.transpose(ow_ref[u].astype(F32)).astype(BF16)
        gains[2 + u] = column(hg_ref[u : u + 1, :])
    gains[1] = column(ng_ref[1:2, :])

    def gate_out(i, carry):
        gate0[i] = sigmoid(dot(gt[0], n_buf[i]))
        return carry

    lax.fori_loop(0, R, gate_out, 0, unroll=8)

    pltpu.make_async_copy(recv_a, recv_a, a_rsem).wait()

    per = K // R

    def send_b(r2, b2):
        c2 = column_chan(r2, b2)
        src = out_b.at[b2, pl.ds(pl.multiple_of(r2 * R, R), R)]
        dst = recv_b.at[hid]
        own = jnp.logical_and(r2 == r, c2 == c)

        @pl.when(own)
        def _():
            pltpu.make_async_copy(src, dst, b_rsem.at[r // 8]).start()

        @pl.when(jnp.logical_not(own))
        def _():
            pltpu.make_async_remote_copy(
                src, dst, b_ssem, b_rsem.at[r // 8], device_id=(r2, c2), device_id_type=MESH
            ).start()

    def chunk_b(s, carry):
        b = row_plane(r, s)
        rows = pl.ds(pl.multiple_of(b * K, K), K)
        left = jnp.concatenate([recv_a[0, n, rows, :] for n in range(TOK // K)], axis=1)
        right = jnp.concatenate([recv_a[1, n] for n in range(TOK // K)], axis=1)
        total = dot(left, right, ((1,), (1,))).astype(BF16)
        for n in range(TOK // K):
            out_b[n, rows, :] = total[:, n * K : (n + 1) * K]

        def send(t, carry):
            send_b(row_in_plane(r, b, t // 2), lax.rem(t + c, 2))
            return carry

        lax.fori_loop(0, per * 2, send, 0)
        return carry

    lax.fori_loop(0, TOK // K, chunk_b, 0)

    def late_b(t, carry):
        send_b(row_in_plane(r, row_plane(r, t // 16), lax.rem(t, 16) // 2), 2 + lax.rem(t + c, 2))
        return carry

    lax.fori_loop(0, ROWS * 2, late_b, 0)

    take_hidden(recv_b, b_rsem, z0, stat, r)

    def update_out(i, carry):
        h = normed_hidden(z0, stat, gains[2], i)
        m = (x_buf[i].astype(F32) + gate0[i] * dot(ot[0], h)).astype(BF16)
        mid[i] = m
        n_buf[i] = norm_rows(m.astype(F32), gains[1])
        return carry

    lax.fori_loop(0, R, update_out, 0, unroll=8)

    def chunk_c(s, carry):
        q = lax.rem(s + c + 1, CHAN)
        project(1, q, send_c)

        def send(t, carry):
            r2 = row_in_plane(r, row_plane(r, t // 8), lax.rem(t, 8))
            h2 = q * ROWS + r2
            right_src, right_dst = send_c.at[h2, 1], right_c.at[mine, my_rows]

            @pl.when(h2 == hid)
            def _():
                pltpu.make_async_copy(right_src, right_dst, cr_rsem).start()

            @pl.when(h2 != hid)
            def _():
                pltpu.make_async_remote_copy(
                    right_src, right_dst, cr_ssem, cr_rsem, device_id=(r2, q), device_id_type=MESH
                ).start()

            @pl.when(mine < BLOCKS)
            def _():
                left_src, left_dst = send_c.at[h2, 0], left_c.at[mine, my_rows]

                @pl.when(h2 == hid)
                def _():
                    pltpu.make_async_copy(left_src, left_dst, cl_rsem).start()

                @pl.when(h2 != hid)
                def _():
                    pltpu.make_async_remote_copy(
                        left_src, left_dst, cl_ssem, cl_rsem,
                        device_id=(r2, q), device_id_type=MESH,
                    ).start()

            return carry

        lax.fori_loop(0, ROWS, send, 0)
        return carry

    lax.fori_loop(0, CHAN, chunk_c, 0)

    sends_m = r * R < WIN
    row_block = r // per
    m_rows = pl.ds(pl.multiple_of(lax.rem(r, per) * R, R), R)

    def m_copy(n):
        g = lax.rem(n + r, per)
        r2 = mine * per + g
        m_chan = column_chan(r2, row_block)
        src = send_m.at[pl.ds(pl.multiple_of(g * R, R), R)]
        dst = recv_m.at[:, m_rows, :]
        own = jnp.logical_and(r2 == r, m_chan == c)
        local = lambda: pltpu.make_async_copy(src, dst, m_rsem)
        remote = lambda: pltpu.make_async_remote_copy(
            src, dst, m_ssem.at[g], m_rsem, device_id=(r2, m_chan), device_id_type=MESH
        )
        return own, local, remote

    @pl.when(sends_m)
    def _():
        def turn_mid(i, carry):
            z0[pl.ds(i, K, stride=R), :] = jnp.transpose(mid[i].astype(F32))
            return carry

        lax.fori_loop(0, R, turn_mid, 0, unroll=8)

        def pack(j, carry):
            send_m[j] = z0[pl.ds(pl.multiple_of(j * R, R), R), :].astype(BF16)
            return carry

        lax.fori_loop(0, K, pack, 0, unroll=8)

        def send(g, carry):
            own, local, remote = m_copy(g)

            @pl.when(own)
            def _():
                local().start()

            @pl.when(jnp.logical_not(own))
            def _():
                remote().start()

            return carry

        lax.fori_loop(0, per, send, 0)

    pltpu.make_async_copy(left_c, left_c, cl_rsem).wait()
    pltpu.make_async_copy(right_c, right_c, cr_rsem).wait()

    tail = WIN - (BLOCKS - 1) * K
    group = K // tail

    def send_d(r2, b2):
        c2 = column_chan(r2, b2)
        src = out_d.at[b2, pl.ds(pl.multiple_of(r2 * R, R), R)]
        dst = recv_d.at[hid]
        own = jnp.logical_and(r2 == r, c2 == c)

        @pl.when(own)
        def _():
            pltpu.make_async_copy(src, dst, d_rsem.at[r // 8]).start()

        @pl.when(jnp.logical_not(own))
        def _():
            pltpu.make_async_remote_copy(
                src, dst, d_ssem, d_rsem.at[r // 8], device_id=(r2, c2), device_id_type=MESH
            ).start()

    def chunk_d(s, carry):
        b = row_plane(r, s)
        cols = pl.ds(pl.multiple_of(b * K, K), K)
        left = jnp.concatenate([left_c[n] for n in range(BLOCKS)], axis=1)
        total = dot(right_c[b], left, ((0,), (0,))).astype(BF16)
        for n in range(BLOCKS):
            out_d[n, cols, :] = total[:, n * K : (n + 1) * K]

        def send(t, carry):
            send_d(row_in_plane(r, b, t // 2), lax.rem(t + c, 2))
            return carry

        lax.fori_loop(0, per * 2, send, 0)
        return carry

    lax.fori_loop(0, TOK // K, chunk_d, 0)

    def late_d(t, carry):
        send_d(row_in_plane(r, row_plane(r, t // 8), lax.rem(t, 8)), BLOCKS - 1)
        return carry

    lax.fori_loop(0, ROWS, late_d, 0)

    @pl.when(block < BLOCKS)
    def _():
        @pl.when(block < BLOCKS - 1)
        def _():
            pltpu.make_async_copy(recv_m, recv_m, m_rsem).wait()

        @pl.when(block == BLOCKS - 1)
        def _():
            part = recv_m.at[:, pl.ds(0, tail), :]
            pltpu.make_async_copy(part, part, m_rsem).wait()

        def gate_in(j, carry):
            m = jnp.transpose(recv_m[j].astype(F32))
            resid[j] = m.astype(BF16)
            gate1[j] = sigmoid(dot(gt[1], norm_rows(m, gains[1])))
            return carry

        lax.fori_loop(0, R, gate_in, 0, unroll=8)

        take_hidden(recv_d, d_rsem, z1, stat, r)

        def update_in(j):
            h = normed_hidden(z1, stat, gains[3], j)
            return (resid[j].astype(F32) + gate1[j] * dot(ot[1], h)).astype(BF16)

        def send(src, dst, sem):
            for s in range(1, CHAN):
                c2 = lax.rem(c + s, CHAN)
                rows = pl.ds(pl.multiple_of(c2 * share, share), share)
                pltpu.make_async_remote_copy(
                    src.at[..., rows, :], dst, e_ssem, sem, device_id=(r, c2), device_id_type=MESH
                ).start()
            rows = pl.ds(pl.multiple_of(c * share, share), share)
            pltpu.make_async_copy(src.at[..., rows, :], dst, sem).start()

        @pl.when(block < BLOCKS - 1)
        def _():
            def whole(g, carry):
                first = pl.multiple_of(g * group, group)
                for t in range(group):
                    out_e[first + t] = update_in(first + t)
                some = pl.ds(first, group)
                send(out_e.at[some], recv_e.at[block, some], e_rsem)
                return carry

            lax.fori_loop(0, R // group, whole, 0)

        @pl.when(block == BLOCKS - 1)
        def _():
            def packed(g, carry):
                first = pl.multiple_of(g * group, group)
                parts = [update_in(first + t)[:, :tail] for t in range(group)]
                out_t[g] = jnp.concatenate(parts, axis=1)
                send(out_t.at[g], recv_t.at[g], t_rsem)
                return carry

            lax.fori_loop(0, R // group, packed, 0)

    pltpu.make_async_copy(recv_e, recv_e, e_rsem).wait()
    for b in range(BLOCKS - 1):
        out_ref[:, :, b * K : (b + 1) * K] = recv_e[b]

    pltpu.make_async_copy(recv_t, recv_t, t_rsem).wait()
    for g in range(R // group):
        for t in range(group):
            out_ref[g * group + t, :, WIN - tail :] = recv_t[g, :, t * tail : (t + 1) * tail]

    def drain(ref, sem):
        pltpu.make_async_copy(ref, ref, sem).wait()

    drain(send_a.at[pl.ds(0, DEV - 1)], a_ssem)
    drain(recv_b.at[pl.ds(0, DEV - 1)], b_ssem)
    drain(recv_b.at[pl.ds(0, DEV - 1)], cr_ssem)

    @pl.when(mine < BLOCKS)
    def _():
        drain(recv_b.at[pl.ds(0, DEV - 1)], cl_ssem)

    @pl.when(block < BLOCKS)
    def _():
        drain(recv_b.at[pl.ds(0, ROWS * BLOCKS - 1)], d_ssem)

    @pl.when(block == BLOCKS)
    def _():
        drain(recv_b.at[pl.ds(0, ROWS * BLOCKS)], d_ssem)

    tiles = R * share // R

    @pl.when(block < BLOCKS - 1)
    def _():
        drain(recv_b.at[pl.ds(0, (CHAN - 1) * tiles)], e_ssem)

    @pl.when(block == BLOCKS - 1)
    def _():
        drain(recv_b.at[pl.ds(0, (CHAN - 1) * tiles // group)], e_ssem)

    @pl.when(sends_m)
    def _():
        def done(g, carry):
            own, _local, remote = m_copy(g)

            @pl.when(jnp.logical_not(own))
            def _():
                remote().wait_send()

            return carry

        lax.fori_loop(0, per, done, 0)


def shards(pair, norm_gain, proj_weight, gate_weight, hidden_gain, out_weight):
    vmem = pl.BlockSpec(memory_space=pltpu.VMEM)
    sem = pltpu.SemaphoreType.DMA
    tiles = lambda n: pltpu.VMEM((n, R, K), BF16)
    return pl.pallas_call(
        kernel,
        out_shape=jax.ShapeDtypeStruct((R, C // CHAN, WIN), BF16),
        in_specs=[pl.BlockSpec(memory_space=pltpu.HBM)] * 6,
        out_specs=vmem,
        scratch_shapes=[
            pltpu.VMEM((2, C), F32),
            pltpu.VMEM((2, 4, C, H), BF16),
            pltpu.VMEM((2, C, C), BF16),
            pltpu.VMEM((2, H), F32),
            pltpu.VMEM((2, H, C), BF16),
            pltpu.VMEM((R, C, K), BF16),
            pltpu.VMEM((R, C, K), BF16),
            pltpu.VMEM((2, CHAN, 4 * H // CHAN, C), BF16),
            pltpu.VMEM((2, C, C), BF16),
            pltpu.VMEM((2, C, H), BF16),
            pltpu.VMEM((4, C, K), F32),
            pltpu.VMEM((H * R, K), F32),
            pltpu.VMEM((H * R, K), F32),
            pltpu.VMEM((H, 2, R, K), BF16),
            pltpu.VMEM((2, CHAN, TOK, K), BF16),
            pltpu.VMEM((CHAN, TOK, K), BF16),
            tiles(H),
            pltpu.VMEM((R, C, K), F32),
            pltpu.VMEM((R, C, K), BF16),
            pltpu.VMEM((H, 2, R, K), BF16),
            pltpu.VMEM((BLOCKS, TOK, K), BF16),
            pltpu.VMEM((CHAN, TOK, K), BF16),
            pltpu.VMEM((K, R, C), BF16),
            pltpu.VMEM((R, K, C), BF16),
            pltpu.VMEM((BLOCKS, TOK, K), BF16),
            tiles(H),
            pltpu.VMEM((2, R, K), F32),
            pltpu.VMEM((R, C, K), F32),
            pltpu.VMEM((R, C, K), BF16),
            pltpu.VMEM((R, C, K), BF16),
            pltpu.VMEM((R // 4, C, K), BF16),
            pltpu.VMEM((BLOCKS - 1, R, C // CHAN, K), BF16),
            pltpu.VMEM((R // 4, C // CHAN, K), BF16),
            sem((6,)), pltpu.SemaphoreType.REGULAR, sem, sem, sem, sem((4,)), sem, sem, sem, sem,
            sem((K // R,)), sem, sem, sem((4,)), sem, sem, sem,
        ],
        compiler_params=pltpu.CompilerParams(
            collective_id=0, has_side_effects=True, vmem_limit_bytes=VMEM_BYTES
        ),
    )(pair, norm_gain, proj_weight, gate_weight, hidden_gain, out_weight)


def solution(mesh):
    in_specs = (P("rows", None, None), P(), P(), P(), P(), P())
    out_specs = P("rows", "chan", None)
    return jax.shard_map(shards, mesh=mesh, in_specs=in_specs, out_specs=out_specs, check_vma=False)
```

```python
import functools

import jax
import jax.numpy as jnp
from jax import lax
from jax.experimental import pallas as pl
from jax.experimental.pallas import tpu as pltpu
from jax.sharding import PartitionSpec as P

MESH = pl.DeviceIdType.MESH
F32 = jnp.float32
BF16 = jnp.bfloat16
C = 128
H = 128
TOK = 512
WIN = 288
ROWS = 32
CHAN = 4
DEV = ROWS * CHAN
R = TOK // ROWS
K = TOK // CHAN
BLOCKS = 3
SPREAD = 37
VMEM_BYTES = 63 * 1024 * 1024


def swap(n):
    return 2 * lax.rem(n, 2) + n // 2


def turned(r):
    return lax.rem(r // 2 + r // 8, 2)


def column_block(r, c):
    return swap(lax.rem(c + 2 * turned(r), CHAN))


def column_chan(r, b):
    return lax.rem(swap(b) + 2 * turned(r), CHAN)


def far_first(n):
    return jnp.where(n == 0, 2, jnp.where(n == 3, 0, 2 * n - 1))


def row_plane(r, s):
    return lax.rem(r // 8 + far_first(s), 4)


def row_in_plane(r, plane, t):
    x = lax.rem(r // 2 + far_first(t // 2), 4)
    return plane * 8 + x * 2 + lax.rem(r + 1 + t, 2)


def sigmoid(v):
    return 0.5 * jnp.tanh(0.5 * v) + 0.5


def norm_rows(x, gain):
    average = jnp.mean(x, axis=0, keepdims=True)
    centred = x - average
    spread = jnp.mean(centred * centred, axis=0, keepdims=True)
    return (centred * lax.rsqrt(spread + 1e-05) * gain).astype(BF16)


def take_hidden(src, sem, z, stat, r):
    planes, lanes = 4, 4
    near = H // CHAN // planes
    steps = CHAN * near // lanes

    def plane_of(s):
        return lax.rem(r // 8 + planes - far_first(s), planes)

    def some(plane, n):
        first = n * lanes // near * (H // CHAN) + plane * near + lax.rem(n * lanes, near)
        return pl.multiple_of(first, lanes)

    def load(first):
        return src[pl.ds(first, lanes)].astype(F32)

    zero = jnp.zeros((lanes, R, K), F32)
    pivot = None
    sums = (zero, zero)
    for s in range(planes):
        plane = plane_of(s)
        landed = src.at[pl.ds(0, CHAN * near)]
        pltpu.make_async_copy(landed, landed, sem.at[plane]).wait()
        if s == 0:
            total = lax.fori_loop(
                0, steps, lambda n, t: t + load(some(plane, n)), zero, unroll=True
            )
            pivot = jnp.sum(total, axis=0) * (1.0 / (CHAN * near))

        def add(n, carry):
            first = some(plane, n)
            x = load(first)
            rows = pl.ds(pl.multiple_of(first * R, lanes * R), lanes * R)
            z[rows, :] = x.reshape(lanes * R, K)
            d = x - pivot
            return carry[0] + d, carry[1] + d * d

        sums = lax.fori_loop(0, steps, add, sums, unroll=True)
    shift = jnp.sum(sums[0], axis=0) * (1.0 / H)
    spread = jnp.sum(sums[1], axis=0) * (1.0 / H) - shift * shift
    stat[0] = pivot + shift
    stat[1] = lax.rsqrt(spread + 1e-05)


def normed_hidden(z, stat, gain, i):
    row = pl.ds(i, 1)
    return ((z[pl.ds(i, H, stride=R), :] - stat[0, row, :]) * stat[1, row, :] * gain).astype(BF16)


def dot(a, b, dims=((1,), (0,))):
    return lax.dot_general(a, b, (dims, ((), ())), preferred_element_type=F32)


def kernel(
    pair_hbm, ng_hbm, pw_hbm, gw_hbm, hg_hbm, ow_hbm, out_ref,
    ng_ref, pw_ref, gw_ref, hg_ref, ow_ref, x_buf, n_buf, wt, gt, ot, gains, z0, z1,
    send_a, recv_a, out_b, recv_b, gate0, mid,
    send_c, left_c, right_c, send_m, recv_m, out_d, recv_d, stat, gate1, resid, out_e, out_t, recv_e, recv_t,
    load_sem, ready, a_ssem, a_rsem, b_ssem, b_rsem, cl_ssem, cr_ssem, cl_rsem, cr_rsem,
    m_ssem, m_rsem, d_ssem, d_rsem, e_ssem, e_rsem, t_rsem,
):
    r = lax.axis_index("rows")
    c = lax.axis_index("chan")
    hid = c * ROWS + r
    mine = column_block(r, c)
    block = mine

    loads = [
        pltpu.make_async_copy(src, dst, load_sem.at[n])
        for n, (src, dst) in enumerate(
            [
                (pw_hbm, pw_ref),
                (ng_hbm, ng_ref),
                (pair_hbm.at[:, :, pl.ds(pl.multiple_of(mine * K, K), K)], x_buf),
                (gw_hbm, gw_ref),
                (ow_hbm, ow_ref),
                (hg_hbm, hg_ref),
            ]
        )
    ]
    for load in loads:
        load.start()

    barrier = pltpu.get_barrier_semaphore()

    def greet(n, carry):
        r2 = r + n
        r2 = jnp.where(r2 >= ROWS, r2 - ROWS, r2)
        pl.semaphore_signal(barrier, inc=1, device_id=(r2, c), device_id_type=MESH)
        pl.semaphore_signal(barrier, inc=1, device_id=(r2, opposite), device_id_type=MESH)
        return carry

    opposite = lax.rem(c + 2, CHAN)
    partner = 2 * (c // 2) + lax.rem(c + 1, 2)
    lax.fori_loop(0, ROWS, greet, 0, unroll=4)
    pl.semaphore_signal(barrier, inc=1, device_id=(r, partner), device_id_type=MESH)

    share = H // CHAN

    def turn(u):
        def one(m, carry):
            w = jnp.transpose(pw_ref[u, m].astype(F32)).astype(BF16)
            for q in range(CHAN):
                wt[u, q, pl.ds(pl.multiple_of(m * share, share), share), :] = w[
                    q * share : (q + 1) * share
                ]
            return carry

        lax.fori_loop(0, 4, one, 0)

    def column(row):
        return jnp.transpose(jnp.broadcast_to(row, (C, C)))

    loads[0].wait()
    turn(0)
    loads[1].wait()
    gains[0] = column(ng_ref[0:1, :])
    loads[2].wait()

    def norm_in(i, carry):
        n_buf[i] = norm_rows(x_buf[i].astype(F32), gains[0])
        return carry

    lax.fori_loop(0, R, norm_in, 0, unroll=8)

    def project(u, q, dst):
        def one(i, carry):
            y = dot(wt[u, q], n_buf[i])
            z0[pl.ds(i, share, stride=R), :] = sigmoid(y[share : 2 * share]) * y[:share]
            z1[pl.ds(i, share, stride=R), :] = (
                sigmoid(y[3 * share :]) * y[2 * share : 3 * share]
            )
            return carry

        lax.fori_loop(0, R, one, 0, unroll=8)

        def pack(h, carry):
            rows = pl.ds(pl.multiple_of(h * R, R), R)
            dst[q * share + h, 0] = z0[rows, :].astype(BF16)
            dst[q * share + h, 1] = z1[rows, :].astype(BF16)
            return carry

        lax.fori_loop(0, share, pack, 0, unroll=8)

    my_rows = pl.ds(pl.multiple_of(r * R, R), R)

    def chunk_a(s, carry):
        q = 2 * lax.rem(s + c // 2 + 1, 2) + lax.rem(c + s // 2, 2)
        project(0, q, send_a)

        @pl.when(s == 0)
        def _():
            pl.semaphore_wait(barrier, 2 * ROWS + 1)
            pl.semaphore_signal(ready, inc=1, device_id=(r, partner), device_id_type=MESH)

        @pl.when(s == 2)
        def _():
            pl.semaphore_wait(ready, 1)

        def send(t, carry):
            r2 = row_in_plane(r, row_plane(r, t // 8), lax.rem(t, 8))
            h2 = q * ROWS + r2
            src = send_a.at[h2]
            dst = recv_a.at[:, mine, my_rows]

            @pl.when(h2 == hid)
            def _():
                pltpu.make_async_copy(src, dst, a_rsem).start()

            @pl.when(h2 != hid)
            def _():
                pltpu.make_async_remote_copy(
                    src, dst, a_ssem, a_rsem, device_id=(r2, q), device_id_type=MESH
                ).start()

            return carry

        lax.fori_loop(0, ROWS, send, 0)
        return carry

    lax.fori_loop(0, CHAN, chunk_a, 0)

    for load in loads[3:]:
        load.wait()
    turn(1)
    for u in range(2):
        gt[u] = jnp.transpose(gw_ref[u].astype(F32)).astype(BF16)
        ot[u] = jnp.transpose(ow_ref[u].astype(F32)).astype(BF16)
        gains[2 + u] = column(hg_ref[u : u + 1, :])
    gains[1] = column(ng_ref[1:2, :])

    def gate_out(i, carry):
        gate0[i] = sigmoid(dot(gt[0], n_buf[i]))
        return carry

    lax.fori_loop(0, R, gate_out, 0, unroll=8)

    pltpu.make_async_copy(recv_a, recv_a, a_rsem).wait()

    per = K // R

    def send_b(r2, b2):
        c2 = column_chan(r2, b2)
        src = out_b.at[b2, pl.ds(pl.multiple_of(r2 * R, R), R)]
        dst = recv_b.at[hid]
        own = jnp.logical_and(r2 == r, c2 == c)

        @pl.when(own)
        def _():
            pltpu.make_async_copy(src, dst, b_rsem.at[r // 8]).start()

        @pl.when(jnp.logical_not(own))
        def _():
            pltpu.make_async_remote_copy(
                src, dst, b_ssem, b_rsem.at[r // 8], device_id=(r2, c2), device_id_type=MESH
            ).start()

    def chunk_b(s, carry):
        b = row_plane(r, s)
        rows = pl.ds(pl.multiple_of(b * K, K), K)
        left = jnp.concatenate([recv_a[0, n, rows, :] for n in range(TOK // K)], axis=1)
        right = jnp.concatenate([recv_a[1, n] for n in range(TOK // K)], axis=1)
        total = dot(left, right, ((1,), (1,))).astype(BF16)
        for n in range(TOK // K):
            out_b[n, rows, :] = total[:, n * K : (n + 1) * K]

        def send(t, carry):
            send_b(row_in_plane(r, b, t // 2), lax.rem(t + c, 2))
            return carry

        lax.fori_loop(0, per * 2, send, 0)
        return carry

    lax.fori_loop(0, TOK // K, chunk_b, 0)

    def late_b(t, carry):
        send_b(row_in_plane(r, row_plane(r, t // 16), lax.rem(t, 16) // 2), 2 + lax.rem(t + c, 2))
        return carry

    lax.fori_loop(0, ROWS * 2, late_b, 0)

    take_hidden(recv_b, b_rsem, z0, stat, r)

    def update_out(i, carry):
        h = normed_hidden(z0, stat, gains[2], i)
        m = (x_buf[i].astype(F32) + gate0[i] * dot(ot[0], h)).astype(BF16)
        mid[i] = m
        n_buf[i] = norm_rows(m.astype(F32), gains[1])
        return carry

    lax.fori_loop(0, R, update_out, 0, unroll=8)

    def chunk_c(s, carry):
        q = lax.rem(s + c + 1, CHAN)
        project(1, q, send_c)

        def send(t, carry):
            r2 = row_in_plane(r, row_plane(r, t // 8), lax.rem(t, 8))
            h2 = q * ROWS + r2
            right_src, right_dst = send_c.at[h2, 1], right_c.at[mine, my_rows]

            @pl.when(h2 == hid)
            def _():
                pltpu.make_async_copy(right_src, right_dst, cr_rsem).start()

            @pl.when(h2 != hid)
            def _():
                pltpu.make_async_remote_copy(
                    right_src, right_dst, cr_ssem, cr_rsem, device_id=(r2, q), device_id_type=MESH
                ).start()

            @pl.when(mine < BLOCKS)
            def _():
                left_src, left_dst = send_c.at[h2, 0], left_c.at[mine, my_rows]

                @pl.when(h2 == hid)
                def _():
                    pltpu.make_async_copy(left_src, left_dst, cl_rsem).start()

                @pl.when(h2 != hid)
                def _():
                    pltpu.make_async_remote_copy(
                        left_src, left_dst, cl_ssem, cl_rsem,
                        device_id=(r2, q), device_id_type=MESH,
                    ).start()

            return carry

        lax.fori_loop(0, ROWS, send, 0)
        return carry

    lax.fori_loop(0, CHAN, chunk_c, 0)

    sends_m = r * R < WIN
    row_block = r // per
    m_rows = pl.ds(pl.multiple_of(lax.rem(r, per) * R, R), R)

    def m_copy(n):
        g = lax.rem(n + r, per)
        r2 = mine * per + g
        m_chan = column_chan(r2, row_block)
        src = send_m.at[pl.ds(pl.multiple_of(g * R, R), R)]
        dst = recv_m.at[:, m_rows, :]
        own = jnp.logical_and(r2 == r, m_chan == c)
        local = lambda: pltpu.make_async_copy(src, dst, m_rsem)
        remote = lambda: pltpu.make_async_remote_copy(
            src, dst, m_ssem.at[g], m_rsem, device_id=(r2, m_chan), device_id_type=MESH
        )
        return own, local, remote

    @pl.when(sends_m)
    def _():
        def turn_mid(i, carry):
            z0[pl.ds(i, K, stride=R), :] = jnp.transpose(mid[i].astype(F32))
            return carry

        lax.fori_loop(0, R, turn_mid, 0, unroll=8)

        def pack(j, carry):
            send_m[j] = z0[pl.ds(pl.multiple_of(j * R, R), R), :].astype(BF16)
            return carry

        lax.fori_loop(0, K, pack, 0, unroll=8)

        def send(g, carry):
            own, local, remote = m_copy(g)

            @pl.when(own)
            def _():
                local().start()

            @pl.when(jnp.logical_not(own))
            def _():
                remote().start()

            return carry

        lax.fori_loop(0, per, send, 0)

    pltpu.make_async_copy(left_c, left_c, cl_rsem).wait()
    pltpu.make_async_copy(right_c, right_c, cr_rsem).wait()

    tail = WIN - (BLOCKS - 1) * K
    group = K // tail

    def send_d(r2, b2):
        c2 = column_chan(r2, b2)
        src = out_d.at[b2, pl.ds(pl.multiple_of(r2 * R, R), R)]
        dst = recv_d.at[hid]
        own = jnp.logical_and(r2 == r, c2 == c)

        @pl.when(own)
        def _():
            pltpu.make_async_copy(src, dst, d_rsem.at[r // 8]).start()

        @pl.when(jnp.logical_not(own))
        def _():
            pltpu.make_async_remote_copy(
                src, dst, d_ssem, d_rsem.at[r // 8], device_id=(r2, c2), device_id_type=MESH
            ).start()

    def chunk_d(s, carry):
        b = row_plane(r, s)
        cols = pl.ds(pl.multiple_of(b * K, K), K)
        left = jnp.concatenate([left_c[n] for n in range(BLOCKS)], axis=1)
        total = dot(right_c[b], left, ((0,), (0,))).astype(BF16)
        for n in range(BLOCKS):
            out_d[n, cols, :] = total[:, n * K : (n + 1) * K]

        def send(t, carry):
            send_d(row_in_plane(r, b, t // 2), lax.rem(t + c, 2))
            return carry

        lax.fori_loop(0, per * 2, send, 0)
        return carry

    lax.fori_loop(0, TOK // K, chunk_d, 0)

    def late_d(t, carry):
        send_d(row_in_plane(r, row_plane(r, t // 8), lax.rem(t, 8)), BLOCKS - 1)
        return carry

    lax.fori_loop(0, ROWS, late_d, 0)

    @pl.when(block < BLOCKS)
    def _():
        @pl.when(block < BLOCKS - 1)
        def _():
            pltpu.make_async_copy(recv_m, recv_m, m_rsem).wait()

        @pl.when(block == BLOCKS - 1)
        def _():
            part = recv_m.at[:, pl.ds(0, tail), :]
            pltpu.make_async_copy(part, part, m_rsem).wait()

        def gate_in(j, carry):
            m = jnp.transpose(recv_m[j].astype(F32))
            resid[j] = m.astype(BF16)
            gate1[j] = sigmoid(dot(gt[1], norm_rows(m, gains[1])))
            return carry

        lax.fori_loop(0, R, gate_in, 0, unroll=8)

        take_hidden(recv_d, d_rsem, z1, stat, r)

        def update_in(j):
            h = normed_hidden(z1, stat, gains[3], j)
            return (resid[j].astype(F32) + gate1[j] * dot(ot[1], h)).astype(BF16)

        def send(src, dst, sem):
            for s in range(1, CHAN):
                c2 = lax.rem(c + s, CHAN)
                rows = pl.ds(pl.multiple_of(c2 * share, share), share)
                pltpu.make_async_remote_copy(
                    src.at[..., rows, :], dst, e_ssem, sem, device_id=(r, c2), device_id_type=MESH
                ).start()
            rows = pl.ds(pl.multiple_of(c * share, share), share)
            pltpu.make_async_copy(src.at[..., rows, :], dst, sem).start()

        @pl.when(block < BLOCKS - 1)
        def _():
            def whole(g, carry):
                first = pl.multiple_of(g * group, group)
                for t in range(group):
                    out_e[first + t] = update_in(first + t)
                some = pl.ds(first, group)
                send(out_e.at[some], recv_e.at[block, some], e_rsem)
                return carry

            lax.fori_loop(0, R // group, whole, 0)

        @pl.when(block == BLOCKS - 1)
        def _():
            def packed(g, carry):
                first = pl.multiple_of(g * group, group)
                parts = [update_in(first + t)[:, :tail] for t in range(group)]
                out_t[g] = jnp.concatenate(parts, axis=1)
                send(out_t.at[g], recv_t.at[g], t_rsem)
                return carry

            lax.fori_loop(0, R // group, packed, 0)

    pltpu.make_async_copy(recv_e, recv_e, e_rsem).wait()
    for b in range(BLOCKS - 1):
        out_ref[:, :, b * K : (b + 1) * K] = recv_e[b]

    pltpu.make_async_copy(recv_t, recv_t, t_rsem).wait()
    for g in range(R // group):
        for t in range(group):
            out_ref[g * group + t, :, WIN - tail :] = recv_t[g, :, t * tail : (t + 1) * tail]

    def drain(ref, sem):
        pltpu.make_async_copy(ref, ref, sem).wait()

    drain(send_a.at[pl.ds(0, DEV - 1)], a_ssem)
    drain(recv_b.at[pl.ds(0, DEV - 1)], b_ssem)
    drain(recv_b.at[pl.ds(0, DEV - 1)], cr_ssem)

    @pl.when(mine < BLOCKS)
    def _():
        drain(recv_b.at[pl.ds(0, DEV - 1)], cl_ssem)

    @pl.when(block < BLOCKS)
    def _():
        drain(recv_b.at[pl.ds(0, ROWS * BLOCKS - 1)], d_ssem)

    @pl.when(block == BLOCKS)
    def _():
        drain(recv_b.at[pl.ds(0, ROWS * BLOCKS)], d_ssem)

    tiles = R * share // R

    @pl.when(block < BLOCKS - 1)
    def _():
        drain(recv_b.at[pl.ds(0, (CHAN - 1) * tiles)], e_ssem)

    @pl.when(block == BLOCKS - 1)
    def _():
        drain(recv_b.at[pl.ds(0, (CHAN - 1) * tiles // group)], e_ssem)

    @pl.when(sends_m)
    def _():
        def done(g, carry):
            own, _local, remote = m_copy(g)

            @pl.when(jnp.logical_not(own))
            def _():
                remote().wait_send()

            return carry

        lax.fori_loop(0, per, done, 0)


def shards(pair, norm_gain, proj_weight, gate_weight, hidden_gain, out_weight):
    vmem = pl.BlockSpec(memory_space=pltpu.VMEM)
    sem = pltpu.SemaphoreType.DMA
    tiles = lambda n: pltpu.VMEM((n, R, K), BF16)
    return pl.pallas_call(
        kernel,
        out_shape=jax.ShapeDtypeStruct((R, C // CHAN, WIN), BF16),
        in_specs=[pl.BlockSpec(memory_space=pltpu.HBM)] * 6,
        out_specs=vmem,
        scratch_shapes=[
            pltpu.VMEM((2, C), F32),
            pltpu.VMEM((2, 4, C, H), BF16),
            pltpu.VMEM((2, C, C), BF16),
            pltpu.VMEM((2, H), F32),
            pltpu.VMEM((2, H, C), BF16),
            pltpu.VMEM((R, C, K), BF16),
            pltpu.VMEM((R, C, K), BF16),
            pltpu.VMEM((2, CHAN, 4 * H // CHAN, C), BF16),
            pltpu.VMEM((2, C, C), BF16),
            pltpu.VMEM((2, C, H), BF16),
            pltpu.VMEM((4, C, K), F32),
            pltpu.VMEM((H * R + R, K), F32),
            pltpu.VMEM((H * R + R, K), F32),
            pltpu.VMEM((H, 2, R, K), BF16),
            pltpu.VMEM((2, CHAN, TOK, K), BF16),
            pltpu.VMEM((CHAN, TOK, K), BF16),
            tiles(H),
            pltpu.VMEM((R, C, K), F32),
            pltpu.VMEM((R, C, K), BF16),
            pltpu.VMEM((H, 2, R, K), BF16),
            pltpu.VMEM((BLOCKS, TOK, K), BF16),
            pltpu.VMEM((CHAN, TOK, K), BF16),
            pltpu.VMEM((K, R, C), BF16),
            pltpu.VMEM((R, K, C), BF16),
            pltpu.VMEM((BLOCKS, TOK, K), BF16),
            tiles(H),
            pltpu.VMEM((2, R, K), F32),
            pltpu.VMEM((R, C, K), F32),
            pltpu.VMEM((R, C, K), BF16),
            pltpu.VMEM((R, C, K), BF16),
            pltpu.VMEM((R // 4, C, K), BF16),
            pltpu.VMEM((BLOCKS - 1, R, C // CHAN, K), BF16),
            pltpu.VMEM((R // 4, C // CHAN, K), BF16),
            sem((6,)), pltpu.SemaphoreType.REGULAR, sem, sem, sem, sem((4,)), sem, sem, sem, sem,
            sem((K // R,)), sem, sem, sem((4,)), sem, sem, sem,
        ],
        compiler_params=pltpu.CompilerParams(
            collective_id=0, has_side_effects=True, vmem_limit_bytes=VMEM_BYTES
        ),
    )(pair, norm_gain, proj_weight, gate_weight, hidden_gain, out_weight)


def solution(mesh):
    in_specs = (P("rows", None, None), P(), P(), P(), P(), P())
    out_specs = P("rows", "chan", None)
    return jax.shard_map(shards, mesh=mesh, in_specs=in_specs, out_specs=out_specs, check_vma=False)
```

```python
import functools

import jax
import jax.numpy as jnp
from jax import lax
from jax.experimental import pallas as pl
from jax.experimental.pallas import tpu as pltpu
from jax.sharding import PartitionSpec as P

MESH = pl.DeviceIdType.MESH
F32 = jnp.float32
BF16 = jnp.bfloat16
C = 128
H = 128
TOK = 512
WIN = 288
ROWS = 32
CHAN = 4
DEV = ROWS * CHAN
R = TOK // ROWS
K = TOK // CHAN
BLOCKS = 3
SPREAD = 37
VMEM_BYTES = 63 * 1024 * 1024


def swap(n):
    return 2 * lax.rem(n, 2) + n // 2


def turned(r):
    return lax.rem(r // 2 + r // 8, 2)


def column_block(r, c):
    return swap(lax.rem(c + 2 * turned(r), CHAN))


def column_chan(r, b):
    return lax.rem(swap(b) + 2 * turned(r), CHAN)


def far_first(n):
    return jnp.where(n == 0, 2, jnp.where(n == 3, 0, 2 * n - 1))


def row_plane(r, s):
    return lax.rem(r // 8 + far_first(s), 4)


def row_in_plane(r, plane, t):
    x = lax.rem(r // 2 + far_first(t // 2), 4)
    return plane * 8 + x * 2 + lax.rem(r + 1 + t, 2)


def sigmoid(v):
    return 0.5 * jnp.tanh(0.5 * v) + 0.5


def norm_rows(x, gain):
    average = jnp.mean(x, axis=0, keepdims=True)
    centred = x - average
    spread = jnp.mean(centred * centred, axis=0, keepdims=True)
    return (centred * lax.rsqrt(spread + 1e-05) * gain).astype(BF16)


def take_hidden(src, sem, z, stat, r):
    planes, lanes = 4, 4
    near = H // CHAN // planes
    steps = CHAN * near // lanes

    def plane_of(s):
        return lax.rem(r // 8 + planes - far_first(s), planes)

    def some(plane, n):
        first = n * lanes // near * (H // CHAN) + plane * near + lax.rem(n * lanes, near)
        return pl.multiple_of(first, lanes)

    def load(first):
        return src[pl.ds(first, lanes)].astype(F32)

    zero = jnp.zeros((lanes, R, K), F32)
    pivot = None
    sums = (zero, zero)
    for s in range(planes):
        plane = plane_of(s)
        landed = src.at[pl.ds(0, CHAN * near)]
        pltpu.make_async_copy(landed, landed, sem.at[plane]).wait()
        if s == 0:
            total = lax.fori_loop(
                0, steps, lambda n, t: t + load(some(plane, n)), zero, unroll=True
            )
            pivot = jnp.sum(total, axis=0) * (1.0 / (CHAN * near))

        def add(n, carry):
            first = some(plane, n)
            x = load(first)
            rows = pl.ds(pl.multiple_of(first * R, lanes * R), lanes * R)
            z[rows, :] = x.reshape(lanes * R, K)
            d = x - pivot
            return carry[0] + d, carry[1] + d * d

        sums = lax.fori_loop(0, steps, add, sums, unroll=True)
    shift = jnp.sum(sums[0], axis=0) * (1.0 / H)
    spread = jnp.sum(sums[1], axis=0) * (1.0 / H) - shift * shift
    stat[0] = pivot + shift
    stat[1] = lax.rsqrt(spread + 1e-05)


def normed_hidden(z, stat, gain, i):
    row = pl.ds(i, 1)
    return ((z[pl.ds(i, H, stride=R), :] - stat[0, row, :]) * stat[1, row, :] * gain).astype(BF16)


def dot(a, b, dims=((1,), (0,))):
    return lax.dot_general(a, b, (dims, ((), ())), preferred_element_type=F32)


def kernel(
    pair_hbm, ng_hbm, pw_hbm, gw_hbm, hg_hbm, ow_hbm, out_ref,
    ng_ref, pw_ref, gw_ref, hg_ref, ow_ref, x_buf, n_buf, wt, gt, ot, gains, z0, z1,
    send_a, recv_a, out_b, recv_b, gate0, mid,
    send_c, left_c, right_c, send_m, recv_m, out_d, recv_d, stat, gate1, resid, out_e, out_t, recv_e, recv_t,
    load_sem, ready, a_ssem, a_rsem, b_ssem, b_rsem, cl_ssem, cr_ssem, cl_rsem, cr_rsem,
    m_ssem, m_rsem, d_ssem, d_rsem, e_ssem, e_rsem, t_rsem,
):
    r = lax.axis_index("rows")
    c = lax.axis_index("chan")
    hid = c * ROWS + r
    mine = column_block(r, c)
    block = mine

    loads = [
        pltpu.make_async_copy(src, dst, load_sem.at[n])
        for n, (src, dst) in enumerate(
            [
                (pw_hbm, pw_ref),
                (ng_hbm, ng_ref),
                (pair_hbm.at[:, :, pl.ds(pl.multiple_of(mine * K, K), K)], x_buf),
                (gw_hbm, gw_ref),
                (ow_hbm, ow_ref),
                (hg_hbm, hg_ref),
            ]
        )
    ]
    for load in loads:
        load.start()

    barrier = pltpu.get_barrier_semaphore()

    def greet(n, carry):
        r2 = r + n
        r2 = jnp.where(r2 >= ROWS, r2 - ROWS, r2)
        pl.semaphore_signal(barrier, inc=1, device_id=(r2, c), device_id_type=MESH)
        pl.semaphore_signal(barrier, inc=1, device_id=(r2, opposite), device_id_type=MESH)
        return carry

    opposite = lax.rem(c + 2, CHAN)
    partner = 2 * (c // 2) + lax.rem(c + 1, 2)
    lax.fori_loop(0, ROWS, greet, 0, unroll=4)
    pl.semaphore_signal(barrier, inc=1, device_id=(r, partner), device_id_type=MESH)

    share = H // CHAN

    def turn(u):
        def one(m, carry):
            w = jnp.transpose(pw_ref[u, m].astype(F32)).astype(BF16)
            for q in range(CHAN):
                wt[u, q, pl.ds(pl.multiple_of(m * share, share), share), :] = w[
                    q * share : (q + 1) * share
                ]
            return carry

        lax.fori_loop(0, 4, one, 0)

    def column(row):
        return jnp.transpose(jnp.broadcast_to(row, (C, C)))

    loads[0].wait()
    turn(0)
    loads[1].wait()
    gains[0] = column(ng_ref[0:1, :])
    loads[2].wait()

    def norm_in(i, carry):
        n_buf[i] = norm_rows(x_buf[i].astype(F32), gains[0])
        return carry

    lax.fori_loop(0, R, norm_in, 0, unroll=8)

    def project(u, q, dst):
        def one(i, carry):
            y = dot(wt[u, q], n_buf[i])
            z0[pl.ds(i, share, stride=R), :] = sigmoid(y[share : 2 * share]) * y[:share]
            z1[pl.ds(i, share, stride=R), :] = (
                sigmoid(y[3 * share :]) * y[2 * share : 3 * share]
            )
            return carry

        lax.fori_loop(0, R, one, 0, unroll=8)

        def pack(h, carry):
            rows = pl.ds(pl.multiple_of(h * R, R), R)
            dst[q * share + h, 0] = z0[rows, :].astype(BF16)
            dst[q * share + h, 1] = z1[rows, :].astype(BF16)
            return carry

        lax.fori_loop(0, share, pack, 0, unroll=8)

    my_rows = pl.ds(pl.multiple_of(r * R, R), R)

    def chunk_a(s, carry):
        q = 2 * lax.rem(s + c // 2 + 1, 2) + lax.rem(c + s // 2, 2)
        project(0, q, send_a)

        @pl.when(s == 0)
        def _():
            pl.semaphore_wait(barrier, 2 * ROWS + 1)
            pl.semaphore_signal(ready, inc=1, device_id=(r, partner), device_id_type=MESH)

        @pl.when(s == 2)
        def _():
            pl.semaphore_wait(ready, 1)

        def send(t, carry):
            r2 = row_in_plane(r, row_plane(r, t // 8), lax.rem(t, 8))
            h2 = q * ROWS + r2
            src = send_a.at[h2]
            dst = recv_a.at[:, mine, my_rows]

            @pl.when(h2 == hid)
            def _():
                pltpu.make_async_copy(src, dst, a_rsem).start()

            @pl.when(h2 != hid)
            def _():
                pltpu.make_async_remote_copy(
                    src, dst, a_ssem, a_rsem, device_id=(r2, q), device_id_type=MESH
                ).start()

            return carry

        lax.fori_loop(0, ROWS, send, 0)
        return carry

    lax.fori_loop(0, CHAN, chunk_a, 0)

    for load in loads[3:]:
        load.wait()
    turn(1)
    for u in range(2):
        gt[u] = jnp.transpose(gw_ref[u].astype(F32)).astype(BF16)
        ot[u] = jnp.transpose(ow_ref[u].astype(F32)).astype(BF16)
        gains[2 + u] = column(hg_ref[u : u + 1, :])
    gains[1] = column(ng_ref[1:2, :])

    def gate_out(i, carry):
        gate0[i] = sigmoid(dot(gt[0], n_buf[i]))
        return carry

    lax.fori_loop(0, R, gate_out, 0, unroll=8)

    pltpu.make_async_copy(recv_a, recv_a, a_rsem).wait()

    per = K // R

    def send_b(r2, b2):
        c2 = column_chan(r2, b2)
        src = out_b.at[b2, pl.ds(pl.multiple_of(r2 * R, R), R)]
        dst = recv_b.at[hid]
        own = jnp.logical_and(r2 == r, c2 == c)

        @pl.when(own)
        def _():
            pltpu.make_async_copy(src, dst, b_rsem.at[r // 8]).start()

        @pl.when(jnp.logical_not(own))
        def _():
            pltpu.make_async_remote_copy(
                src, dst, b_ssem, b_rsem.at[r // 8], device_id=(r2, c2), device_id_type=MESH
            ).start()

    def chunk_b(s, carry):
        b = row_plane(r, s)
        rows = pl.ds(pl.multiple_of(b * K, K), K)
        left = jnp.concatenate([recv_a[0, n, rows, :] for n in range(TOK // K)], axis=1)
        right = jnp.concatenate([recv_a[1, n] for n in range(TOK // K)], axis=1)
        total = dot(left, right, ((1,), (1,))).astype(BF16)
        for n in range(TOK // K):
            out_b[n, rows, :] = total[:, n * K : (n + 1) * K]

        def send(t, carry):
            send_b(row_in_plane(r, b, t // 2), lax.rem(t + c, 2))
            return carry

        lax.fori_loop(0, per * 2, send, 0)
        return carry

    lax.fori_loop(0, TOK // K, chunk_b, 0)

    def late_b(t, carry):
        send_b(row_in_plane(r, row_plane(r, t // 16), lax.rem(t, 16) // 2), 2 + lax.rem(t + c, 2))
        return carry

    lax.fori_loop(0, ROWS * 2, late_b, 0)

    take_hidden(recv_b, b_rsem, z0, stat, r)

    def update_out(i, carry):
        h = normed_hidden(z0, stat, gains[2], i)
        m = (x_buf[i].astype(F32) + gate0[i] * dot(ot[0], h)).astype(BF16)
        mid[i] = m
        n_buf[i] = norm_rows(m.astype(F32), gains[1])
        return carry

    lax.fori_loop(0, R, update_out, 0, unroll=8)

    def chunk_c(s, carry):
        q = lax.rem(s + c + 1, CHAN)
        project(1, q, send_c)

        def send(t, carry):
            r2 = row_in_plane(r, row_plane(r, t // 8), lax.rem(t, 8))
            h2 = q * ROWS + r2
            right_src, right_dst = send_c.at[h2, 1], right_c.at[mine, my_rows]

            @pl.when(h2 == hid)
            def _():
                pltpu.make_async_copy(right_src, right_dst, cr_rsem).start()

            @pl.when(h2 != hid)
            def _():
                pltpu.make_async_remote_copy(
                    right_src, right_dst, cr_ssem, cr_rsem, device_id=(r2, q), device_id_type=MESH
                ).start()

            @pl.when(mine < BLOCKS)
            def _():
                left_src, left_dst = send_c.at[h2, 0], left_c.at[mine, my_rows]

                @pl.when(h2 == hid)
                def _():
                    pltpu.make_async_copy(left_src, left_dst, cl_rsem).start()

                @pl.when(h2 != hid)
                def _():
                    pltpu.make_async_remote_copy(
                        left_src, left_dst, cl_ssem, cl_rsem,
                        device_id=(r2, q), device_id_type=MESH,
                    ).start()

            return carry

        lax.fori_loop(0, ROWS, send, 0)
        return carry

    lax.fori_loop(0, CHAN, chunk_c, 0)

    sends_m = r * R < WIN
    row_block = r // per
    m_rows = pl.ds(pl.multiple_of(lax.rem(r, per) * R, R), R)

    def m_copy(n):
        g = lax.rem(n + r, per)
        r2 = mine * per + g
        m_chan = column_chan(r2, row_block)
        src = send_m.at[pl.ds(pl.multiple_of(g * R, R), R)]
        dst = recv_m.at[:, m_rows, :]
        own = jnp.logical_and(r2 == r, m_chan == c)
        local = lambda: pltpu.make_async_copy(src, dst, m_rsem)
        remote = lambda: pltpu.make_async_remote_copy(
            src, dst, m_ssem.at[g], m_rsem, device_id=(r2, m_chan), device_id_type=MESH
        )
        return own, local, remote

    @pl.when(sends_m)
    def _():
        def turn_mid(i, carry):
            z0[pl.ds(i, K, stride=R), :] = jnp.transpose(mid[i].astype(F32))
            return carry

        lax.fori_loop(0, R, turn_mid, 0, unroll=8)

        def pack(j, carry):
            send_m[j] = z0[pl.ds(pl.multiple_of(j * R, R), R), :].astype(BF16)
            return carry

        lax.fori_loop(0, K, pack, 0, unroll=8)

        def send(g, carry):
            own, local, remote = m_copy(g)

            @pl.when(own)
            def _():
                local().start()

            @pl.when(jnp.logical_not(own))
            def _():
                remote().start()

            return carry

        lax.fori_loop(0, per, send, 0)

    pltpu.make_async_copy(left_c, left_c, cl_rsem).wait()
    pltpu.make_async_copy(right_c, right_c, cr_rsem).wait()

    tail = WIN - (BLOCKS - 1) * K
    group = K // tail

    def send_d(r2, b2):
        c2 = column_chan(r2, b2)
        src = out_d.at[b2, pl.ds(pl.multiple_of(r2 * R, R), R)]
        dst = recv_d.at[hid]
        own = jnp.logical_and(r2 == r, c2 == c)

        @pl.when(own)
        def _():
            pltpu.make_async_copy(src, dst, d_rsem.at[r // 8]).start()

        @pl.when(jnp.logical_not(own))
        def _():
            pltpu.make_async_remote_copy(
                src, dst, d_ssem, d_rsem.at[r // 8], device_id=(r2, c2), device_id_type=MESH
            ).start()

    def chunk_d(s, carry):
        b = row_plane(r, s)
        cols = pl.ds(pl.multiple_of(b * K, K), K)
        left = jnp.concatenate([left_c[n] for n in range(BLOCKS)], axis=1)
        total = dot(right_c[b], left, ((0,), (0,))).astype(BF16)
        for n in range(BLOCKS):
            out_d[n, cols, :] = total[:, n * K : (n + 1) * K]

        def send(t, carry):
            send_d(row_in_plane(r, b, t // 2), lax.rem(t + c, 2))
            return carry

        lax.fori_loop(0, per * 2, send, 0)
        return carry

    lax.fori_loop(0, TOK // K, chunk_d, 0)

    def late_d(t, carry):
        send_d(row_in_plane(r, row_plane(r, t // 8), lax.rem(t, 8)), BLOCKS - 1)
        return carry

    lax.fori_loop(0, ROWS, late_d, 0)

    @pl.when(block < BLOCKS)
    def _():
        @pl.when(block < BLOCKS - 1)
        def _():
            pltpu.make_async_copy(recv_m, recv_m, m_rsem).wait()

        @pl.when(block == BLOCKS - 1)
        def _():
            part = recv_m.at[:, pl.ds(0, tail), :]
            pltpu.make_async_copy(part, part, m_rsem).wait()

        def gate_in(j, carry):
            m = jnp.transpose(recv_m[j].astype(F32))
            resid[j] = m.astype(BF16)
            gate1[j] = sigmoid(dot(gt[1], norm_rows(m, gains[1])))
            return carry

        lax.fori_loop(0, R, gate_in, 0, unroll=8)

        take_hidden(recv_d, d_rsem, z1, stat, r)

        def update_in(j):
            h = normed_hidden(z1, stat, gains[3], j)
            return (resid[j].astype(F32) + gate1[j] * dot(ot[1], h)).astype(BF16)

        def send(src, dst, sem):
            for s in range(1, CHAN):
                c2 = lax.rem(c + s, CHAN)
                rows = pl.ds(pl.multiple_of(c2 * share, share), share)
                pltpu.make_async_remote_copy(
                    src.at[..., rows, :], dst, e_ssem, sem, device_id=(r, c2), device_id_type=MESH
                ).start()
            rows = pl.ds(pl.multiple_of(c * share, share), share)
            pltpu.make_async_copy(src.at[..., rows, :], dst, sem).start()

        @pl.when(block < BLOCKS - 1)
        def _():
            def whole(g, carry):
                first = pl.multiple_of(g * group, group)
                for t in range(group):
                    out_e[first + t] = update_in(first + t)
                some = pl.ds(first, group)
                send(out_e.at[some], recv_e.at[block, some], e_rsem)
                return carry

            lax.fori_loop(0, R // group, whole, 0, unroll=True)

        @pl.when(block == BLOCKS - 1)
        def _():
            def packed(g, carry):
                first = pl.multiple_of(g * group, group)
                parts = [update_in(first + t)[:, :tail] for t in range(group)]
                out_t[g] = jnp.concatenate(parts, axis=1)
                send(out_t.at[g], recv_t.at[g], t_rsem)
                return carry

            lax.fori_loop(0, R // group, packed, 0)

    pltpu.make_async_copy(recv_e, recv_e, e_rsem).wait()
    for b in range(BLOCKS - 1):
        out_ref[:, :, b * K : (b + 1) * K] = recv_e[b]

    pltpu.make_async_copy(recv_t, recv_t, t_rsem).wait()
    for g in range(R // group):
        for t in range(group):
            out_ref[g * group + t, :, WIN - tail :] = recv_t[g, :, t * tail : (t + 1) * tail]

    def drain(ref, sem):
        pltpu.make_async_copy(ref, ref, sem).wait()

    drain(send_a.at[pl.ds(0, DEV - 1)], a_ssem)
    drain(recv_b.at[pl.ds(0, DEV - 1)], b_ssem)
    drain(recv_b.at[pl.ds(0, DEV - 1)], cr_ssem)

    @pl.when(mine < BLOCKS)
    def _():
        drain(recv_b.at[pl.ds(0, DEV - 1)], cl_ssem)

    @pl.when(block < BLOCKS)
    def _():
        drain(recv_b.at[pl.ds(0, ROWS * BLOCKS - 1)], d_ssem)

    @pl.when(block == BLOCKS)
    def _():
        drain(recv_b.at[pl.ds(0, ROWS * BLOCKS)], d_ssem)

    tiles = R * share // R

    @pl.when(block < BLOCKS - 1)
    def _():
        drain(recv_b.at[pl.ds(0, (CHAN - 1) * tiles)], e_ssem)

    @pl.when(block == BLOCKS - 1)
    def _():
        drain(recv_b.at[pl.ds(0, (CHAN - 1) * tiles // group)], e_ssem)

    @pl.when(sends_m)
    def _():
        def done(g, carry):
            own, _local, remote = m_copy(g)

            @pl.when(jnp.logical_not(own))
            def _():
                remote().wait_send()

            return carry

        lax.fori_loop(0, per, done, 0)


def shards(pair, norm_gain, proj_weight, gate_weight, hidden_gain, out_weight):
    vmem = pl.BlockSpec(memory_space=pltpu.VMEM)
    sem = pltpu.SemaphoreType.DMA
    tiles = lambda n: pltpu.VMEM((n, R, K), BF16)
    return pl.pallas_call(
        kernel,
        out_shape=jax.ShapeDtypeStruct((R, C // CHAN, WIN), BF16),
        in_specs=[pl.BlockSpec(memory_space=pltpu.HBM)] * 6,
        out_specs=vmem,
        scratch_shapes=[
            pltpu.VMEM((2, C), F32),
            pltpu.VMEM((2, 4, C, H), BF16),
            pltpu.VMEM((2, C, C), BF16),
            pltpu.VMEM((2, H), F32),
            pltpu.VMEM((2, H, C), BF16),
            pltpu.VMEM((R, C, K), BF16),
            pltpu.VMEM((R, C, K), BF16),
            pltpu.VMEM((2, CHAN, 4 * H // CHAN, C), BF16),
            pltpu.VMEM((2, C, C), BF16),
            pltpu.VMEM((2, C, H), BF16),
            pltpu.VMEM((4, C, K), F32),
            pltpu.VMEM((H * R + R, K), F32),
            pltpu.VMEM((H * R + R, K), F32),
            pltpu.VMEM((H, 2, R, K), BF16),
            pltpu.VMEM((2, CHAN, TOK, K), BF16),
            pltpu.VMEM((CHAN, TOK, K), BF16),
            tiles(H),
            pltpu.VMEM((R, C, K), F32),
            pltpu.VMEM((R, C, K), BF16),
            pltpu.VMEM((H, 2, R, K), BF16),
            pltpu.VMEM((BLOCKS, TOK, K), BF16),
            pltpu.VMEM((CHAN, TOK, K), BF16),
            pltpu.VMEM((K, R, C), BF16),
            pltpu.VMEM((R, K, C), BF16),
            pltpu.VMEM((BLOCKS, TOK, K), BF16),
            tiles(H),
            pltpu.VMEM((2, R, K), F32),
            pltpu.VMEM((R, C, K), F32),
            pltpu.VMEM((R, C, K), BF16),
            pltpu.VMEM((R, C, K), BF16),
            pltpu.VMEM((R // 4, C, K), BF16),
            pltpu.VMEM((BLOCKS - 1, R, C // CHAN, K), BF16),
            pltpu.VMEM((R // 4, C // CHAN, K), BF16),
            sem((6,)), pltpu.SemaphoreType.REGULAR, sem, sem, sem, sem((4,)), sem, sem, sem, sem,
            sem((K // R,)), sem, sem, sem((4,)), sem, sem, sem,
        ],
        compiler_params=pltpu.CompilerParams(
            collective_id=0, has_side_effects=True, vmem_limit_bytes=VMEM_BYTES
        ),
    )(pair, norm_gain, proj_weight, gate_weight, hidden_gain, out_weight)


def solution(mesh):
    in_specs = (P("rows", None, None), P(), P(), P(), P(), P())
    out_specs = P("rows", "chan", None)
    return jax.shard_map(shards, mesh=mesh, in_specs=in_specs, out_specs=out_specs, check_vma=False)
```

```python
import functools

import jax
import jax.numpy as jnp
from jax import lax
from jax.experimental import pallas as pl
from jax.experimental.pallas import tpu as pltpu
from jax.sharding import PartitionSpec as P

MESH = pl.DeviceIdType.MESH
F32 = jnp.float32
BF16 = jnp.bfloat16
C = 128
H = 128
TOK = 512
WIN = 288
ROWS = 32
CHAN = 4
DEV = ROWS * CHAN
R = TOK // ROWS
K = TOK // CHAN
BLOCKS = 3
SPREAD = 37
VMEM_BYTES = 63 * 1024 * 1024


def swap(n):
    return 2 * lax.rem(n, 2) + n // 2


def turned(r):
    return lax.rem(r // 2 + r // 8, 2)


def column_block(r, c):
    return swap(lax.rem(c + 2 * turned(r), CHAN))


def column_chan(r, b):
    return lax.rem(swap(b) + 2 * turned(r), CHAN)


def far_first(n):
    return jnp.where(n == 0, 2, jnp.where(n == 3, 0, 2 * n - 1))


def row_plane(r, s):
    return lax.rem(r // 8 + far_first(s), 4)


def row_in_plane(r, plane, t):
    x = lax.rem(r // 2 + far_first(t // 2), 4)
    return plane * 8 + x * 2 + lax.rem(r + 1 + t, 2)


def sigmoid(v):
    return 0.5 * jnp.tanh(0.5 * v) + 0.5


def norm_rows(x, gain):
    average = jnp.mean(x, axis=0, keepdims=True)
    centred = x - average
    spread = jnp.mean(centred * centred, axis=0, keepdims=True)
    return (centred * lax.rsqrt(spread + 1e-05) * gain).astype(BF16)


def take_hidden(src, sem, z, stat, r):
    planes, lanes = 4, 4
    near = H // CHAN // planes
    steps = CHAN * near // lanes

    def plane_of(s):
        return lax.rem(r // 8 + planes - far_first(s), planes)

    def some(plane, n):
        first = n * lanes // near * (H // CHAN) + plane * near + lax.rem(n * lanes, near)
        return pl.multiple_of(first, lanes)

    def load(first):
        return src[pl.ds(first, lanes)].astype(F32)

    zero = jnp.zeros((lanes, R, K), F32)
    pivot = None
    sums = (zero, zero)
    for s in range(planes):
        plane = plane_of(s)
        landed = src.at[pl.ds(0, CHAN * near)]
        pltpu.make_async_copy(landed, landed, sem.at[plane]).wait()
        if s == 0:
            total = lax.fori_loop(
                0, steps, lambda n, t: t + load(some(plane, n)), zero, unroll=True
            )
            pivot = jnp.sum(total, axis=0) * (1.0 / (CHAN * near))

        def add(n, carry):
            first = some(plane, n)
            x = load(first)
            rows = pl.ds(pl.multiple_of(first * R, lanes * R), lanes * R)
            z[rows, :] = x.reshape(lanes * R, K)
            d = x - pivot
            return carry[0] + d, carry[1] + d * d

        sums = lax.fori_loop(0, steps, add, sums, unroll=True)
    shift = jnp.sum(sums[0], axis=0) * (1.0 / H)
    spread = jnp.sum(sums[1], axis=0) * (1.0 / H) - shift * shift
    stat[0] = pivot + shift
    stat[1] = lax.rsqrt(spread + 1e-05)


def normed_hidden(z, stat, gain, i):
    row = pl.ds(i, 1)
    return ((z[pl.ds(i, H, stride=R), :] - stat[0, row, :]) * stat[1, row, :] * gain).astype(BF16)


def dot(a, b, dims=((1,), (0,))):
    return lax.dot_general(a, b, (dims, ((), ())), preferred_element_type=F32)


def kernel(
    pair_hbm, ng_hbm, pw_hbm, gw_hbm, hg_hbm, ow_hbm, out_ref,
    ng_ref, pw_ref, gw_ref, hg_ref, ow_ref, x_buf, n_buf, wt, gt, ot, gains, z0, z1,
    send_a, recv_a, out_b, recv_b, gate0, mid,
    send_c, left_c, right_c, send_m, recv_m, out_d, recv_d, stat, gate1, resid, out_e, out_t, recv_e, recv_t,
    load_sem, ready, a_ssem, a_rsem, b_ssem, b_rsem, cl_ssem, cr_ssem, cl_rsem, cr_rsem,
    m_ssem, m_rsem, d_ssem, d_rsem, e_ssem, e_rsem, t_rsem,
):
    r = lax.axis_index("rows")
    c = lax.axis_index("chan")
    hid = c * ROWS + r
    mine = column_block(r, c)
    block = mine

    loads = [
        pltpu.make_async_copy(src, dst, load_sem.at[n])
        for n, (src, dst) in enumerate(
            [
                (pw_hbm, pw_ref),
                (ng_hbm, ng_ref),
                (pair_hbm.at[:, :, pl.ds(pl.multiple_of(mine * K, K), K)], x_buf),
                (gw_hbm, gw_ref),
                (ow_hbm, ow_ref),
                (hg_hbm, hg_ref),
            ]
        )
    ]
    for load in loads:
        load.start()

    barrier = pltpu.get_barrier_semaphore()

    def greet(n, carry):
        r2 = r + n
        r2 = jnp.where(r2 >= ROWS, r2 - ROWS, r2)
        pl.semaphore_signal(barrier, inc=1, device_id=(r2, c), device_id_type=MESH)
        pl.semaphore_signal(barrier, inc=1, device_id=(r2, opposite), device_id_type=MESH)
        return carry

    opposite = lax.rem(c + 2, CHAN)
    partner = 2 * (c // 2) + lax.rem(c + 1, 2)
    lax.fori_loop(0, ROWS, greet, 0, unroll=4)
    pl.semaphore_signal(barrier, inc=1, device_id=(r, partner), device_id_type=MESH)

    share = H // CHAN

    def turn(u):
        def one(m, carry):
            w = jnp.transpose(pw_ref[u, m].astype(F32)).astype(BF16)
            for q in range(CHAN):
                wt[u, q, pl.ds(pl.multiple_of(m * share, share), share), :] = w[
                    q * share : (q + 1) * share
                ]
            return carry

        lax.fori_loop(0, 4, one, 0, unroll=True)

    def column(row):
        return jnp.transpose(jnp.broadcast_to(row, (C, C)))

    loads[0].wait()
    turn(0)
    loads[1].wait()
    gains[0] = column(ng_ref[0:1, :])
    loads[2].wait()

    def norm_in(i, carry):
        n_buf[i] = norm_rows(x_buf[i].astype(F32), gains[0])
        return carry

    lax.fori_loop(0, R, norm_in, 0, unroll=8)

    def project(u, q, dst):
        def one(i, carry):
            y = dot(wt[u, q], n_buf[i])
            z0[pl.ds(i, share, stride=R), :] = sigmoid(y[share : 2 * share]) * y[:share]
            z1[pl.ds(i, share, stride=R), :] = (
                sigmoid(y[3 * share :]) * y[2 * share : 3 * share]
            )
            return carry

        lax.fori_loop(0, R, one, 0, unroll=8)

        def pack(h, carry):
            rows = pl.ds(pl.multiple_of(h * R, R), R)
            dst[q * share + h, 0] = z0[rows, :].astype(BF16)
            dst[q * share + h, 1] = z1[rows, :].astype(BF16)
            return carry

        lax.fori_loop(0, share, pack, 0, unroll=8)

    my_rows = pl.ds(pl.multiple_of(r * R, R), R)

    def chunk_a(s, carry):
        q = 2 * lax.rem(s + c // 2 + 1, 2) + lax.rem(c + s // 2, 2)
        project(0, q, send_a)

        @pl.when(s == 0)
        def _():
            pl.semaphore_wait(barrier, 2 * ROWS + 1)
            pl.semaphore_signal(ready, inc=1, device_id=(r, partner), device_id_type=MESH)

        @pl.when(s == 2)
        def _():
            pl.semaphore_wait(ready, 1)

        def send(t, carry):
            r2 = row_in_plane(r, row_plane(r, t // 8), lax.rem(t, 8))
            h2 = q * ROWS + r2
            src = send_a.at[h2]
            dst = recv_a.at[:, mine, my_rows]

            @pl.when(h2 == hid)
            def _():
                pltpu.make_async_copy(src, dst, a_rsem).start()

            @pl.when(h2 != hid)
            def _():
                pltpu.make_async_remote_copy(
                    src, dst, a_ssem, a_rsem, device_id=(r2, q), device_id_type=MESH
                ).start()

            return carry

        lax.fori_loop(0, ROWS, send, 0)
        return carry

    lax.fori_loop(0, CHAN, chunk_a, 0)

    for load in loads[3:]:
        load.wait()
    turn(1)
    for u in range(2):
        gt[u] = jnp.transpose(gw_ref[u].astype(F32)).astype(BF16)
        ot[u] = jnp.transpose(ow_ref[u].astype(F32)).astype(BF16)
        gains[2 + u] = column(hg_ref[u : u + 1, :])
    gains[1] = column(ng_ref[1:2, :])

    def gate_out(i, carry):
        gate0[i] = sigmoid(dot(gt[0], n_buf[i]))
        return carry

    lax.fori_loop(0, R, gate_out, 0, unroll=8)

    pltpu.make_async_copy(recv_a, recv_a, a_rsem).wait()

    per = K // R

    def send_b(r2, b2):
        c2 = column_chan(r2, b2)
        src = out_b.at[b2, pl.ds(pl.multiple_of(r2 * R, R), R)]
        dst = recv_b.at[hid]
        own = jnp.logical_and(r2 == r, c2 == c)

        @pl.when(own)
        def _():
            pltpu.make_async_copy(src, dst, b_rsem.at[r // 8]).start()

        @pl.when(jnp.logical_not(own))
        def _():
            pltpu.make_async_remote_copy(
                src, dst, b_ssem, b_rsem.at[r // 8], device_id=(r2, c2), device_id_type=MESH
            ).start()

    def chunk_b(s, carry):
        b = row_plane(r, s)
        rows = pl.ds(pl.multiple_of(b * K, K), K)
        left = jnp.concatenate([recv_a[0, n, rows, :] for n in range(TOK // K)], axis=1)
        right = jnp.concatenate([recv_a[1, n] for n in range(TOK // K)], axis=1)
        total = dot(left, right, ((1,), (1,))).astype(BF16)
        for n in range(TOK // K):
            out_b[n, rows, :] = total[:, n * K : (n + 1) * K]

        def send(t, carry):
            send_b(row_in_plane(r, b, t // 2), lax.rem(t + c, 2))
            return carry

        lax.fori_loop(0, per * 2, send, 0)
        return carry

    lax.fori_loop(0, TOK // K, chunk_b, 0)

    def late_b(t, carry):
        send_b(row_in_plane(r, row_plane(r, t // 16), lax.rem(t, 16) // 2), 2 + lax.rem(t + c, 2))
        return carry

    lax.fori_loop(0, ROWS * 2, late_b, 0)

    take_hidden(recv_b, b_rsem, z0, stat, r)

    def update_out(i, carry):
        h = normed_hidden(z0, stat, gains[2], i)
        m = (x_buf[i].astype(F32) + gate0[i] * dot(ot[0], h)).astype(BF16)
        mid[i] = m
        n_buf[i] = norm_rows(m.astype(F32), gains[1])
        return carry

    lax.fori_loop(0, R, update_out, 0, unroll=8)

    def chunk_c(s, carry):
        q = lax.rem(s + c + 1, CHAN)
        project(1, q, send_c)

        def send(t, carry):
            r2 = row_in_plane(r, row_plane(r, t // 8), lax.rem(t, 8))
            h2 = q * ROWS + r2
            right_src, right_dst = send_c.at[h2, 1], right_c.at[mine, my_rows]

            @pl.when(h2 == hid)
            def _():
                pltpu.make_async_copy(right_src, right_dst, cr_rsem).start()

            @pl.when(h2 != hid)
            def _():
                pltpu.make_async_remote_copy(
                    right_src, right_dst, cr_ssem, cr_rsem, device_id=(r2, q), device_id_type=MESH
                ).start()

            @pl.when(mine < BLOCKS)
            def _():
                left_src, left_dst = send_c.at[h2, 0], left_c.at[mine, my_rows]

                @pl.when(h2 == hid)
                def _():
                    pltpu.make_async_copy(left_src, left_dst, cl_rsem).start()

                @pl.when(h2 != hid)
                def _():
                    pltpu.make_async_remote_copy(
                        left_src, left_dst, cl_ssem, cl_rsem,
                        device_id=(r2, q), device_id_type=MESH,
                    ).start()

            return carry

        lax.fori_loop(0, ROWS, send, 0)
        return carry

    lax.fori_loop(0, CHAN, chunk_c, 0)

    sends_m = r * R < WIN
    row_block = r // per
    m_rows = pl.ds(pl.multiple_of(lax.rem(r, per) * R, R), R)

    def m_copy(n):
        g = lax.rem(n + r, per)
        r2 = mine * per + g
        m_chan = column_chan(r2, row_block)
        src = send_m.at[pl.ds(pl.multiple_of(g * R, R), R)]
        dst = recv_m.at[:, m_rows, :]
        own = jnp.logical_and(r2 == r, m_chan == c)
        local = lambda: pltpu.make_async_copy(src, dst, m_rsem)
        remote = lambda: pltpu.make_async_remote_copy(
            src, dst, m_ssem.at[g], m_rsem, device_id=(r2, m_chan), device_id_type=MESH
        )
        return own, local, remote

    @pl.when(sends_m)
    def _():
        def turn_mid(i, carry):
            z0[pl.ds(i, K, stride=R), :] = jnp.transpose(mid[i].astype(F32))
            return carry

        lax.fori_loop(0, R, turn_mid, 0, unroll=8)

        def pack(j, carry):
            send_m[j] = z0[pl.ds(pl.multiple_of(j * R, R), R), :].astype(BF16)
            return carry

        lax.fori_loop(0, K, pack, 0, unroll=8)

        def send(g, carry):
            own, local, remote = m_copy(g)

            @pl.when(own)
            def _():
                local().start()

            @pl.when(jnp.logical_not(own))
            def _():
                remote().start()

            return carry

        lax.fori_loop(0, per, send, 0)

    pltpu.make_async_copy(left_c, left_c, cl_rsem).wait()
    pltpu.make_async_copy(right_c, right_c, cr_rsem).wait()

    tail = WIN - (BLOCKS - 1) * K
    group = K // tail

    def send_d(r2, b2):
        c2 = column_chan(r2, b2)
        src = out_d.at[b2, pl.ds(pl.multiple_of(r2 * R, R), R)]
        dst = recv_d.at[hid]
        own = jnp.logical_and(r2 == r, c2 == c)

        @pl.when(own)
        def _():
            pltpu.make_async_copy(src, dst, d_rsem.at[r // 8]).start()

        @pl.when(jnp.logical_not(own))
        def _():
            pltpu.make_async_remote_copy(
                src, dst, d_ssem, d_rsem.at[r // 8], device_id=(r2, c2), device_id_type=MESH
            ).start()

    def chunk_d(s, carry):
        b = row_plane(r, s)
        cols = pl.ds(pl.multiple_of(b * K, K), K)
        left = jnp.concatenate([left_c[n] for n in range(BLOCKS)], axis=1)
        total = dot(right_c[b], left, ((0,), (0,))).astype(BF16)
        for n in range(BLOCKS):
            out_d[n, cols, :] = total[:, n * K : (n + 1) * K]

        def send(t, carry):
            send_d(row_in_plane(r, b, t // 2), lax.rem(t + c, 2))
            return carry

        lax.fori_loop(0, per * 2, send, 0)
        return carry

    lax.fori_loop(0, TOK // K, chunk_d, 0)

    def late_d(t, carry):
        send_d(row_in_plane(r, row_plane(r, t // 8), lax.rem(t, 8)), BLOCKS - 1)
        return carry

    lax.fori_loop(0, ROWS, late_d, 0)

    @pl.when(block < BLOCKS)
    def _():
        @pl.when(block < BLOCKS - 1)
        def _():
            pltpu.make_async_copy(recv_m, recv_m, m_rsem).wait()

        @pl.when(block == BLOCKS - 1)
        def _():
            part = recv_m.at[:, pl.ds(0, tail), :]
            pltpu.make_async_copy(part, part, m_rsem).wait()

        def gate_in(j, carry):
            m = jnp.transpose(recv_m[j].astype(F32))
            resid[j] = m.astype(BF16)
            gate1[j] = sigmoid(dot(gt[1], norm_rows(m, gains[1])))
            return carry

        lax.fori_loop(0, R, gate_in, 0, unroll=8)

        take_hidden(recv_d, d_rsem, z1, stat, r)

        def update_in(j):
            h = normed_hidden(z1, stat, gains[3], j)
            return (resid[j].astype(F32) + gate1[j] * dot(ot[1], h)).astype(BF16)

        def send(src, dst, sem):
            for s in range(1, CHAN):
                c2 = lax.rem(c + s, CHAN)
                rows = pl.ds(pl.multiple_of(c2 * share, share), share)
                pltpu.make_async_remote_copy(
                    src.at[..., rows, :], dst, e_ssem, sem, device_id=(r, c2), device_id_type=MESH
                ).start()
            rows = pl.ds(pl.multiple_of(c * share, share), share)
            pltpu.make_async_copy(src.at[..., rows, :], dst, sem).start()

        @pl.when(block < BLOCKS - 1)
        def _():
            def whole(g, carry):
                first = pl.multiple_of(g * group, group)
                for t in range(group):
                    out_e[first + t] = update_in(first + t)
                some = pl.ds(first, group)
                send(out_e.at[some], recv_e.at[block, some], e_rsem)
                return carry

            lax.fori_loop(0, R // group, whole, 0)

        @pl.when(block == BLOCKS - 1)
        def _():
            def packed(g, carry):
                first = pl.multiple_of(g * group, group)
                parts = [update_in(first + t)[:, :tail] for t in range(group)]
                out_t[g] = jnp.concatenate(parts, axis=1)
                send(out_t.at[g], recv_t.at[g], t_rsem)
                return carry

            lax.fori_loop(0, R // group, packed, 0)

    pltpu.make_async_copy(recv_e, recv_e, e_rsem).wait()
    for b in range(BLOCKS - 1):
        out_ref[:, :, b * K : (b + 1) * K] = recv_e[b]

    pltpu.make_async_copy(recv_t, recv_t, t_rsem).wait()
    for g in range(R // group):
        for t in range(group):
            out_ref[g * group + t, :, WIN - tail :] = recv_t[g, :, t * tail : (t + 1) * tail]

    def drain(ref, sem):
        pltpu.make_async_copy(ref, ref, sem).wait()

    drain(send_a.at[pl.ds(0, DEV - 1)], a_ssem)
    drain(recv_b.at[pl.ds(0, DEV - 1)], b_ssem)
    drain(recv_b.at[pl.ds(0, DEV - 1)], cr_ssem)

    @pl.when(mine < BLOCKS)
    def _():
        drain(recv_b.at[pl.ds(0, DEV - 1)], cl_ssem)

    @pl.when(block < BLOCKS)
    def _():
        drain(recv_b.at[pl.ds(0, ROWS * BLOCKS - 1)], d_ssem)

    @pl.when(block == BLOCKS)
    def _():
        drain(recv_b.at[pl.ds(0, ROWS * BLOCKS)], d_ssem)

    tiles = R * share // R

    @pl.when(block < BLOCKS - 1)
    def _():
        drain(recv_b.at[pl.ds(0, (CHAN - 1) * tiles)], e_ssem)

    @pl.when(block == BLOCKS - 1)
    def _():
        drain(recv_b.at[pl.ds(0, (CHAN - 1) * tiles // group)], e_ssem)

    @pl.when(sends_m)
    def _():
        def done(g, carry):
            own, _local, remote = m_copy(g)

            @pl.when(jnp.logical_not(own))
            def _():
                remote().wait_send()

            return carry

        lax.fori_loop(0, per, done, 0)


def shards(pair, norm_gain, proj_weight, gate_weight, hidden_gain, out_weight):
    vmem = pl.BlockSpec(memory_space=pltpu.VMEM)
    sem = pltpu.SemaphoreType.DMA
    tiles = lambda n: pltpu.VMEM((n, R, K), BF16)
    return pl.pallas_call(
        kernel,
        out_shape=jax.ShapeDtypeStruct((R, C // CHAN, WIN), BF16),
        in_specs=[pl.BlockSpec(memory_space=pltpu.HBM)] * 6,
        out_specs=vmem,
        scratch_shapes=[
            pltpu.VMEM((2, C), F32),
            pltpu.VMEM((2, 4, C, H), BF16),
            pltpu.VMEM((2, C, C), BF16),
            pltpu.VMEM((2, H), F32),
            pltpu.VMEM((2, H, C), BF16),
            pltpu.VMEM((R, C, K), BF16),
            pltpu.VMEM((R, C, K), BF16),
            pltpu.VMEM((2, CHAN, 4 * H // CHAN, C), BF16),
            pltpu.VMEM((2, C, C), BF16),
            pltpu.VMEM((2, C, H), BF16),
            pltpu.VMEM((4, C, K), F32),
            pltpu.VMEM((H * R + R, K), F32),
            pltpu.VMEM((H * R + R, K), F32),
            pltpu.VMEM((H, 2, R, K), BF16),
            pltpu.VMEM((2, CHAN, TOK, K), BF16),
            pltpu.VMEM((CHAN, TOK, K), BF16),
            tiles(H),
            pltpu.VMEM((R, C, K), F32),
            pltpu.VMEM((R, C, K), BF16),
            pltpu.VMEM((H, 2, R, K), BF16),
            pltpu.VMEM((BLOCKS, TOK, K), BF16),
            pltpu.VMEM((CHAN, TOK, K), BF16),
            pltpu.VMEM((K, R, C), BF16),
            pltpu.VMEM((R, K, C), BF16),
            pltpu.VMEM((BLOCKS, TOK, K), BF16),
            tiles(H),
            pltpu.VMEM((2, R, K), F32),
            pltpu.VMEM((R, C, K), F32),
            pltpu.VMEM((R, C, K), BF16),
            pltpu.VMEM((R, C, K), BF16),
            pltpu.VMEM((R // 4, C, K), BF16),
            pltpu.VMEM((BLOCKS - 1, R, C // CHAN, K), BF16),
            pltpu.VMEM((R // 4, C // CHAN, K), BF16),
            sem((6,)), pltpu.SemaphoreType.REGULAR, sem, sem, sem, sem((4,)), sem, sem, sem, sem,
            sem((K // R,)), sem, sem, sem((4,)), sem, sem, sem,
        ],
        compiler_params=pltpu.CompilerParams(
            collective_id=0, has_side_effects=True, vmem_limit_bytes=VMEM_BYTES
        ),
    )(pair, norm_gain, proj_weight, gate_weight, hidden_gain, out_weight)


def solution(mesh):
    in_specs = (P("rows", None, None), P(), P(), P(), P(), P())
    out_specs = P("rows", "chan", None)
    return jax.shard_map(shards, mesh=mesh, in_specs=in_specs, out_specs=out_specs, check_vma=False)
```
